32 devices in a mesh: dp: 16 (over z, y, x), tensor: 2 (over core).
Axes of the slice: x: 2, y: 2, z: 4, core: 2. Of those that a mesh axis runs over, the one named last changes fastest.
Arguments:
- tokens: bfloat16 [32768, 512], P(('dp', 'tensor')), may hold values from -6 to 6
- lengths: int32 [16, 6], P('dp'), may hold values from 1 to 1024, 2048 in all within a row
- w_qkv: bfloat16 [512, 3, 512], P(None, None, 'tensor'), may hold values from -0.25 to 0.25
- w_attn: bfloat16 [512, 512], P('tensor'), may hold values from -1 to 1
- w_in: bfloat16 [512, 2048], P(None, 'tensor'), may hold values from -0.25 to 0.25
- w_out: bfloat16 [2048, 512], P('tensor'), may hold values from -0.125 to 0.125
- gain_attn: float32 [512], replicated, may hold values from 0.5 to 1.5
- gain_mlp: float32 [512], replicated, may hold values from 0.5 to 1.5
- blend: float32 [2, 8], P(None, 'tensor'), may hold values from 0.5 to 2
- cotangent: bfloat16 [32768, 512], P(('dp', 'tensor')), may hold values from -6 to 6
Outputs:
- output: bfloat16 [32768, 512], P(('dp', 'tensor'))
- grad_input: bfloat16 [32768, 512], P(('dp', 'tensor'))
- grad_w_qkv: float32 [512, 3, 512], P(None, None, 'tensor')
- grad_w_attn: float32 [512, 512], P('tensor')
- grad_w_in: float32 [512, 2048], P(None, 'tensor')
- grad_w_out: float32 [2048, 512], P('tensor')
- grad_gain_attn: float32 [512], replicated
- grad_gain_mlp: float32 [512], replicated
- grad_blend: float32 [2, 8], P(None, 'tensor')
The draws below stay inside these ranges and needn't reach their ends.
Inputs may be any that keep to these rules, and one draw needn't show every extreme that they name: In every row the 6 lengths sum to 2048, and the longest is exactly 1024.
All inputs are finite; a program needn't handle non-finite values.
Results may differ from the reference program's by a relative error of at most 0.012.
Values may be sent and summed in bfloat16 or wider, within the bound.
No kernel may reach another device: no remote copies, remote signals or barrier semaphores. Data moves between devices by JAX's collectives and lax.ppermute only.
A program may use at most 192 MiB of HBM per device.

```python
import math
import jax
import jax.numpy as jnp
import numpy as np
from jax import lax

D = 512
HEADS = 8
HEAD_DIM = 64
FF = 2048
BAND = 30
ROW_LEN = 2048
DOCS = 6
MOST = 1024
TOKENS = 32768
N_DP = 16


def block_scale(rng, shape, cuts, low, high):
    level = 1.0
    for dim, parts in cuts:
        heights = jax.random.uniform(jax.random.fold_in(jax.random.fold_in(rng, 6), dim), (parts,), jnp.float32, low / len(cuts), high / len(cuts))
        level = level * jnp.repeat(jnp.exp(heights), shape[dim] // parts).reshape((-1,) + (1,) * (len(shape) - 1 - dim))
    return level


def profile(count, total, limit, skew):
    weights = [(1 << 20) // math.isqrt(rank ** skew) + 1 for rank in range(2, count + 1)]
    spare, holding = total - limit - (count - 1), [1] * (count - 1)
    while spare > 0:
        movable = [i for i in range(count - 1) if holding[i] < limit]
        pool, left = sum([weights[i] for i in movable]), spare
        for i in movable:
            extra = min(limit - holding[i], max(1, left * weights[i] // pool), spare)
            holding[i] = holding[i] + extra
            spare = spare - extra
    return np.array([limit] + holding)


def ragged(stream_key, number_of, total, limit, skew):
    if number_of == 2:
        one = jax.random.randint(stream_key, (), max(1, total - limit), min(limit, total - 1) + 1)
        return jnp.stack([one, total - one])
    sizes = jnp.asarray(profile(number_of, total, limit, skew), jnp.int32)
    pairs = (number_of - 1) // 2
    donor, taker = sizes[1:1 + 2 * pairs:2], sizes[2:2 + 2 * pairs:2]
    room = jnp.minimum(donor - 1, limit - taker)
    passed = jax.random.randint(jax.random.fold_in(stream_key, 1), (pairs,), 0, 1 << 20) % (room + 1)
    sizes = sizes.at[1:1 + 2 * pairs:2].set(donor - passed).at[2:2 + 2 * pairs:2].set(taker + passed)
    return sizes[jax.random.permutation(jax.random.fold_in(stream_key, 2), number_of)]


def centred(stream_key, extent, deviation, reach, cuts=(), kind=jnp.bfloat16):
    drawn = deviation * jax.random.normal(stream_key, extent, jnp.float32)
    if cuts:
        drawn = drawn * block_scale(stream_key, extent, cuts, -0.22, 0.18)
    return jnp.clip(drawn, -reach, reach).astype(kind)


def setup_inputs(seed: int = 0) -> dict:
    key_of = jax.random.split(jax.random.key(seed), 11)
    tokens = centred(key_of[0], (TOKENS, D), 1.0, 6.0, ((0, 32),))
    lengths = jax.vmap(lambda own: ragged(own, DOCS, ROW_LEN, MOST, 2))(jax.random.split(key_of[1], N_DP)).reshape((N_DP, DOCS)).astype(jnp.int32)
    w_qkv = centred(key_of[2], (D, 3, D), D ** -0.5, 0.25, ((2, 2),))
    w_attn = centred(key_of[3], (D, D), (D // 16) ** -0.5, 1.0, ((0, 2),))
    w_in = centred(key_of[4], (D, FF), D ** -0.5, 0.25, ((1, 2),))
    w_out = centred(key_of[5], (FF, D), FF ** -0.5, 0.125, ((0, 2),))
    gain_attn = jnp.clip(1.0 + 0.1 * jax.random.normal(key_of[6], (D,), jnp.float32), 0.5, 1.5)
    gain_mlp = jnp.clip(1.0 + 0.1 * jax.random.normal(key_of[7], (D,), jnp.float32), 0.5, 1.5)
    blend = jnp.clip(0.5 + 1.5 * jax.random.uniform(key_of[8], (2, HEADS), jnp.float32) ** block_scale(key_of[8], (2, HEADS), ((1, 2),), -0.2, 0.2), 0.5, 2.0)
    cotangent = centred(key_of[9], (TOKENS, D), 1.0, 6.0, ((0, 32),))
    return {"tokens": tokens, "lengths": lengths, "w_qkv": w_qkv, "w_attn": w_attn, "w_in": w_in, "w_out": w_out, "gain_attn": gain_attn, "gain_mlp": gain_mlp, "blend": blend, "cotangent": cotangent}


@jax.custom_vjp
def low(v):
    return lax.optimization_barrier(v.astype(jnp.bfloat16)).astype(jnp.float32)

@jax.custom_vjp
def low_back(v):
    return v

def low_keep(v):
    return (low(v), None)

def low_pass(kept, grad):
    return (grad,)

def back_keep(v):
    return (v, None)

def back_low(kept, grad):
    return (low(grad),)
low.defvjp(low_keep, low_pass)
low_back.defvjp(back_keep, back_low)
highest = lax.Precision.HIGHEST

def rms_scale(values, gain):
    return values * lax.rsqrt(lax.optimization_barrier(jnp.mean(values * values, axis=-1, keepdims=True)) + 1e-06) * gain

def gelu_tanh(values):
    return jax.nn.gelu(values, approximate=True)

def features(values):
    first = low_back(low(jax.nn.elu(values) + 1.0))
    second = low_back(low(jnp.tanh(values)))
    return (first, second)

def head_mixer(packed):
    queries, keys, values, segment, mixing = packed
    places = jnp.arange(ROW_LEN, dtype=jnp.int32)
    same = segment[:, None] == segment[None, :]
    behind = places[:, None] - places[None, :]
    causal = same & (behind >= 0)
    banded = causal & (behind < BAND)
    scores = low_back(jnp.dot(queries, keys.T, precision=highest)) * HEAD_DIM ** (-0.5)
    scores = jnp.where(banded, scores, -1e+30)
    top = lax.optimization_barrier(jnp.max(scores, axis=-1, keepdims=True))
    raised = jnp.exp(scores - top)
    near_weights = low(raised / lax.optimization_barrier(jnp.sum(raised, axis=-1, keepdims=True)))
    near = low_back(jnp.dot(near_weights, values, precision=highest))
    far_mask = causal.astype(jnp.float32)
    query_one, query_two = features(queries)
    key_one, key_two = features(keys)
    first = low_back(jnp.dot(query_one, key_one.T, precision=highest)) * far_mask
    second = low_back(jnp.dot(query_two, key_two.T, precision=highest)) * far_mask
    numer_one = low_back(jnp.dot(low(first), values, precision=highest))
    numer_two = low_back(jnp.dot(low(second), values, precision=highest))
    far_one = numer_one / lax.optimization_barrier(jnp.sum(first, axis=-1, keepdims=True))
    far_two = numer_two / lax.optimization_barrier(jnp.sum(far_mask, axis=-1, keepdims=True))
    return near + mixing[0] * far_one + mixing[1] * far_two

def reference(tokens, lengths, w_qkv, w_attn, w_in, w_out, gain_attn, gain_mlp, blend, cotangent):
    row_count = lengths.shape[0]
    ends = jnp.cumsum(lengths, axis=1).astype(jnp.int32)
    places = jnp.arange(ROW_LEN, dtype=jnp.int32)
    segment = lax.optimization_barrier(jnp.sum((places[None, :, None] >= ends[:, None, :]).astype(jnp.int32), axis=2)).astype(jnp.int32)
    segment_heads = jnp.repeat(segment, HEADS, axis=0)

    def layer(inputs, qkv_weight, attn_weight, in_weight, out_weight, first_gain, second_gain, mixing):
        normed = low(rms_scale(inputs, first_gain))
        projected = low_back(low(jnp.dot(normed, qkv_weight.reshape(D, 3 * D), precision=highest)))
        split = projected.reshape(row_count, ROW_LEN, 3, HEADS, HEAD_DIM).transpose(2, 0, 3, 1, 4)
        split = split.reshape(3, row_count * HEADS, ROW_LEN, HEAD_DIM)
        mixing_heads = jnp.tile(mixing.T, (row_count, 1))
        mixed = lax.map(jax.checkpoint(head_mixer), (split[0], split[1], split[2], segment_heads, mixing_heads))
        mixed = mixed.reshape(row_count, HEADS, ROW_LEN, HEAD_DIM).transpose(0, 2, 1, 3).reshape(row_count * ROW_LEN, D)
        mixed = low_back(low(mixed))
        hidden = inputs + low_back(jnp.dot(mixed, attn_weight, precision=highest))
        normed_two = low(rms_scale(hidden, second_gain))
        before = low_back(jnp.dot(normed_two, in_weight, precision=highest))
        active = low_back(low(gelu_tanh(before)))
        return hidden + jnp.dot(active, out_weight, precision=highest)
    output, pullback = jax.vjp(layer, tokens.astype(jnp.float32), w_qkv.astype(jnp.float32), w_attn.astype(jnp.float32), w_in.astype(jnp.float32), w_out.astype(jnp.float32), gain_attn.astype(jnp.float32), gain_mlp.astype(jnp.float32), blend.astype(jnp.float32))
    grads = pullback(cotangent.astype(jnp.float32))
    return (output.astype(jnp.bfloat16), grads[0].astype(jnp.bfloat16), grads[1], grads[2], grads[3], grads[4], grads[5], grads[6], grads[7])
```

```python
from functools import partial

import jax
import jax.numpy as jnp
from jax import lax
from jax.experimental import pallas as pl
from jax.experimental.pallas import tpu as pltpu
from jax.sharding import PartitionSpec as P

BAND = 30
HALO = 32
BLOCK = 128
EPS = 1e-06
BF = jnp.bfloat16
F32 = jnp.float32
VMEM_BYTES = 60 * 1024 * 1024
GELU_A = 0.7978845608028654
GELU_B = 0.044715


def nn(left, right):
    return lax.dot_general(left, right, (((1,), (0,)), ((), ())), preferred_element_type=F32)


def nt(left, right):
    return lax.dot_general(left, right, (((1,), (1,)), ((), ())), preferred_element_type=F32)


def tn(left, right):
    return lax.dot_general(left, right, (((0,), (0,)), ((), ())), preferred_element_type=F32)


def iota(shape, dim):
    return lax.broadcasted_iota(jnp.int32, shape, dim)


def whole(shape):
    return pl.BlockSpec(shape, lambda *_: (0,) * len(shape))


def params():
    return pltpu.CompilerParams(vmem_limit_bytes=VMEM_BYTES)


def starts_of(ends_ref, places, docs):
    start = jnp.full(places.shape, ends_ref[docs], jnp.int32)
    for doc in range(docs):
        end = ends_ref[doc]
        start = jnp.where(places >= end, jnp.maximum(start, end), start)
    return start


def start_at(ends_ref, place, docs):
    start = ends_ref[docs]
    for doc in range(docs):
        end = ends_ref[doc]
        start = jnp.where(place >= end, jnp.maximum(start, end), start)
    return start


def norm_project_kernel(x_ref, gain_ref, w_ref, normed_ref, out_ref):
    x = x_ref[...].astype(F32)
    r = lax.rsqrt(jnp.mean(x * x, axis=1, keepdims=True) + EPS)
    normed = (x * r * gain_ref[...]).astype(BF)
    normed_ref[...] = normed
    out_ref[...] = nn(normed, w_ref[...]).astype(BF)


def first_feature(values):
    return jnp.where(values > 0, values + 1.0, jnp.exp(jnp.minimum(values, 0.0))).astype(BF)


def second_feature(values):
    return jnp.tanh(values).astype(BF)


def pair_diag(rows, cols):
    row = iota((rows, cols), 0)
    col = iota((rows, cols), 1)
    return ((row // 64) % 2) == ((col // 64) % 2)


def project_state_kernel(docs, ends_ref, normed_ref, w_ref, own_ref, out_ref, state_ref, sum_ref, halo_ref):
    rows = normed_ref.shape[0]
    other = nn(normed_ref[...], w_ref[...]).astype(BF)
    out_ref[...] = other
    member_from = start_at(ends_ref, rows - 1, docs)
    member = iota((rows, 1), 0) >= member_from
    diag = pair_diag(256, 128)
    for pair in range(4):
        src = own_ref if pair < 2 else out_ref
        col = 128 * (pair % 2)
        slot = (pair + 2) % 4
        keys = src[:, 256 + col : 384 + col]
        values = src[:, 512 + col : 640 + col]
        wide = jnp.where(member, keys.astype(F32), 0.0)
        one = jnp.where(member, first_feature(wide).astype(F32), 0.0)
        two = second_feature(wide)
        features = jnp.concatenate([one.astype(BF), two], axis=1)
        state = jnp.where(diag, tn(features, values), 0.0)
        state_ref[slot] = state.astype(BF)
        sum_ref[slot] = jnp.broadcast_to(jnp.sum(one, axis=0, keepdims=True), (8, 128))
        halo_ref[:, 128 * slot : 128 * slot + 128] = keys[rows - HALO :]
        halo_ref[:, 512 + 128 * slot : 640 + 128 * slot] = values[rows - HALO :]


def block_masks(ends_ref, docs, first):
    row_places = first + iota((1, 256), 1) % BLOCK
    start_row = starts_of(ends_ref, row_places, docs)
    window_places = first - HALO + iota((BLOCK + HALO, 256), 0)
    banded = (window_places <= row_places) & (
        window_places >= jnp.maximum(start_row, row_places - (BAND - 1))
    )
    key_places = first + iota((BLOCK, 256), 0)
    causal = (key_places <= row_places) & (key_places >= start_row)
    col_places = first + iota((BLOCK, 1), 0)
    start_col = starts_of(ends_ref, col_places, docs)
    key_lane = first + iota((BLOCK, BLOCK), 1)
    causal_q = ((key_lane <= col_places) & (key_lane >= start_col)).astype(F32).astype(BF)
    count = (col_places - start_col + 1).astype(F32)
    carried = start_col < first
    member_from = start_at(ends_ref, first + BLOCK - 1, docs)
    member = col_places >= member_from
    keep = member_from < first
    return banded, causal, causal_q, count, carried, member, keep


def stack_heads(values):
    lane = iota(values.shape, 1) % 128
    zero = jnp.zeros_like(values)
    return jnp.concatenate(
        [jnp.where(lane < 64, values, zero), jnp.where(lane >= 64, values, zero)], axis=0
    )


def pick_heads(values):
    half = values.shape[0] // 2
    lane = iota((half, values.shape[1]), 1) % 128
    return jnp.where(lane < 64, values[:half], values[half:])


def pair_front(q, k, prev_k, blend_one, blend_two, carry, masks, ones_diag):
    banded, causal, causal_q, count, carried, member, keep = masks
    wide_q = q.astype(F32)
    wide_k = k.astype(F32)
    q_one = first_feature(wide_q)
    q_two = second_feature(wide_q)
    k_one = first_feature(wide_k)
    k_two = second_feature(wide_k)
    sums = nn(causal_q, k_one) + jnp.where(carried, carry, 0.0)
    total = nn((q_one.astype(F32) * sums).astype(BF), ones_diag)
    ratio_one = blend_one / total
    ratio_two = blend_two / count
    q_scaled = jnp.concatenate(
        [
            (q_one.astype(F32) * ratio_one).astype(BF),
            (q_two.astype(F32) * ratio_two).astype(BF),
        ],
        axis=1,
    )
    k_both = jnp.concatenate([k_one, k_two], axis=1)
    q_stack = stack_heads(q)
    s_stack = stack_heads(q_scaled)
    window = jnp.concatenate([prev_k, k], axis=0)
    scores = jnp.where(banded, nt(window, q_stack) * 0.125, -1e30)
    raised = jnp.exp(scores - jnp.max(scores, axis=0, keepdims=True))
    near = raised * (1.0 / jnp.sum(raised, axis=0, keepdims=True))
    far = jnp.where(causal, nt(k_both, s_stack), 0.0)
    weights = jnp.concatenate([near[:HALO], near[HALO:] + far], axis=0).astype(BF)
    return dict(
        q_one=q_one,
        q_two=q_two,
        k_one=k_one,
        k_two=k_two,
        sums=sums,
        total=total,
        ratio_one=ratio_one,
        ratio_two=ratio_two,
        q_scaled=q_scaled,
        k_both=k_both,
        q_stack=q_stack,
        s_stack=s_stack,
        window=window,
        near=near,
        weights=weights,
    )


def ones_diagonal():
    return pair_diag(128, 128).astype(F32).astype(BF)


def mixer_forward_kernel(
    docs,
    ends_ref,
    own_ref,
    other_ref,
    halo_ref,
    state_in_ref,
    sum_in_ref,
    blend_ref,
    mixed_ref,
    state_out_ref,
    sum_out_ref,
    prev_out_ref,
    state_ref,
    sum_ref,
    prev_ref,
):
    index = pl.program_id(0)
    first = index * BLOCK

    @pl.when(index == 0)
    def _():
        state_ref[...] = state_in_ref[...].astype(F32)
        sum_ref[...] = sum_in_ref[...]
        prev_ref[...] = halo_ref[...]

    masks = block_masks(ends_ref, docs, first)
    banded, causal, causal_q, count, carried, member, keep = masks
    diag = pair_diag(256, 128)
    ones_diag = ones_diagonal()
    prev_out_ref[0] = prev_ref[...]
    for pair in range(4):
        src = own_ref if pair < 2 else other_ref
        col = 128 * (pair % 2)
        lanes = slice(128 * pair, 128 * pair + 128)
        value_lanes = slice(512 + 128 * pair, 640 + 128 * pair)
        q = src[:, col : col + 128]
        k = src[:, 256 + col : 384 + col]
        v = src[:, 512 + col : 640 + col]
        state = state_ref[pair]
        carry = sum_ref[pair][0:1]
        state_low = state.astype(BF)
        state_out_ref[0, pair] = state_low
        sum_out_ref[0, pair] = sum_ref[pair]
        front = pair_front(
            q, k, prev_ref[:, lanes], blend_ref[0:1, lanes], blend_ref[1:2, lanes], carry, masks, ones_diag
        )
        v_window = jnp.concatenate([prev_ref[:, value_lanes], v], axis=0)
        out = pick_heads(tn(front["weights"], v_window))
        q_carried = jnp.where(carried, front["q_scaled"], jnp.zeros_like(front["q_scaled"]))
        out = out + nn(q_carried, state_low)
        mixed_ref[:, lanes] = out.astype(BF)
        k_member = jnp.where(member, front["k_both"], jnp.zeros_like(front["k_both"]))
        added = jnp.where(diag, tn(k_member, v), 0.0)
        state_ref[pair] = jnp.where(keep, state, 0.0) + added
        sum_ref[pair] = jnp.broadcast_to(front["sums"][BLOCK - 1 : BLOCK], (8, 128))
        prev_ref[:, lanes] = k[BLOCK - HALO :]
        prev_ref[:, value_lanes] = v[BLOCK - HALO :]


def mixer_backward_kernel(
    docs,
    ends_ref,
    own_ref,
    other_ref,
    prev_ref,
    state_ref,
    sum_ref,
    blend_ref,
    grad_ref,
    gq_ref,
    gk_ref,
    gv_ref,
    halo_ref,
    back_state_ref,
    back_sum_ref,
    blend_out_ref,
    dk_ref,
    dv_ref,
):
    step = pl.program_id(0)
    index = pl.num_programs(0) - 1 - step
    first = index * BLOCK

    @pl.when(step == 0)
    def _():
        back_state_ref[...] = jnp.zeros_like(back_state_ref)
        back_sum_ref[...] = jnp.zeros_like(back_sum_ref)
        blend_out_ref[...] = jnp.zeros_like(blend_out_ref)
        dk_ref[...] = jnp.zeros_like(dk_ref)
        dv_ref[...] = jnp.zeros_like(dv_ref)

    masks = block_masks(ends_ref, docs, first)
    banded, causal, causal_q, count, carried, member, keep = masks
    diag = pair_diag(256, 128)
    ones_diag = ones_diagonal()
    for pair in range(4):
        src = own_ref if pair < 2 else other_ref
        col = 128 * (pair % 2)
        lanes = slice(128 * pair, 128 * pair + 128)
        value_lanes = slice(512 + 128 * pair, 640 + 128 * pair)
        q = src[:, col : col + 128]
        k = src[:, 256 + col : 384 + col]
        v = src[:, 512 + col : 640 + col]
        grad = grad_ref[:, lanes]
        front = pair_front(
            q,
            k,
            prev_ref[0, :, lanes],
            blend_ref[0:1, lanes],
            blend_ref[1:2, lanes],
            sum_ref[0, pair][0:1],
            masks,
            ones_diag,
        )
        state = state_ref[0, pair]
        v_window = jnp.concatenate([prev_ref[0, :, value_lanes], v], axis=0)
        g_stack = stack_heads(grad)
        grad_weights = nt(v_window, g_stack)
        near = front["near"]
        inner = near * grad_weights
        dscores = (
            (inner - near * jnp.sum(inner, axis=0, keepdims=True)) * 0.125
        ).astype(BF)
        far = jnp.where(causal, grad_weights[HALO:], 0.0).astype(BF)
        up = pick_heads(tn(far, front["k_both"]))
        g_carried = jnp.where(carried, grad, jnp.zeros_like(grad))
        up = up + nt(g_carried, state)
        up_one = up[:, :128]
        up_two = up[:, 128:]
        q_one = front["q_one"].astype(F32)
        mean_one = nn((q_one * up_one).astype(BF), ones_diag) / front["total"]
        grad_one = front["ratio_one"] * (up_one - mean_one * front["sums"])
        grad_two = front["ratio_two"] * up_two
        tanh_q = jnp.tanh(q.astype(F32))
        slope_q = jnp.exp(jnp.minimum(q.astype(F32), 0.0))
        gq = pick_heads(tn(dscores, front["window"]))
        gq = gq + grad_one * slope_q + grad_two * (1.0 - tanh_q * tanh_q)
        gq_ref[:, lanes] = gq.astype(BF)
        blend_out_ref[0, pair] += jnp.broadcast_to(
            jnp.sum(mean_one, axis=0, keepdims=True) / 64.0, (8, 128)
        )
        blend_out_ref[1, pair] += jnp.broadcast_to(
            jnp.sum(front["q_two"].astype(F32) * up_two / count, axis=0, keepdims=True), (8, 128)
        )

        back = back_state_ref[pair]
        back_low = back.astype(BF)
        back_sum = back_sum_ref[pair][0:1]
        k_member = jnp.where(member, front["k_both"], jnp.zeros_like(front["k_both"]))
        v_member = jnp.where(member, v, jnp.zeros_like(v))
        dv = nn(front["weights"], g_stack)
        dv_own = dv[HALO:] + nn(k_member, back_low)
        weighted = (mean_one * front["q_scaled"][:, :128].astype(F32)).astype(BF)
        dfeat = nn(far, front["s_stack"]) + nt(v_member, back_low)
        d_one = dfeat[:, :128] - tn(causal_q, weighted) - jnp.where(member, back_sum, 0.0)
        d_two = dfeat[:, 128:]
        dk = nn(dscores, front["q_stack"])
        tanh_k = jnp.tanh(k.astype(F32))
        slope_k = jnp.exp(jnp.minimum(k.astype(F32), 0.0))
        gk = dk[HALO:] + d_one * slope_k + d_two * (1.0 - tanh_k * tanh_k)
        gk_ref[: BLOCK - HALO, lanes] = gk[: BLOCK - HALO].astype(BF)
        gk_ref[BLOCK - HALO :, lanes] = (gk[BLOCK - HALO :] + dk_ref[:, lanes]).astype(BF)
        gv_ref[: BLOCK - HALO, lanes] = dv_own[: BLOCK - HALO].astype(BF)
        gv_ref[BLOCK - HALO :, lanes] = (dv_own[BLOCK - HALO :] + dv_ref[:, lanes]).astype(BF)
        dk_ref[:, lanes] = dk[:HALO]
        dv_ref[:, lanes] = dv[:HALO]
        q_carried = jnp.where(carried, front["q_scaled"], jnp.zeros_like(front["q_scaled"]))
        added = jnp.where(diag, tn(q_carried, grad), 0.0)
        back_state_ref[pair] = jnp.where(keep, back, 0.0) + added
        added_sum = jnp.sum(
            jnp.where(carried, weighted.astype(F32), 0.0), axis=0, keepdims=True
        )
        back_sum_ref[pair] = jnp.broadcast_to(
            jnp.where(keep, back_sum, 0.0) + added_sum, (8, 128)
        )

    @pl.when(index == 0)
    def _():
        halo_ref[:, :512] = dk_ref[...]
        halo_ref[:, 512:] = dv_ref[...]


def feed_kernel(
    mixed_ref,
    x_ref,
    cot_ref,
    gain_ref,
    wa_own_ref,
    wa_other_ref,
    wi_own_ref,
    wi_other_ref,
    wo_own_ref,
    wo_other_ref,
    out_ref,
    normed_ref,
    active_ref,
    gpre_ref,
    ghid_ref,
    branch_ref,
    gmix_ref,
    ggain_ref,
):
    step = pl.program_id(0)
    x = x_ref[...].astype(F32)
    hidden = x + (nn(mixed_ref[:, :256], wa_own_ref[...]) + nn(mixed_ref[:, 256:], wa_other_ref[...]))
    r = lax.rsqrt(jnp.mean(hidden * hidden, axis=1, keepdims=True) + EPS)
    y = hidden * r
    gain = gain_ref[...]
    normed = (y * gain).astype(BF)
    normed_ref[...] = normed
    grad = cot_ref[...]
    total = hidden
    back = None
    for half, (wi_ref, wo_ref) in enumerate(((wi_own_ref, wo_own_ref), (wi_other_ref, wo_other_ref))):
        width = wi_ref.shape[1]
        for part in range(2):
            cols = slice(part * width // 2, (part + 1) * width // 2)
            dest = slice(half * width + part * width // 2, half * width + (part + 1) * width // 2)
            u = nn(normed, wi_ref[:, cols])
            square = u * u
            t = jnp.tanh(u * (GELU_A + (GELU_A * GELU_B) * square))
            gate = 0.5 + 0.5 * t
            active = (u * gate).astype(BF)
            slope = gate + u * (0.5 - 0.5 * t * t) * (GELU_A + (3.0 * GELU_A * GELU_B) * square)
            active_ref[:, dest] = active
            total = total + nn(active, wo_ref[cols, :])
            gact = nt(grad, wo_ref[cols, :])
            gpre = (gact * slope).astype(BF)
            gpre_ref[:, dest] = gpre
            term = nt(gpre, wi_ref[:, cols])
            back = term if back is None else back + term
    out_ref[...] = total.astype(BF)
    scaled = back * gain
    ghid = grad.astype(F32) + r * (scaled - y * jnp.mean(scaled * y, axis=1, keepdims=True))
    ghid_ref[...] = ghid
    branch = ghid.astype(BF)
    branch_ref[...] = branch
    gmix_ref[:, :256] = nt(branch, wa_own_ref[...]).astype(BF)
    gmix_ref[:, 256:] = nt(branch, wa_other_ref[...]).astype(BF)

    @pl.when(step == 0)
    def _():
        ggain_ref[...] = jnp.zeros_like(ggain_ref)

    ggain_ref[0:1] += jnp.sum(back * y, axis=0, keepdims=True)


def weight_grads_kernel(mixed_ref, branch_ref, active_ref, cot_ref, normed_ref, gpre_ref, wo_ref, wi_ref):
    for half in range(2):
        wo_ref[half, 0:1024] = tn(active_ref[:, 1024 * half : 1024 * half + 1024], cot_ref[...]).astype(BF)
        wo_ref[half, 1024:1280] = tn(mixed_ref[:, 256 * half : 256 * half + 256], branch_ref[...]).astype(BF)
        wi_ref[half] = tn(normed_ref[...], gpre_ref[:, 1024 * half : 1024 * half + 1024]).astype(BF)


def finish_kernel(
    docs,
    ends_ref,
    flag_ref,
    own_ref,
    other_ref,
    normed_ref,
    gq_ref,
    gk_ref,
    gv_ref,
    halo_ref,
    back_state_ref,
    back_sum_ref,
    gproj_ref,
    wgrad_ref,
):
    rows = own_ref.shape[0]
    flag = flag_ref[0]
    member_from = start_at(ends_ref, rows - 1, docs)
    member = (iota((rows, 1), 0) >= member_from) & (flag == 0)
    live = flag == 0
    for pair in range(4):
        src = own_ref if pair < 2 else other_ref
        col = 128 * (pair % 2)
        lanes = slice(128 * pair, 128 * pair + 128)
        base = 768 * (pair // 2) + col
        slot = (pair + 2) % 4
        k = src[:, 256 + col : 384 + col].astype(F32)
        v = src[:, 512 + col : 640 + col]
        back = back_state_ref[slot].astype(BF)
        back_sum = back_sum_ref[slot][0:1]
        t = jnp.tanh(k)
        slope = jnp.exp(jnp.minimum(k, 0.0))
        k_both = jnp.concatenate([first_feature(k), t.astype(BF)], axis=1)
        dfeat = nt(v, back)
        extra_k = (dfeat[:, :128] - back_sum) * slope + dfeat[:, 128:] * (1.0 - t * t)
        extra_v = nn(k_both, back)
        gk = gk_ref[:, lanes].astype(F32) + jnp.where(member, extra_k, 0.0)
        gv = gv_ref[:, lanes].astype(F32) + jnp.where(member, extra_v, 0.0)
        other_lanes = slice(128 * slot, 128 * slot + 128)
        other_values = slice(512 + 128 * slot, 640 + 128 * slot)
        halo_k = jnp.where(live, halo_ref[:, other_lanes], 0.0)
        halo_v = jnp.where(live, halo_ref[:, other_values], 0.0)
        cut = rows - HALO
        gproj_ref[:, base : base + 128] = gq_ref[:, lanes]
        gproj_ref[:cut, base + 256 : base + 384] = gk[:cut].astype(BF)
        gproj_ref[cut:, base + 256 : base + 384] = (gk[cut:] + halo_k).astype(BF)
        gproj_ref[:cut, base + 512 : base + 640] = gv[:cut].astype(BF)
        gproj_ref[cut:, base + 512 : base + 640] = (gv[cut:] + halo_v).astype(BF)
    for half in range(2):
        wgrad_ref[half] = tn(normed_ref[...], gproj_ref[:, 768 * half : 768 * half + 768]).astype(BF)


def input_grad_kernel(gproj_ref, x_ref, ghid_ref, gain_ref, w_own_ref, w_other_ref, out_ref, ggain_ref):
    step = pl.program_id(0)
    gnormed = nt(gproj_ref[:, :768], w_own_ref[...]) + nt(gproj_ref[:, 768:], w_other_ref[...])
    x = x_ref[...].astype(F32)
    r = lax.rsqrt(jnp.mean(x * x, axis=1, keepdims=True) + EPS)
    y = x * r
    scaled = gnormed * gain_ref[...]
    grad = ghid_ref[...] + r * (scaled - y * jnp.mean(scaled * y, axis=1, keepdims=True))
    out_ref[...] = grad.astype(BF)

    @pl.when(step == 0)
    def _():
        ggain_ref[...] = jnp.zeros_like(ggain_ref)

    ggain_ref[0:1] += jnp.sum(gnormed * y, axis=0, keepdims=True)


def dp_dims(count):
    dims = []
    stride = 1
    left = count
    for size in (2, 2):
        if left % size == 0 and left > 1:
            dims.append((size, stride))
            stride *= size
            left //= size
    while left > 1:
        size = 4 if left % 4 == 0 else (2 if left % 2 == 0 else left)
        dims.append((size, stride))
        stride *= size
        left //= size
    return dims


def shift_pairs(count, size, stride, offset):
    pairs = []
    for src in range(count):
        place = (src // stride) % size
        pairs.append((src, src + ((place + offset) % size - place) * stride))
    return pairs


def scatter_step(values, count, size, stride):
    place = (lax.axis_index("dp") // stride) % size
    parts = values.reshape((size, values.shape[0] // size) + values.shape[1:])
    total = lax.dynamic_index_in_dim(parts, place, 0, keepdims=False).astype(F32)
    for offset in range(1, size):
        sent = lax.dynamic_index_in_dim(parts, (place + offset) % size, 0, keepdims=False)
        got = lax.ppermute(sent, "dp", shift_pairs(count, size, stride, offset))
        total = total + got.astype(F32)
    return total.astype(values.dtype)


def gather_step(values, count, size, stride):
    place = (lax.axis_index("dp") // stride) % size
    whole_values = jnp.zeros((size,) + values.shape, values.dtype)
    whole_values = lax.dynamic_update_index_in_dim(whole_values, values, place, 0)
    for offset in range(1, size):
        got = lax.ppermute(values, "dp", shift_pairs(count, size, stride, offset))
        whole_values = lax.dynamic_update_index_in_dim(
            whole_values, got, (place - offset) % size, 0
        )
    return whole_values.reshape((size * values.shape[0],) + values.shape[1:])


def reduce_all(values, count):
    dims = dp_dims(count)
    if not dims:
        return values
    orders = [dims]
    if len(dims) > 1:
        orders.append([dims[1], dims[0]] + dims[2:])
    pieces = []
    for part, order in zip(jnp.split(values, len(orders), axis=0), orders):
        for size, stride in order:
            part = scatter_step(part, count, size, stride)
        for size, stride in reversed(order):
            part = gather_step(part, count, size, stride)
        pieces.append(part)
    return jnp.concatenate(pieces, axis=0)


def reduce_small(values, count):
    for size, stride in dp_dims(count):
        total = values
        for offset in range(1, size):
            total = total + lax.ppermute(values, "dp", shift_pairs(count, size, stride, offset))
        values = total
    return values


def swap(values):
    return lax.ppermute(values, "tensor", [(0, 1), (1, 0)])


def body(count, tokens, lengths, w_qkv, w_attn, w_in, w_out, gain_attn, gain_mlp, blend, cotangent):
    rows, width = tokens.shape
    docs = lengths.shape[1]
    half = lax.axis_index("tensor").astype(jnp.int32)
    blocks = rows // BLOCK

    wq_own = w_qkv.reshape(width, -1)
    wq_other = swap(wq_own)
    wa_other, wi_other, wo_other = swap(w_attn), swap(w_in), swap(w_out)
    blend_both = jnp.repeat(jnp.concatenate([blend, swap(blend)], axis=1), 64, axis=1)
    ends = jnp.concatenate([jnp.cumsum(lengths[0]), jnp.zeros((1,), jnp.int32)]).astype(jnp.int32) - half * rows
    flag = half.reshape(1)
    gain_one = gain_attn.reshape(1, width)
    gain_two = gain_mlp.reshape(1, width)
    smem = pl.BlockSpec(memory_space=pltpu.SMEM)

    def row_block(size, cols):
        return pl.BlockSpec((size, cols), lambda i: (i, 0))

    own_cols = wq_own.shape[1]
    normed, own = pl.pallas_call(
        norm_project_kernel,
        grid=(4,),
        in_specs=[row_block(rows // 4, width), whole((1, width)), whole(wq_own.shape)],
        out_specs=[row_block(rows // 4, width), row_block(rows // 4, own_cols)],
        out_shape=[jax.ShapeDtypeStruct((rows, width), BF), jax.ShapeDtypeStruct((rows, own_cols), BF)],
        compiler_params=params(),
        name="norm_project",
    )(tokens, gain_one, wq_own)
    other, state_end, sum_end, halo_end = pl.pallas_call(
        partial(project_state_kernel, docs),
        in_specs=[smem] + [pl.BlockSpec(memory_space=pltpu.VMEM)] * 3,
        out_shape=[
            jax.ShapeDtypeStruct((rows, own_cols), BF),
            jax.ShapeDtypeStruct((4, 256, 128), BF),
            jax.ShapeDtypeStruct((4, 8, 128), F32),
            jax.ShapeDtypeStruct((HALO, 1024), BF),
        ],
        compiler_params=params(),
        name="project_state",
    )(ends, normed, wq_other, own)
    state_in, sum_in, halo_in = swap(state_end), swap(sum_end), swap(halo_end)

    mixed, states, sums, prevs = pl.pallas_call(
        partial(mixer_forward_kernel, docs),
        grid=(blocks,),
        in_specs=[
            smem,
            row_block(BLOCK, own_cols),
            row_block(BLOCK, own_cols),
            whole((HALO, 1024)),
            whole((4, 256, 128)),
            whole((4, 8, 128)),
            whole(blend_both.shape),
        ],
        out_specs=[
            row_block(BLOCK, width),
            pl.BlockSpec((1, 4, 256, 128), lambda i: (i, 0, 0, 0)),
            pl.BlockSpec((1, 4, 8, 128), lambda i: (i, 0, 0, 0)),
            pl.BlockSpec((1, HALO, 1024), lambda i: (i, 0, 0)),
        ],
        out_shape=[
            jax.ShapeDtypeStruct((rows, width), BF),
            jax.ShapeDtypeStruct((blocks, 4, 256, 128), BF),
            jax.ShapeDtypeStruct((blocks, 4, 8, 128), F32),
            jax.ShapeDtypeStruct((blocks, HALO, 1024), BF),
        ],
        scratch_shapes=[
            pltpu.VMEM((4, 256, 128), F32),
            pltpu.VMEM((4, 8, 128), F32),
            pltpu.VMEM((HALO, 1024), BF),
        ],
        compiler_params=params(),
        name="mixer_forward",
    )(ends, own, other, halo_in, state_in, sum_in, blend_both)

    hidden_units = 2 * w_in.shape[1]
    tall = rows // 4
    output, normed_two, active, gpre, ghid, branch, gmix, ggain_mlp = pl.pallas_call(
        feed_kernel,
        grid=(4,),
        in_specs=[
            row_block(tall, width),
            row_block(tall, width),
            row_block(tall, width),
            whole((1, width)),
            whole(w_attn.shape),
            whole(w_attn.shape),
            whole(w_in.shape),
            whole(w_in.shape),
            whole(w_out.shape),
            whole(w_out.shape),
        ],
        out_specs=[
            row_block(tall, width),
            row_block(tall, width),
            row_block(tall, hidden_units),
            row_block(tall, hidden_units),
            row_block(tall, width),
            row_block(tall, width),
            row_block(tall, width),
            whole((8, width)),
        ],
        out_shape=[
            jax.ShapeDtypeStruct((rows, width), BF),
            jax.ShapeDtypeStruct((rows, width), BF),
            jax.ShapeDtypeStruct((rows, hidden_units), BF),
            jax.ShapeDtypeStruct((rows, hidden_units), BF),
            jax.ShapeDtypeStruct((rows, width), F32),
            jax.ShapeDtypeStruct((rows, width), BF),
            jax.ShapeDtypeStruct((rows, width), BF),
            jax.ShapeDtypeStruct((8, width), F32),
        ],
        compiler_params=params(),
        name="feed",
    )(mixed, tokens, cotangent, gain_two, w_attn, wa_other, w_in, wi_other, w_out, wo_other)

    wo_grads, wi_grads = pl.pallas_call(
        weight_grads_kernel,
        out_shape=[
            jax.ShapeDtypeStruct((2, w_out.shape[0] + w_attn.shape[0], width), BF),
            jax.ShapeDtypeStruct((2, width, w_in.shape[1]), BF),
        ],
        compiler_params=params(),
        name="weight_grads",
    )(mixed, branch, active, cotangent, normed_two, gpre)

    def join_halves(pair):
        return (pair[0].astype(F32) + swap(pair[1]).astype(F32)).astype(BF)

    wo_sum = reduce_all(join_halves(wo_grads), count)
    wi_sum = reduce_all(join_halves(wi_grads), count)

    back_block = lambda size, cols: pl.BlockSpec((size, cols), lambda i: (blocks - 1 - i, 0))
    gq, gk, gv, halo_back, back_state, back_sum, gblend = pl.pallas_call(
        partial(mixer_backward_kernel, docs),
        grid=(blocks,),
        in_specs=[
            smem,
            back_block(BLOCK, own_cols),
            back_block(BLOCK, own_cols),
            pl.BlockSpec((1, HALO, 1024), lambda i: (blocks - 1 - i, 0, 0)),
            pl.BlockSpec((1, 4, 256, 128), lambda i: (blocks - 1 - i, 0, 0, 0)),
            pl.BlockSpec((1, 4, 8, 128), lambda i: (blocks - 1 - i, 0, 0, 0)),
            whole(blend_both.shape),
            back_block(BLOCK, width),
        ],
        out_specs=[
            back_block(BLOCK, width),
            back_block(BLOCK, width),
            back_block(BLOCK, width),
            whole((HALO, 1024)),
            whole((4, 256, 128)),
            whole((4, 8, 128)),
            whole((2, 4, 8, 128)),
        ],
        out_shape=[
            jax.ShapeDtypeStruct((rows, width), BF),
            jax.ShapeDtypeStruct((rows, width), BF),
            jax.ShapeDtypeStruct((rows, width), BF),
            jax.ShapeDtypeStruct((HALO, 1024), F32),
            jax.ShapeDtypeStruct((4, 256, 128), F32),
            jax.ShapeDtypeStruct((4, 8, 128), F32),
            jax.ShapeDtypeStruct((2, 4, 8, 128), F32),
        ],
        scratch_shapes=[pltpu.VMEM((HALO, 512), F32), pltpu.VMEM((HALO, 512), F32)],
        compiler_params=params(),
        name="mixer_backward",
    )(ends, own, other, prevs, states, sums, blend_both, gmix)
    halo_got, back_state_got, back_sum_got = swap(halo_back), swap(back_state), swap(back_sum)

    gproj, wq_grads = pl.pallas_call(
        partial(finish_kernel, docs),
        in_specs=[smem, smem] + [pl.BlockSpec(memory_space=pltpu.VMEM)] * 9,
        out_shape=[
            jax.ShapeDtypeStruct((rows, 2 * own_cols), BF),
            jax.ShapeDtypeStruct((2, width, own_cols), BF),
        ],
        compiler_params=params(),
        name="finish",
    )(ends, flag, own, other, normed, gq, gk, gv, halo_got, back_state_got, back_sum_got)
    wq_sum = reduce_all(join_halves(wq_grads), count)

    grad_input, ggain_attn = pl.pallas_call(
        input_grad_kernel,
        grid=(4,),
        in_specs=[
            row_block(tall, 2 * own_cols),
            row_block(tall, width),
            row_block(tall, width),
            whole((1, width)),
            whole(wq_own.shape),
            whole(wq_own.shape),
        ],
        out_specs=[row_block(tall, width), whole((8, width))],
        out_shape=[jax.ShapeDtypeStruct((rows, width), BF), jax.ShapeDtypeStruct((8, width), F32)],
        compiler_params=params(),
        name="input_grad",
    )(gproj, tokens, ghid, gain_one, wq_own, wq_other)

    gblend_heads = jnp.sum(gblend[:, :, 0].reshape(2, 8, 64), axis=2)
    gblend_own = gblend_heads[:, :4] + swap(gblend_heads[:, 4:])
    gains = jnp.concatenate([ggain_attn[:1], ggain_mlp[:1]], axis=0)
    gains = gains + swap(gains)
    small = jnp.concatenate([gains, jnp.pad(gblend_own.reshape(1, 8), ((0, 0), (0, width - 8)))], axis=0)
    small = reduce_small(small, count)

    units = w_out.shape[0]
    return (
        output,
        grad_input,
        wq_sum.astype(F32).reshape(w_qkv.shape),
        wo_sum[units:].astype(F32),
        wi_sum.astype(F32),
        wo_sum[:units].astype(F32),
        small[0],
        small[1],
        small[2, :8].reshape(2, 4),
    )


def solution(mesh):
    return jax.shard_map(
        partial(body, mesh.shape["dp"]),
        mesh=mesh,
        in_specs=(
            P(("dp", "tensor"), None),
            P("dp", None),
            P(None, None, "tensor"),
            P("tensor", None),
            P(None, "tensor"),
            P("tensor", None),
            P(),
            P(),
            P(None, "tensor"),
            P(("dp", "tensor"), None),
        ),
        out_specs=(
            P(("dp", "tensor"), None),
            P(("dp", "tensor"), None),
            P(None, None, "tensor"),
            P("tensor", None),
            P(None, "tensor"),
            P("tensor", None),
            P(),
            P(),
            P(None, "tensor"),
        ),
        check_vma=False,
    )
```

```python
from functools import partial

import jax
import jax.numpy as jnp
from jax import lax
from jax.experimental import pallas as pl
from jax.experimental.pallas import tpu as pltpu
from jax.sharding import PartitionSpec as P

BAND = 30
HALO = 32
EXTRA = 64
BLOCK = 128
EPS = 1e-06
BF = jnp.bfloat16
F32 = jnp.float32
VMEM_BYTES = 60 * 1024 * 1024
GELU_A = 0.7978845608028654
GELU_B = 0.044715


def nn(left, right):
    return lax.dot_general(left, right, (((1,), (0,)), ((), ())), preferred_element_type=F32)


def nt(left, right):
    return lax.dot_general(left, right, (((1,), (1,)), ((), ())), preferred_element_type=F32)


def tn(left, right):
    return lax.dot_general(left, right, (((0,), (0,)), ((), ())), preferred_element_type=F32)


def iota(shape, dim):
    return lax.broadcasted_iota(jnp.int32, shape, dim)


def whole(shape):
    return pl.BlockSpec(shape, lambda *_: (0,) * len(shape))


def params():
    return pltpu.CompilerParams(vmem_limit_bytes=VMEM_BYTES)


def cost(micros):
    return pl.CostEstimate(flops=int(micros * 1e7), bytes_accessed=1 << 20, transcendentals=0)


def tie(*values):
    return lax.optimization_barrier(values)


def starts_of(ends_ref, places, docs):
    start = jnp.full(places.shape, ends_ref[docs], jnp.int32)
    for doc in range(docs):
        end = ends_ref[doc]
        start = jnp.where(places >= end, jnp.maximum(start, end), start)
    return start


def start_at(ends_ref, place, docs):
    start = ends_ref[docs]
    for doc in range(docs):
        end = ends_ref[doc]
        start = jnp.where(place >= end, jnp.maximum(start, end), start)
    return start


def norm_project_kernel(x_ref, gain_ref, w_ref, normed_ref, out_ref):
    x = x_ref[...].astype(F32)
    r = lax.rsqrt(jnp.mean(x * x, axis=1, keepdims=True) + EPS)
    normed = (x * r * gain_ref[...]).astype(BF)
    normed_ref[...] = normed
    project(normed, w_ref, out_ref)


def project(normed, w_ref, out_ref):
    cols = w_ref.shape[2]
    for kind in range(3):
        out_ref[:, cols * kind : cols * kind + cols] = nn(normed, w_ref[kind]).astype(BF)


PACKET = 4 * (128 + 16) + 8 * HALO


def pack(packet_ref, pair, state, total):
    base = 144 * pair
    packet_ref[base : base + 64] = (state[:64] + state[64:128]).astype(BF)
    packet_ref[base + 64 : base + 128] = (state[128:192] + state[192:]).astype(BF)
    packet_ref[base + 128 : base + 144] = jnp.broadcast_to(total, (16, 128)).astype(BF)


def pack_halo(packet_ref, kind, pair, rows):
    base = 576 + HALO * (4 * kind + pair)
    packet_ref[base : base + HALO] = rows


def unpack(packet_ref, pair, diag):
    base = 144 * pair
    one = packet_ref[base : base + 64].astype(F32)
    two = packet_ref[base + 64 : base + 128].astype(F32)
    state = jnp.where(diag, jnp.concatenate([one, one, two, two], axis=0), 0.0)
    return state, packet_ref[base + 128 : base + 136].astype(F32)


def unpack_halo(packet_ref, kind, pair):
    base = 576 + HALO * (4 * kind + pair)
    return packet_ref[base : base + HALO]


def first_feature(values):
    return jnp.where(values > 0, values + 1.0, jnp.exp(jnp.minimum(values, 0.0))).astype(BF)


def second_feature(values):
    return jnp.tanh(values).astype(BF)


def pair_diag(rows, cols):
    row = iota((rows, cols), 0)
    col = iota((rows, cols), 1)
    return ((row // 64) % 2) == ((col // 64) % 2)


def project_state_kernel(docs, ends_ref, normed_ref, w_ref, own_ref, out_ref, packet_ref):
    rows = normed_ref.shape[0]
    project(normed_ref[...], w_ref, out_ref)
    member_from = start_at(ends_ref, rows - 1, docs)
    member = iota((rows, 1), 0) >= member_from
    diag = pair_diag(256, 128)
    for pair in range(4):
        src = own_ref if pair < 2 else out_ref
        col = 128 * (pair % 2)
        slot = (pair + 2) % 4
        keys = src[:, 256 + col : 384 + col]
        values = src[:, 512 + col : 640 + col]
        wide = jnp.where(member, keys.astype(F32), 0.0)
        one = jnp.where(member, first_feature(wide).astype(F32), 0.0)
        two = second_feature(wide)
        features = jnp.concatenate([one.astype(BF), two], axis=1)
        state = jnp.where(diag, tn(features, values), 0.0)
        pack(packet_ref, slot, state, jnp.sum(one, axis=0, keepdims=True))
        pack_halo(packet_ref, 0, slot, keys[rows - HALO :])
        pack_halo(packet_ref, 1, slot, values[rows - HALO :])


def block_masks(ends_ref, docs, first):
    row_places = first + iota((1, 256), 1) % BLOCK
    start_row = starts_of(ends_ref, row_places, docs)
    window_places = first - HALO + iota((BLOCK + HALO, 256), 0)
    banded = (window_places <= row_places) & (
        window_places >= jnp.maximum(start_row, row_places - (BAND - 1))
    )
    key_places = first + iota((BLOCK, 256), 0)
    causal = (key_places <= row_places) & (key_places >= start_row)
    col_places = first + iota((BLOCK, 1), 0)
    start_col = starts_of(ends_ref, col_places, docs)
    key_lane = first + iota((BLOCK, BLOCK), 1)
    causal_q = ((key_lane <= col_places) & (key_lane >= start_col)).astype(F32).astype(BF)
    count = (col_places - start_col + 1).astype(F32)
    carried = start_col < first
    member_from = start_at(ends_ref, first + BLOCK - 1, docs)
    member = col_places >= member_from
    keep = member_from < first
    return banded, causal, causal_q, count, carried, member, keep


def stack_heads(values):
    lane = iota(values.shape, 1) % 128
    zero = jnp.zeros_like(values)
    return jnp.concatenate(
        [jnp.where(lane < 64, values, zero), jnp.where(lane >= 64, values, zero)], axis=0
    )


def pick_heads(values):
    half = values.shape[0] // 2
    lane = iota((half, values.shape[1]), 1) % 128
    return jnp.where(lane < 64, values[:half], values[half:])


def pair_front(q, k, prev_k, blend_one, blend_two, carry, masks, ones_diag):
    banded, causal, causal_q, count, carried, member, keep = masks
    wide_q = q.astype(F32)
    wide_k = k.astype(F32)
    q_one = first_feature(wide_q)
    q_two = second_feature(wide_q)
    k_one = first_feature(wide_k)
    k_two = second_feature(wide_k)
    sums = nn(causal_q, k_one) + jnp.where(carried, carry, 0.0)
    total = nn((q_one.astype(F32) * sums).astype(BF), ones_diag)
    ratio_one = blend_one / total
    ratio_two = blend_two / count
    q_scaled = jnp.concatenate(
        [
            (q_one.astype(F32) * ratio_one).astype(BF),
            (q_two.astype(F32) * ratio_two).astype(BF),
        ],
        axis=1,
    )
    k_both = jnp.concatenate([k_one, k_two], axis=1)
    q_stack = stack_heads(q)
    s_stack = stack_heads(q_scaled)
    window = jnp.concatenate([prev_k, k], axis=0)
    scores = jnp.where(banded, nt(window, q_stack) * 0.125, -1e30)
    raised = jnp.exp(scores - jnp.max(scores, axis=0, keepdims=True))
    near = raised * (1.0 / jnp.sum(raised, axis=0, keepdims=True))
    far = jnp.where(causal, nt(k_both, s_stack), 0.0)
    weights = jnp.concatenate([near[:HALO], near[HALO:] + far], axis=0).astype(BF)
    return dict(
        q_one=q_one,
        q_two=q_two,
        k_one=k_one,
        k_two=k_two,
        sums=sums,
        total=total,
        ratio_one=ratio_one,
        ratio_two=ratio_two,
        q_scaled=q_scaled,
        k_both=k_both,
        q_stack=q_stack,
        s_stack=s_stack,
        window=window,
        near=near,
        weights=weights,
    )


def ones_diagonal():
    return pair_diag(128, 128).astype(F32).astype(BF)


def mixer_forward_kernel(
    docs,
    ends_ref,
    own_ref,
    other_ref,
    packet_ref,
    blend_ref,
    mixed_ref,
    state_out_ref,
    sum_out_ref,
    prev_out_ref,
    state_ref,
    sum_ref,
    prev_ref,
):
    index = pl.program_id(0)
    first = index * BLOCK

    @pl.when(index == 0)
    def _():
        for pair in range(4):
            state_ref[pair], sum_ref[pair] = unpack(packet_ref, pair, pair_diag(256, 128))
            for kind in range(2):
                lane = 512 * kind + 128 * pair
                prev_ref[:, lane : lane + 128] = unpack_halo(packet_ref, kind, pair)

    masks = block_masks(ends_ref, docs, first)
    banded, causal, causal_q, count, carried, member, keep = masks
    diag = pair_diag(256, 128)
    ones_diag = ones_diagonal()
    prev_out_ref[0] = prev_ref[...]
    for pair in range(4):
        src = own_ref if pair < 2 else other_ref
        col = 128 * (pair % 2)
        lanes = slice(128 * pair, 128 * pair + 128)
        value_lanes = slice(512 + 128 * pair, 640 + 128 * pair)
        q = src[:, col : col + 128]
        k = src[:, 256 + col : 384 + col]
        v = src[:, 512 + col : 640 + col]
        state = state_ref[pair]
        carry = sum_ref[pair][0:1]
        state_low = state.astype(BF)
        state_out_ref[0, pair] = state_low
        sum_out_ref[0, pair] = sum_ref[pair]
        front = pair_front(
            q, k, prev_ref[:, lanes], blend_ref[0:1, lanes], blend_ref[1:2, lanes], carry, masks, ones_diag
        )
        v_window = jnp.concatenate([prev_ref[:, value_lanes], v], axis=0)
        out = pick_heads(tn(front["weights"], v_window))
        q_carried = jnp.where(carried, front["q_scaled"], jnp.zeros_like(front["q_scaled"]))
        out = out + nn(q_carried, state_low)
        mixed_ref[:, lanes] = out.astype(BF)
        k_member = jnp.where(member, front["k_both"], jnp.zeros_like(front["k_both"]))
        added = jnp.where(diag, tn(k_member, v), 0.0)
        state_ref[pair] = jnp.where(keep, state, 0.0) + added
        sum_ref[pair] = jnp.broadcast_to(front["sums"][BLOCK - 1 : BLOCK], (8, 128))
        prev_ref[:, lanes] = k[BLOCK - HALO :]
        prev_ref[:, value_lanes] = v[BLOCK - HALO :]


def mixer_backward_kernel(
    docs,
    top,
    resumed,
    ends_ref,
    own_ref,
    other_ref,
    prev_ref,
    state_ref,
    sum_ref,
    blend_ref,
    grad_ref,
    *refs,
):
    carried_in = refs[:4] if resumed else None
    gq_ref, gk_ref, gv_ref, halo_ref, back_state_ref, back_sum_ref, blend_out_ref, packet_ref = refs[-8:]
    step = pl.program_id(0)
    first = (top - step) * BLOCK

    @pl.when(step == 0)
    def _():
        for place, ref in enumerate((halo_ref, back_state_ref, back_sum_ref, blend_out_ref)):
            ref[...] = carried_in[place][...] if resumed else jnp.zeros_like(ref)

    masks = block_masks(ends_ref, docs, first)
    banded, causal, causal_q, count, carried, member, keep = masks
    diag = pair_diag(256, 128)
    ones_diag = ones_diagonal()
    for pair in range(4):
        src = own_ref if pair < 2 else other_ref
        col = 128 * (pair % 2)
        lanes = slice(128 * pair, 128 * pair + 128)
        value_lanes = slice(512 + 128 * pair, 640 + 128 * pair)
        q = src[:, col : col + 128]
        k = src[:, 256 + col : 384 + col]
        v = src[:, 512 + col : 640 + col]
        grad = grad_ref[:, lanes]
        front = pair_front(
            q,
            k,
            prev_ref[0, :, lanes],
            blend_ref[0:1, lanes],
            blend_ref[1:2, lanes],
            sum_ref[0, pair][0:1],
            masks,
            ones_diag,
        )
        state = state_ref[0, pair]
        v_window = jnp.concatenate([prev_ref[0, :, value_lanes], v], axis=0)
        g_stack = stack_heads(grad)
        grad_weights = nt(v_window, g_stack)
        near = front["near"]
        inner = near * grad_weights
        dscores = (
            (inner - near * jnp.sum(inner, axis=0, keepdims=True)) * 0.125
        ).astype(BF)
        far = jnp.where(causal, grad_weights[HALO:], 0.0).astype(BF)
        up = pick_heads(tn(far, front["k_both"]))
        g_carried = jnp.where(carried, grad, jnp.zeros_like(grad))
        up = up + nt(g_carried, state)
        up_one = up[:, :128]
        up_two = up[:, 128:]
        q_one = front["q_one"].astype(F32)
        mean_one = nn((q_one * up_one).astype(BF), ones_diag) / front["total"]
        grad_one = front["ratio_one"] * (up_one - mean_one * front["sums"])
        grad_two = front["ratio_two"] * up_two
        tanh_q = jnp.tanh(q.astype(F32))
        slope_q = jnp.exp(jnp.minimum(q.astype(F32), 0.0))
        gq = pick_heads(tn(dscores, front["window"]))
        gq = gq + grad_one * slope_q + grad_two * (1.0 - tanh_q * tanh_q)
        gq_ref[:, lanes] = gq.astype(BF)
        blend_out_ref[0, pair] += jnp.broadcast_to(
            jnp.sum(mean_one, axis=0, keepdims=True) / 64.0, (8, 128)
        )
        blend_out_ref[1, pair] += jnp.broadcast_to(
            jnp.sum(front["q_two"].astype(F32) * up_two / count, axis=0, keepdims=True), (8, 128)
        )

        back = back_state_ref[pair]
        back_low = back.astype(BF)
        back_sum = back_sum_ref[pair][0:1]
        k_member = jnp.where(member, front["k_both"], jnp.zeros_like(front["k_both"]))
        v_member = jnp.where(member, v, jnp.zeros_like(v))
        dv = nn(front["weights"], g_stack)
        dv_own = dv[HALO:] + nn(k_member, back_low)
        weighted = (mean_one * front["q_scaled"][:, :128].astype(F32)).astype(BF)
        dfeat = nn(far, front["s_stack"]) + nt(v_member, back_low)
        d_one = dfeat[:, :128] - tn(causal_q, weighted) - jnp.where(member, back_sum, 0.0)
        d_two = dfeat[:, 128:]
        dk = nn(dscores, front["q_stack"])
        tanh_k = jnp.tanh(k.astype(F32))
        slope_k = jnp.exp(jnp.minimum(k.astype(F32), 0.0))
        gk = dk[HALO:] + d_one * slope_k + d_two * (1.0 - tanh_k * tanh_k)
        gk_ref[: BLOCK - HALO, lanes] = gk[: BLOCK - HALO].astype(BF)
        gk_ref[BLOCK - HALO :, lanes] = (gk[BLOCK - HALO :] + halo_ref[:, lanes]).astype(BF)
        gv_ref[: BLOCK - HALO, lanes] = dv_own[: BLOCK - HALO].astype(BF)
        gv_ref[BLOCK - HALO :, lanes] = (dv_own[BLOCK - HALO :] + halo_ref[:, value_lanes]).astype(BF)
        halo_ref[:, lanes] = dk[:HALO]
        halo_ref[:, value_lanes] = dv[:HALO]
        q_carried = jnp.where(carried, front["q_scaled"], jnp.zeros_like(front["q_scaled"]))
        added = jnp.where(diag, tn(q_carried, grad), 0.0)
        back_state_ref[pair] = jnp.where(keep, back, 0.0) + added
        added_sum = jnp.sum(
            jnp.where(carried, weighted.astype(F32), 0.0), axis=0, keepdims=True
        )
        back_sum_ref[pair] = jnp.broadcast_to(
            jnp.where(keep, back_sum, 0.0) + added_sum, (8, 128)
        )

    @pl.when(first == 0)
    def _():
        for pair in range(4):
            slot = (pair + 2) % 4
            pack(packet_ref, slot, back_state_ref[pair], back_sum_ref[pair][0:1])
            for kind in range(2):
                lane = 512 * kind + 128 * pair
                pack_halo(packet_ref, kind, slot, halo_ref[:, lane : lane + 128].astype(BF))


def feed_kernel(
    mixed_ref,
    x_ref,
    cot_ref,
    gain_ref,
    wa_own_ref,
    wa_other_ref,
    wi_own_ref,
    wi_other_ref,
    wo_own_ref,
    wo_other_ref,
    out_ref,
    normed_ref,
    active_ref,
    gpre_ref,
    ghid_ref,
    branch_ref,
    gmix_ref,
    ggain_ref,
):
    x = x_ref[...].astype(F32)
    hidden = x + (nn(mixed_ref[:, :256], wa_own_ref[...]) + nn(mixed_ref[:, 256:], wa_other_ref[...]))
    r = lax.rsqrt(jnp.mean(hidden * hidden, axis=1, keepdims=True) + EPS)
    y = hidden * r
    gain = gain_ref[...]
    normed = (y * gain).astype(BF)
    normed_ref[...] = normed
    grad = cot_ref[...]
    total = hidden
    back = None
    for half, (wi_ref, wo_ref) in enumerate(((wi_own_ref, wo_own_ref), (wi_other_ref, wo_other_ref))):
        width = wi_ref.shape[1]
        for part in range(2):
            cols = slice(part * width // 2, (part + 1) * width // 2)
            dest = slice(half * width + part * width // 2, half * width + (part + 1) * width // 2)
            u = nn(normed, wi_ref[:, cols])
            square = u * u
            t = jnp.tanh(u * (GELU_A + (GELU_A * GELU_B) * square))
            gate = 0.5 + 0.5 * t
            active = (u * gate).astype(BF)
            slope = gate + u * (0.5 - 0.5 * t * t) * (GELU_A + (3.0 * GELU_A * GELU_B) * square)
            active_ref[:, dest] = active
            total = total + nn(active, wo_ref[cols, :])
            gact = nt(grad, wo_ref[cols, :])
            gpre = (gact * slope).astype(BF)
            gpre_ref[:, dest] = gpre
            term = nt(gpre, wi_ref[:, cols])
            back = term if back is None else back + term
    out_ref[...] = total.astype(BF)
    scaled = back * gain
    ghid = grad.astype(F32) + r * (scaled - y * jnp.mean(scaled * y, axis=1, keepdims=True))
    ghid_ref[...] = ghid
    branch = ghid.astype(BF)
    branch_ref[...] = branch
    gmix_ref[:, :256] = nt(branch, wa_own_ref[...]).astype(BF)
    gmix_ref[:, 256:] = nt(branch, wa_other_ref[...]).astype(BF)

    @pl.when(pl.program_id(0) == 0)
    def _():
        ggain_ref[...] = jnp.zeros_like(ggain_ref)

    ggain_ref[0:1] += jnp.sum(back * y, axis=0, keepdims=True)


def out_grads_kernel(mixed_ref, branch_ref, active_ref, cot_ref, *grad_refs):
    units = active_ref.shape[1] // 2
    heads = mixed_ref.shape[1] // 2
    for half, grad_ref in enumerate(grad_refs):
        active = active_ref[:, units * half : units * (half + 1)]
        mixed = mixed_ref[:, heads * half : heads * half + heads // 2]
        grad_ref[:units] = tn(active, cot_ref[...]).astype(BF)
        grad_ref[units:] = tn(mixed, branch_ref[...]).astype(BF)


def in_grads_kernel(mixed_ref, branch_ref, normed_ref, gpre_ref, *grad_refs):
    units = gpre_ref.shape[1] // 2
    heads = mixed_ref.shape[1] // 2
    width = normed_ref.shape[1]
    for half, grad_ref in enumerate(grad_refs):
        mixed = mixed_ref[:, heads * half + heads // 2 : heads * (half + 1)]
        grad_ref[: heads // 2] = tn(mixed, branch_ref[...]).astype(BF)
        for part in range(2):
            first = units * half + part * units // 2
            row = heads // 2 + width * part
            grad_ref[row : row + width] = tn(normed_ref[...], gpre_ref[:, first : first + units // 2]).astype(BF)


def finish_kernel(
    docs,
    ends_ref,
    flag_ref,
    own_ref,
    other_ref,
    normed_ref,
    packet_ref,
    gblend_ref,
    ggain_ref,
    gain_ref,
    w_own_ref,
    w_other_ref,
    *refs,
):
    *grad_refs, gproj_ref, wgrad_own_ref, wgrad_sent_ref = refs

    def grad_rows(kind, lanes):
        parts = [ref[:, lanes] for ref in grad_refs[kind::3]]
        return jnp.concatenate(parts, axis=0)

    rows = own_ref.shape[0]
    flag = flag_ref[0]
    member_from = start_at(ends_ref, rows - 1, docs)
    member = (iota((rows, 1), 0) >= member_from) & (flag == 0)
    live = flag == 0
    diag = pair_diag(256, 128)
    for pair in range(4):
        src = own_ref if pair < 2 else other_ref
        col = 128 * (pair % 2)
        lanes = slice(128 * pair, 128 * pair + 128)
        base = 768 * (pair // 2) + col
        k = src[:, 256 + col : 384 + col].astype(F32)
        v = src[:, 512 + col : 640 + col]
        back, back_sum = unpack(packet_ref, pair, diag)
        back, back_sum = back.astype(BF), back_sum[0:1]
        t = jnp.tanh(k)
        slope = jnp.exp(jnp.minimum(k, 0.0))
        k_both = jnp.concatenate([first_feature(k), t.astype(BF)], axis=1)
        dfeat = nt(v, back)
        extra_k = (dfeat[:, :128] - back_sum) * slope + dfeat[:, 128:] * (1.0 - t * t)
        extra_v = nn(k_both, back)
        gk = grad_rows(1, lanes).astype(F32) + jnp.where(member, extra_k, 0.0)
        gv = grad_rows(2, lanes).astype(F32) + jnp.where(member, extra_v, 0.0)
        halo_k = jnp.where(live, unpack_halo(packet_ref, 0, pair).astype(F32), 0.0)
        halo_v = jnp.where(live, unpack_halo(packet_ref, 1, pair).astype(F32), 0.0)
        cut = rows - HALO
        gproj_ref[:, base : base + 128] = grad_rows(0, lanes)
        gproj_ref[:cut, base + 256 : base + 384] = gk[:cut].astype(BF)
        gproj_ref[cut:, base + 256 : base + 384] = (gk[cut:] + halo_k).astype(BF)
        gproj_ref[:cut, base + 512 : base + 640] = gv[:cut].astype(BF)
        gproj_ref[cut:, base + 512 : base + 640] = (gv[cut:] + halo_v).astype(BF)
    width = normed_ref.shape[1]
    cols = w_own_ref.shape[2]
    normed = normed_ref[...]
    ones = jnp.ones((1, cols), F32)
    gain_grad = jnp.zeros((1, width), F32)
    for half, (wgrad_ref, w_ref) in enumerate(((wgrad_own_ref, w_own_ref), (wgrad_sent_ref, w_other_ref))):
        for kind in range(3):
            first = 3 * cols * half + cols * kind
            wgrad = tn(normed, gproj_ref[:, first : first + cols])
            wgrad_ref[width * kind : width * kind + width] = wgrad.astype(BF)
            products = wgrad * w_ref[kind].astype(F32)
            high = products.astype(BF)
            low = (products - high.astype(F32)).astype(BF)
            gain_grad = gain_grad + nt(ones.astype(BF), high) + nt(ones.astype(BF), low)
    gain_grad = gain_grad / gain_ref[...]
    for half, wgrad_ref in enumerate((wgrad_own_ref, wgrad_sent_ref)):
        blends = [
            jnp.concatenate([gblend_ref[kind, 2 * half + pair][0:1] for pair in range(2)], axis=1)
            for kind in range(2)
        ]
        gains = [gain_grad[:, :256], gain_grad[:, 256:], ggain_ref[0:1, :256], ggain_ref[0:1, 256:]]
        extra = jnp.concatenate(blends + gains + [jnp.zeros((10, 256), F32)], axis=0)
        wgrad_ref[3 * width : 3 * width + 16] = extra.astype(BF)
        wgrad_ref[3 * width + 16 :] = jnp.zeros((EXTRA - 16, 256), BF)


def merged(low, mine, got):
    return jnp.where(low, mine, got), jnp.where(low, got, mine)


def feed_output_kernel(bits_ref, out_mine_ref, out_got_ref, in_mine_ref, in_got_ref, wo_ref, wa_ref, wi_ref):
    units, width = wo_ref.shape
    rows = out_mine_ref.shape[0]
    quarter = wa_ref.shape[0] // 2
    first, second = merged(bits_ref[0] == 0, out_mine_ref[...], out_got_ref[...])
    wo_ref[:rows] = first.astype(F32)
    wo_ref[rows:] = second[: units - rows].astype(F32)
    wa_ref[:quarter] = second[units - rows :].astype(F32)
    first, second = merged(bits_ref[1] == 0, in_mine_ref[...], in_got_ref[...])
    wa_ref[quarter:] = first[:quarter].astype(F32)
    upper = rows - quarter
    wi_ref[:upper, : units // 2] = first[quarter:].astype(F32)
    wi_ref[upper:, : units // 2] = second[: width - upper].astype(F32)
    wi_ref[:, units // 2 :] = second[width - upper :].astype(F32)


def qkv_output_kernel(bits_ref, a_mine_ref, a_got_ref, b_mine_ref, b_got_ref, wq_ref, rest_ref):
    rows = a_mine_ref.shape[0]
    top, upper = merged(bits_ref[0] == 0, a_mine_ref[...], a_got_ref[...])
    wq_ref[:rows] = top.astype(F32)
    wq_ref[rows : 2 * rows] = upper.astype(F32)
    lower, bottom = merged(bits_ref[1] == 0, b_mine_ref[...], b_got_ref[...])
    wq_ref[2 * rows : 3 * rows] = lower.astype(F32)
    wq_ref[3 * rows :] = bottom[: rows - EXTRA].astype(F32)
    rest_ref[...] = bottom[rows - EXTRA : rows - EXTRA + 8].astype(F32)


def input_grad_kernel(gproj_ref, x_ref, ghid_ref, gain_ref, w_own_ref, w_other_ref, out_ref):
    cols = w_own_ref.shape[2]
    gnormed = None
    for half, w_ref in enumerate((w_own_ref, w_other_ref)):
        for kind in range(3):
            first = 3 * cols * half + cols * kind
            term = nt(gproj_ref[:, first : first + cols], w_ref[kind])
            gnormed = term if gnormed is None else gnormed + term
    x = x_ref[...].astype(F32)
    r = lax.rsqrt(jnp.mean(x * x, axis=1, keepdims=True) + EPS)
    y = x * r
    scaled = gnormed * gain_ref[...]
    grad = ghid_ref[...] + r * (scaled - y * jnp.mean(scaled * y, axis=1, keepdims=True))
    out_ref[...] = grad.astype(BF)


def flip(values, count, stride):
    return lax.ppermute(values, "dp", [(src, src ^ stride) for src in range(count)])


def strides_of(count):
    strides = []
    stride = 1
    while stride < count:
        strides.append(stride)
        stride *= 2
    return strides


class Reduction:
    def __init__(self, stacks, count, whole_late=False):
        self.stacks = [[(term, 0) for term in terms] for terms in stacks]
        self.rows = [terms[0].shape[0] for terms in stacks]
        self.count = count
        strides = strides_of(count)
        self.orders = [strides, strides[1::-1] + strides[2:]]
        self.steps = len(strides)
        self.taken = 0
        self.halved = min(2, self.steps) if whole_late else self.steps
        self.place = lax.axis_index("dp")
        self.held = None

    def bit(self, stride):
        return (self.place // stride) % 2

    def after(self, *tokens):
        if self.held is not None:
            *self.gots, first, second = tie(*self.gots, *self.held)
            self.held = [first, second]
            return tokens
        news = [terms[-1][0] for terms in self.stacks]
        if news[0] is news[1]:
            news = news[:1]
        tied = tie(*news, *tokens)
        for stack in range(2):
            offset = self.stacks[stack][-1][1]
            self.stacks[stack][-1] = (tied[min(stack, len(news) - 1)], offset)
        return tied[len(news) :]

    def cut(self, stack, rows, skip):
        total = None
        for term, offset in self.stacks[stack]:
            part = lax.dynamic_slice_in_dim(term, offset + skip, rows, 0).astype(F32)
            total = part if total is None else total + part
        return total.astype(BF)

    def outgoing(self):
        cuts = []
        for stack in range(2):
            if self.taken < self.halved:
                self.rows[stack] //= 2
                bit = self.bit(self.orders[stack][self.taken])
                cuts.append(self.cut(stack, self.rows[stack], (1 - bit) * self.rows[stack]))
            else:
                cuts.append(self.cut(stack, self.rows[stack], 0))
        return cuts if self.taken < 2 else [jnp.concatenate(cuts, axis=0)]

    def send(self, cuts):
        gots = [flip(cut, self.count, self.orders[stack][self.taken]) for stack, cut in enumerate(cuts)]
        for stack in range(2):
            skip = self.rows[0] if stack == 1 and len(cuts) == 1 else 0
            got = gots[min(stack, len(cuts) - 1)]
            if self.taken < self.halved:
                bit = self.bit(self.orders[stack][self.taken])
                kept = [(term, offset + bit * self.rows[stack]) for term, offset in self.stacks[stack]]
            else:
                kept = [(cuts[0], skip)]
            self.stacks[stack] = kept + [(got, skip)]
        self.taken += 1

    def start_gather(self):
        self.held = [self.cut(stack, self.rows[stack], 0) for stack in range(2)]

    def gather_outgoing(self):
        return list(self.held) if self.halved <= 2 else [jnp.concatenate(self.held, axis=0)]

    def gather_send(self, cuts):
        step = self.halved - 1
        gots = [flip(cut, self.count, self.orders[stack][step]) for stack, cut in enumerate(cuts)]
        if len(gots) == 1:
            first = self.held[0].shape[0]
            gots = [gots[0][:first], gots[0][first:]]
        self.gots = gots
        self.halved = step

    def last_bits(self):
        return jnp.stack([self.bit(order[0]) if order else 0 * self.place for order in self.orders])

    def parts(self):
        if self.steps > 0:
            return [self.held[0], self.gots[0], self.held[1], self.gots[1]]
        halves = []
        for held in self.held:
            middle = held.shape[0] // 2
            halves += [held[:middle], held[middle:]]
        return halves

    def gather_take(self):
        for stack in range(2):
            low = self.bit(self.orders[stack][self.halved]) == 0
            mine, got = self.held[stack], self.gots[stack]
            self.held[stack] = jnp.concatenate([jnp.where(low, mine, got), jnp.where(low, got, mine)], axis=0)


def swap(values):
    return lax.ppermute(values, "tensor", [(0, 1), (1, 0)])


def body(count, tokens, lengths, w_qkv, w_attn, w_in, w_out, gain_attn, gain_mlp, blend, cotangent):
    rows, width = tokens.shape
    docs = lengths.shape[1]
    half = lax.axis_index("tensor").astype(jnp.int32)
    blocks = rows // BLOCK

    wq_own = w_qkv.transpose(1, 0, 2)
    wq_other = swap(wq_own)
    wa_other, wi_other, wo_other = swap(w_attn), swap(w_in), swap(w_out)
    blend_both = jnp.repeat(jnp.concatenate([blend, swap(blend)], axis=1), 64, axis=1)
    ends = jnp.concatenate([jnp.cumsum(lengths[0]), jnp.zeros((1,), jnp.int32)]).astype(jnp.int32) - half * rows
    flag = half.reshape(1)
    gain_one = gain_attn.reshape(1, width)
    gain_two = gain_mlp.reshape(1, width)
    smem = pl.BlockSpec(memory_space=pltpu.SMEM)

    def row_block(size, cols):
        return pl.BlockSpec((size, cols), lambda i: (i, 0))

    own_cols = 3 * wq_own.shape[2]
    normed, own = pl.pallas_call(
        norm_project_kernel,
        grid=(4,),
        in_specs=[row_block(rows // 4, width), whole((1, width)), whole(wq_own.shape)],
        out_specs=[row_block(rows // 4, width), row_block(rows // 4, own_cols)],
        out_shape=[jax.ShapeDtypeStruct((rows, width), BF), jax.ShapeDtypeStruct((rows, own_cols), BF)],
        compiler_params=params(),
        cost_estimate=cost(5),
        name="norm_project",
    )(tokens, gain_one, wq_own)
    other, packet = pl.pallas_call(
        partial(project_state_kernel, docs),
        in_specs=[smem] + [pl.BlockSpec(memory_space=pltpu.VMEM)] * 3,
        out_shape=[
            jax.ShapeDtypeStruct((rows, own_cols), BF),
            jax.ShapeDtypeStruct((PACKET, 128), BF),
        ],
        compiler_params=params(),
        cost_estimate=cost(5),
        name="project_state",
    )(ends, normed, wq_other, own)
    packet = swap(packet)

    mixed, states, sums, prevs = pl.pallas_call(
        partial(mixer_forward_kernel, docs),
        grid=(blocks,),
        in_specs=[
            smem,
            row_block(BLOCK, own_cols),
            row_block(BLOCK, own_cols),
            whole((PACKET, 128)),
            whole(blend_both.shape),
        ],
        out_specs=[
            row_block(BLOCK, width),
            pl.BlockSpec((1, 4, 256, 128), lambda i: (i, 0, 0, 0)),
            pl.BlockSpec((1, 4, 8, 128), lambda i: (i, 0, 0, 0)),
            pl.BlockSpec((1, HALO, 1024), lambda i: (i, 0, 0)),
        ],
        out_shape=[
            jax.ShapeDtypeStruct((rows, width), BF),
            jax.ShapeDtypeStruct((blocks, 4, 256, 128), BF),
            jax.ShapeDtypeStruct((blocks, 4, 8, 128), F32),
            jax.ShapeDtypeStruct((blocks, HALO, 1024), BF),
        ],
        scratch_shapes=[
            pltpu.VMEM((4, 256, 128), F32),
            pltpu.VMEM((4, 8, 128), F32),
            pltpu.VMEM((HALO, 1024), BF),
        ],
        compiler_params=params(),
        cost_estimate=cost(20),
        name="mixer_forward",
    )(ends, own, other, packet, blend_both)

    hidden_units = 2 * w_in.shape[1]
    tall = rows // 4
    output, normed_two, active, gpre, ghid, branch, gmix, ggain_mlp = pl.pallas_call(
        feed_kernel,
        grid=(4,),
        in_specs=[
            row_block(tall, width),
            row_block(tall, width),
            row_block(tall, width),
            whole((1, width)),
            whole(w_attn.shape),
            whole(w_attn.shape),
            whole(w_in.shape),
            whole(w_in.shape),
            whole(w_out.shape),
            whole(w_out.shape),
        ],
        out_specs=[
            row_block(tall, width),
            row_block(tall, width),
            row_block(tall, hidden_units),
            row_block(tall, hidden_units),
            row_block(tall, width),
            row_block(tall, width),
            row_block(tall, width),
            whole((8, width)),
        ],
        out_shape=[
            jax.ShapeDtypeStruct((rows, width), BF),
            jax.ShapeDtypeStruct((rows, width), BF),
            jax.ShapeDtypeStruct((rows, hidden_units), BF),
            jax.ShapeDtypeStruct((rows, hidden_units), BF),
            jax.ShapeDtypeStruct((rows, width), F32),
            jax.ShapeDtypeStruct((rows, width), BF),
            jax.ShapeDtypeStruct((rows, width), BF),
            jax.ShapeDtypeStruct((8, width), F32),
        ],
        compiler_params=params(),
        cost_estimate=cost(20),
        name="feed",
    )(mixed, tokens, cotangent, gain_two, w_attn, wa_other, w_in, wi_other, w_out, wo_other)

    units = w_out.shape[0]
    quarter = w_attn.shape[0] // 2
    out_shape = jax.ShapeDtypeStruct((units + quarter, width), BF)
    out_own, out_sent = pl.pallas_call(
        out_grads_kernel,
        out_shape=[out_shape, out_shape],
        compiler_params=params(),
        cost_estimate=cost(6),
        name="out_grads",
    )(mixed, branch, active, cotangent)
    normed_two, gpre, out_sent = tie(normed_two, gpre, out_sent)
    in_shape = jax.ShapeDtypeStruct((quarter + units, width), BF)
    in_own, in_sent = pl.pallas_call(
        in_grads_kernel,
        out_shape=[in_shape, in_shape],
        compiler_params=params(),
        cost_estimate=cost(6),
        name="in_grads",
    )(mixed, branch, normed_two, gpre)
    feed_sum = Reduction([[out_own, swap(out_sent)], [in_own, swap(in_sent)]], count)
    wanted = feed_sum.steps
    if wanted > 0:
        cuts = feed_sum.outgoing()
        gmix, *cuts = tie(gmix, *cuts)
        feed_sum.send(cuts)

    def mixer_backward(first_block, per_call, grads, carried):
        top = first_block + per_call - 1

        def back_block(*shape):
            return pl.BlockSpec(shape, lambda i: (top - i,) + (0,) * (len(shape) - 1))

        def call_block(*shape):
            return pl.BlockSpec(shape, lambda i: (per_call - 1 - i,) + (0,) * (len(shape) - 1))

        carry_shapes = ((HALO, 1024), (4, 256, 128), (4, 8, 128), (2, 4, 8, 128))
        return pl.pallas_call(
            partial(mixer_backward_kernel, docs, top, len(carried) > 0),
            grid=(per_call,),
            in_specs=[
                smem,
                back_block(BLOCK, own_cols),
                back_block(BLOCK, own_cols),
                back_block(1, HALO, 1024),
                back_block(1, 4, 256, 128),
                back_block(1, 4, 8, 128),
                whole(blend_both.shape),
                back_block(BLOCK, width),
            ]
            + [whole(c.shape) for c in carried],
            out_specs=[call_block(BLOCK, width)] * 3 + [whole(shape) for shape in carry_shapes] + [whole((PACKET, 128))],
            out_shape=[jax.ShapeDtypeStruct((per_call * BLOCK, width), BF)] * 3
            + [jax.ShapeDtypeStruct(shape, F32) for shape in carry_shapes]
            + [jax.ShapeDtypeStruct((PACKET, 128), BF)],
            compiler_params=params(),
            cost_estimate=cost(3 * per_call),
            name="mixer_backward",
        )(ends, own, other, prevs, states, sums, blend_both, grads, *carried)

    sizes = (blocks // 2, blocks // 4, blocks // 4)
    left = blocks
    grads = []
    carried = ()
    for call, size in enumerate(sizes):
        left -= size
        *parts, halo_back, back_state, back_sum, gblend, packet_back = mixer_backward(left, size, gmix, carried)
        grads.insert(0, parts)
        if wanted > call + 1:
            back_state, packet_back = feed_sum.after(back_state, packet_back)
            cuts = feed_sum.outgoing()
            back_state, packet_back, *cuts = tie(back_state, packet_back, *cuts)
            feed_sum.send(cuts)
        carried = (halo_back, back_state, back_sum, gblend)
    packet_got = swap(packet_back)

    gproj, wq_mine, wq_sent = pl.pallas_call(
        partial(finish_kernel, docs),
        in_specs=[smem, smem] + [pl.BlockSpec(memory_space=pltpu.VMEM)] * (9 + 3 * len(sizes)),
        out_shape=[
            jax.ShapeDtypeStruct((rows, 2 * own_cols), BF),
            jax.ShapeDtypeStruct((3 * width + EXTRA, own_cols // 3), BF),
            jax.ShapeDtypeStruct((3 * width + EXTRA, own_cols // 3), BF),
        ],
        compiler_params=params(),
        cost_estimate=cost(8),
        name="finish",
    )(
        ends,
        flag,
        own,
        other,
        normed,
        packet_got,
        gblend,
        ggain_mlp,
        gain_one,
        wq_own,
        wq_other,
        *[grad for parts in grads for grad in parts],
    )
    def input_gradient(gproj):
        return pl.pallas_call(
            input_grad_kernel,
            grid=(4,),
            in_specs=[
                row_block(tall, 2 * own_cols),
                row_block(tall, width),
                row_block(tall, width),
                whole((1, width)),
                whole(wq_own.shape),
                whole(wq_own.shape),
            ],
            out_specs=row_block(tall, width),
            out_shape=jax.ShapeDtypeStruct((rows, width), BF),
            compiler_params=params(),
            cost_estimate=cost(7),
            name="input_grad",
        )(gproj, tokens, ghid, gain_one, wq_own, wq_other)

    if wanted > 0:
        (wq_sent,) = feed_sum.after(wq_sent)
    while feed_sum.taken < wanted:
        feed_sum.send(feed_sum.outgoing())
    wq_got = swap(wq_sent)
    cut = wq_got.shape[0] // 2
    wq_sums = Reduction([[wq_mine[:cut], wq_got[:cut]], [wq_mine[cut:], wq_got[cut:]]], count, True)
    feed_sum.start_gather()
    first_round = True
    while feed_sum.halved > 0:
        feed_cuts = feed_sum.gather_outgoing()
        wq_cuts = wq_sums.outgoing() if wq_sums.taken < wanted else []
        gproj, *cuts = tie(gproj, *wq_cuts, *feed_cuts)
        wq_cuts, feed_cuts = cuts[: len(wq_cuts)], cuts[len(wq_cuts) :]
        if wq_cuts:
            wq_sums.send(wq_cuts)
        feed_sum.gather_send(feed_cuts)
        if first_round:
            first_round = False
            grad_input = input_gradient(gproj)
            (grad_input,) = wq_sums.after(grad_input)
        if feed_sum.halved > 0:
            feed_sum.gather_take()
    if first_round:
        grad_input = input_gradient(gproj)
    while wq_sums.taken < wanted:
        wq_sums.send(wq_sums.outgoing())
    wq_sums.start_gather()
    feed_parts = feed_sum.parts()
    if wanted > 1:
        *feed_parts, first, second = tie(*feed_parts, *wq_sums.held)
        wq_sums.held = [first, second]
    wo_grad, wa_grad, wi_grad = pl.pallas_call(
        feed_output_kernel,
        in_specs=[smem] + [pl.BlockSpec(memory_space=pltpu.VMEM)] * 4,
        out_shape=[
            jax.ShapeDtypeStruct(w_out.shape, F32),
            jax.ShapeDtypeStruct(w_attn.shape, F32),
            jax.ShapeDtypeStruct(w_in.shape, F32),
        ],
        compiler_params=params(),
        cost_estimate=cost(3),
        name="feed_output",
    )(feed_sum.last_bits(), *feed_parts)
    while wq_sums.halved > 0:
        wq_sums.gather_send(wq_sums.gather_outgoing())
        if wq_sums.halved > 0:
            wq_sums.gather_take()
    wq_grad, rest = pl.pallas_call(
        qkv_output_kernel,
        in_specs=[smem] + [pl.BlockSpec(memory_space=pltpu.VMEM)] * 4,
        out_shape=[
            jax.ShapeDtypeStruct((3 * width, own_cols // 3), F32),
            jax.ShapeDtypeStruct((8, own_cols // 3), F32),
        ],
        compiler_params=params(),
        cost_estimate=cost(3),
        name="qkv_output",
    )(wq_sums.last_bits(), *wq_sums.parts())

    return (
        output,
        grad_input,
        wq_grad.reshape(wq_own.shape).transpose(1, 0, 2),
        wa_grad,
        wi_grad,
        wo_grad,
        rest[2:4].reshape(width),
        rest[4:6].reshape(width),
        jnp.sum(rest[:2].reshape(2, 4, 64), axis=2),
    )


def solution(mesh):
    return jax.shard_map(
        partial(body, mesh.shape["dp"]),
        mesh=mesh,
        in_specs=(
            P(("dp", "tensor"), None),
            P("dp", None),
            P(None, None, "tensor"),
            P("tensor", None),
            P(None, "tensor"),
            P("tensor", None),
            P(),
            P(),
            P(None, "tensor"),
            P(("dp", "tensor"), None),
        ),
        out_specs=(
            P(("dp", "tensor"), None),
            P(("dp", "tensor"), None),
            P(None, None, "tensor"),
            P("tensor", None),
            P(None, "tensor"),
            P("tensor", None),
            P(),
            P(),
            P(None, "tensor"),
        ),
        check_vma=False,
    )
```

```python
from functools import partial

import jax
import jax.numpy as jnp
from jax import lax
from jax.experimental import pallas as pl
from jax.experimental.pallas import tpu as pltpu
from jax.sharding import PartitionSpec as P

BAND = 30
HALO = 32
EXTRA = 64
BLOCK = 128
EPS = 1e-06
BF = jnp.bfloat16
F32 = jnp.float32
GELU_A = 0.7978845608028654
GELU_B = 0.044715


def nn(left, right):
    return lax.dot_general(left, right, (((1,), (0,)), ((), ())), preferred_element_type=F32)


def nt(left, right):
    return lax.dot_general(left, right, (((1,), (1,)), ((), ())), preferred_element_type=F32)


def tn(left, right):
    return lax.dot_general(left, right, (((0,), (0,)), ((), ())), preferred_element_type=F32)


def iota(shape, dim):
    return lax.broadcasted_iota(jnp.int32, shape, dim)


def whole(shape):
    return pl.BlockSpec(shape, lambda *_: (0,) * len(shape))


def params(mebibytes):
    return pltpu.CompilerParams(vmem_limit_bytes=mebibytes << 20)


def cost(micros):
    return pl.CostEstimate(flops=int(micros * 1e7), bytes_accessed=1 << 20, transcendentals=0)


def tie(*values):
    return lax.optimization_barrier(values)


def document_ends(lengths_ref, rows):
    end = -lax.axis_index("tensor") * rows
    ends = [end]
    for doc in range(lengths_ref.shape[1]):
        end = end + lengths_ref[0, doc]
        ends.append(end)
    return ends[1:] + ends[:1]


def starts_of(ends, places):
    start = jnp.full(places.shape, ends[-1], jnp.int32)
    for end in ends[:-1]:
        start = jnp.where(places >= end, jnp.maximum(start, end), start)
    return start


def start_at(ends, place):
    start = ends[-1]
    for end in ends[:-1]:
        start = jnp.where(place >= end, jnp.maximum(start, end), start)
    return start


def norm_project_kernel(x_ref, gain_ref, w_ref, normed_ref, out_ref):
    x = x_ref[...].astype(F32)
    r = lax.rsqrt(jnp.mean(x * x, axis=1, keepdims=True) + EPS)
    normed = (x * r * gain_ref[...]).astype(BF)
    normed_ref[...] = normed
    project(normed, w_ref, out_ref)


def project(normed, w_ref, out_ref):
    cols = w_ref.shape[2]
    for kind in range(3):
        out_ref[:, cols * kind : cols * kind + cols] = nn(normed, w_ref[kind]).astype(BF)


PACKET = 4 * (128 + 16) + 8 * HALO


def pack(packet_ref, pair, state, total):
    base = 144 * pair
    packet_ref[base : base + 64] = (state[:64] + state[64:128]).astype(BF)
    packet_ref[base + 64 : base + 128] = (state[128:192] + state[192:]).astype(BF)
    packet_ref[base + 128 : base + 144] = jnp.broadcast_to(total, (16, 128)).astype(BF)


def pack_halo(packet_ref, kind, pair, rows):
    base = 576 + HALO * (4 * kind + pair)
    packet_ref[base : base + HALO] = rows


def unpack(packet_ref, pair, diag):
    base = 144 * pair
    one = packet_ref[base : base + 64].astype(F32)
    two = packet_ref[base + 64 : base + 128].astype(F32)
    state = jnp.where(diag, jnp.concatenate([one, one, two, two], axis=0), 0.0)
    return state, packet_ref[base + 128 : base + 136].astype(F32)


def unpack_halo(packet_ref, kind, pair):
    base = 576 + HALO * (4 * kind + pair)
    return packet_ref[base : base + HALO]


def first_feature(values):
    return jnp.where(values > 0, values + 1.0, jnp.exp(jnp.minimum(values, 0.0))).astype(BF)


def second_feature(values):
    return jnp.tanh(values).astype(BF)


def pair_diag(rows, cols):
    row = iota((rows, cols), 0)
    col = iota((rows, cols), 1)
    return ((row // 64) % 2) == ((col // 64) % 2)


def project_state_kernel(lengths_ref, normed_ref, w_ref, own_ref, out_ref, packet_ref):
    rows = normed_ref.shape[0]
    project(normed_ref[...], w_ref, out_ref)
    member_from = start_at(document_ends(lengths_ref, rows), rows - 1)
    member = iota((rows, 1), 0) >= member_from
    diag = pair_diag(256, 128)
    for pair in range(4):
        src = own_ref if pair < 2 else out_ref
        col = 128 * (pair % 2)
        slot = (pair + 2) % 4
        keys = src[:, 256 + col : 384 + col]
        values = src[:, 512 + col : 640 + col]
        wide = jnp.where(member, keys.astype(F32), 0.0)
        one = jnp.where(member, first_feature(wide).astype(F32), 0.0)
        two = second_feature(wide)
        features = jnp.concatenate([one.astype(BF), two], axis=1)
        state = jnp.where(diag, tn(features, values), 0.0)
        pack(packet_ref, slot, state, jnp.sum(one, axis=0, keepdims=True))
        pack_halo(packet_ref, 0, slot, keys[rows - HALO :])
        pack_halo(packet_ref, 1, slot, values[rows - HALO :])


def block_masks(ends, first):
    row_places = first + iota((1, 256), 1) % BLOCK
    start_row = starts_of(ends, row_places)
    window_places = first - HALO + iota((BLOCK + HALO, 256), 0)
    banded = (window_places <= row_places) & (
        window_places >= jnp.maximum(start_row, row_places - (BAND - 1))
    )
    key_places = first + iota((BLOCK, 256), 0)
    causal = (key_places <= row_places) & (key_places >= start_row)
    col_places = first + iota((BLOCK, 1), 0)
    start_col = starts_of(ends, col_places)
    key_lane = first + iota((BLOCK, BLOCK), 1)
    causal_q = ((key_lane <= col_places) & (key_lane >= start_col)).astype(F32).astype(BF)
    count = (col_places - start_col + 1).astype(F32)
    carried = start_col < first
    member_from = start_at(ends, first + BLOCK - 1)
    member = col_places >= member_from
    keep = member_from < first
    return banded, causal, causal_q, count, carried, member, keep


def stack_heads(values):
    lane = iota(values.shape, 1) % 128
    zero = jnp.zeros_like(values)
    return jnp.concatenate(
        [jnp.where(lane < 64, values, zero), jnp.where(lane >= 64, values, zero)], axis=0
    )


def pick_heads(values):
    half = values.shape[0] // 2
    lane = iota((half, values.shape[1]), 1) % 128
    return jnp.where(lane < 64, values[:half], values[half:])


def ones_diagonal():
    return pair_diag(128, 128).astype(F32).astype(BF)


def only(mask, values):
    return jnp.where(mask, values, jnp.zeros_like(values))


def each(function, *lists):
    return [function(*values) for values in zip(*lists)]


class Front:
    def __init__(self, qs, ks, prev_ks, blends, carries, masks, ones_diag):
        banded, causal, causal_q, count, carried, member, keep = masks
        self.q_stack = each(lambda q: stack_heads(q * 0.125), qs)
        self.window = each(lambda prev, k: jnp.concatenate([prev, k], axis=0), prev_ks, ks)
        scores = each(nt, self.window, self.q_stack)
        self.k_one = each(lambda k: first_feature(k.astype(F32)), ks)
        products = each(lambda k_one: nn(causal_q, k_one), self.k_one)
        self.q_one = each(lambda q: first_feature(q.astype(F32)), qs)
        self.sums = each(lambda product, carry: product + jnp.where(carried, carry, 0.0), products, carries)
        self.total = each(
            lambda q_one, sums: nn((q_one.astype(F32) * sums).astype(BF), ones_diag), self.q_one, self.sums
        )
        self.q_two = each(lambda q: second_feature(q.astype(F32)), qs)
        self.k_both = each(
            lambda k_one, k: jnp.concatenate([k_one, second_feature(k.astype(F32))], axis=1), self.k_one, ks
        )
        scores = each(lambda score: jnp.where(banded, score, -1e30), scores)
        raised = each(lambda score: jnp.exp(score - jnp.max(score, axis=0, keepdims=True)), scores)
        self.near = each(lambda r: r * (1.0 / jnp.sum(r, axis=0, keepdims=True)), raised)
        inverse = 1.0 / count
        self.ratio_one = each(lambda blend, total: blend[0] / total, blends, self.total)
        self.ratio_two = each(lambda blend: blend[1] * inverse, blends)
        self.q_scaled = each(
            lambda q_one, q_two, one, two: jnp.concatenate(
                [(q_one.astype(F32) * one).astype(BF), (q_two.astype(F32) * two).astype(BF)], axis=1
            ),
            self.q_one,
            self.q_two,
            self.ratio_one,
            self.ratio_two,
        )
        self.s_stack = each(stack_heads, self.q_scaled)
        far = each(nt, self.k_both, self.s_stack)
        self.weights = each(
            lambda near, far: jnp.concatenate(
                [near[:HALO].astype(BF), (near[HALO:] + jnp.where(causal, far, 0.0)).astype(BF)], axis=0
            ),
            self.near,
            far,
        )


PAIRS = range(4)


def pair_lanes(pair):
    return slice(128 * pair, 128 * pair + 128)


def value_lanes(pair):
    return slice(512 + 128 * pair, 640 + 128 * pair)


def heads_of(own_ref, other_ref, kind):
    first = own_ref.shape[1] // 3 * kind
    return [
        (own_ref if pair < 2 else other_ref)[:, first + 128 * (pair % 2) : first + 128 * (pair % 2) + 128]
        for pair in PAIRS
    ]


def pair_blends(own_ref, other_ref):
    first_head = iota((1, 128), 1) < 64
    rows = []
    for pair in PAIRS:
        ref = own_ref if pair < 2 else other_ref
        head = 2 * (pair % 2)
        rows.append([jnp.where(first_head, ref[kind, head], ref[kind, head + 1]) for kind in range(2)])
    return rows


def mixer_forward_block(
    index,
    total_rows,
    lengths_ref,
    own_ref,
    other_ref,
    packet_ref,
    blend_own_ref,
    blend_other_ref,
    state_out_ref,
    prev_out_ref,
    near_ref,
    weights_ref,
    features_ref,
    sums_ref,
    total_ref,
    state_ref,
    sum_ref,
    prev_ref,
):
    first = index * BLOCK

    @pl.when(index == 0)
    def _():
        for pair in PAIRS:
            state_ref[pair], sum_ref[pair] = unpack(packet_ref, pair, pair_diag(256, 128))
            prev_ref[:, pair_lanes(pair)] = unpack_halo(packet_ref, 0, pair)
            prev_ref[:, value_lanes(pair)] = unpack_halo(packet_ref, 1, pair)

    masks = block_masks(document_ends(lengths_ref, total_rows), first)
    banded, causal, causal_q, count, carried, member, keep = masks
    diag = pair_diag(256, 128)
    qs, ks, vs = [heads_of(own_ref, other_ref, kind) for kind in range(3)]
    prev = prev_ref[...]
    states = [state_ref[pair] for pair in PAIRS]
    sums_in = [sum_ref[pair] for pair in PAIRS]
    blends = pair_blends(blend_own_ref, blend_other_ref)
    front = Front(
        qs,
        ks,
        [prev[:, pair_lanes(pair)] for pair in PAIRS],
        blends,
        [total[0:1] for total in sums_in],
        masks,
        ones_diagonal(),
    )
    state_low = each(lambda state: state.astype(BF), states)
    inter = each(lambda q, state: nn(only(carried, q), state), front.q_scaled, state_low)
    added = each(lambda k, v: tn(only(member, k), v), front.k_both, vs)
    outs = [
        tn(front.weights[pair], jnp.concatenate([prev[:, value_lanes(pair)], vs[pair]], axis=0))
        for pair in PAIRS
    ]
    outs = each(lambda out, term: pick_heads(out) + term, outs, inter)
    for pair in PAIRS:
        state_out_ref[0, pair] = state_low[pair]
        near_ref[0, pair] = front.near[pair].astype(BF)
        weights_ref[0, pair] = front.weights[pair][HALO:]
        features_ref[0, pair, 0] = front.q_scaled[pair]
        features_ref[0, pair, 1] = front.k_both[pair]
        sums_ref[:, pair_lanes(pair)] = front.sums[pair]
        total_ref[:, pair_lanes(pair)] = 1.0 / front.total[pair]
        state_ref[pair] = jnp.where(keep, states[pair], 0.0) + jnp.where(diag, added[pair], 0.0)
        sum_ref[pair] = jnp.broadcast_to(front.sums[pair][BLOCK - 1 : BLOCK], (8, 128))
        prev_ref[:, pair_lanes(pair)] = ks[pair][BLOCK - HALO :]
        prev_ref[:, value_lanes(pair)] = vs[pair][BLOCK - HALO :]
    prev_out_ref[0] = prev
    return jnp.concatenate(outs, axis=1).astype(BF)


def mixer_backward_kernel(
    total_rows,
    lengths_ref,
    own_ref,
    other_ref,
    state_ref,
    prev_ref,
    near_ref,
    weights_ref,
    features_ref,
    sums_ref,
    total_ref,
    blend_own_ref,
    blend_other_ref,
    grad_ref,
    gq_ref,
    gk_ref,
    gv_ref,
    packet_ref,
    blend_out_ref,
    halo_ref,
    back_state_ref,
    back_sum_ref,
):
    step = pl.program_id(0)
    first = (pl.num_programs(0) - 1 - step) * BLOCK

    @pl.when(step == 0)
    def _():
        for ref in (halo_ref, back_state_ref, back_sum_ref, blend_out_ref):
            ref[...] = jnp.zeros_like(ref)

    ends = document_ends(lengths_ref, total_rows)
    blends = pair_blends(blend_own_ref, blend_other_ref)
    row_places = first + iota((1, 256), 1) % BLOCK
    key_places = first + iota((BLOCK, 256), 0)
    causal = (key_places <= row_places) & (key_places >= starts_of(ends, row_places))
    causal_k = causal[:, :BLOCK].astype(F32).astype(BF)
    col_places = first + iota((BLOCK, 1), 0)
    start_col = starts_of(ends, col_places)
    inverse = 1.0 / (col_places - start_col + 1).astype(F32)
    carried = start_col < first
    member_from = start_at(ends, first + BLOCK - 1)
    member = col_places >= member_from
    keep = member_from < first
    diag = pair_diag(256, 128)
    ones_diag = ones_diagonal()
    qs, ks, vs = [heads_of(own_ref, other_ref, kind) for kind in range(3)]
    prev = prev_ref[0]
    grads = [grad_ref[:, pair_lanes(pair)] for pair in PAIRS]
    states = [state_ref[0, pair] for pair in PAIRS]
    backs = [back_state_ref[pair] for pair in PAIRS]
    back_sums = [back_sum_ref[pair][0:1] for pair in PAIRS]
    nears = [near_ref[0, pair] for pair in PAIRS]
    q_scaled = [features_ref[0, pair, 0] for pair in PAIRS]
    k_both = [features_ref[0, pair, 1] for pair in PAIRS]
    g_stack = each(stack_heads, grads)
    v_window = [jnp.concatenate([prev[:, value_lanes(pair)], vs[pair]], axis=0) for pair in PAIRS]
    grad_weights = each(nt, v_window, g_stack)
    dv = [
        nn(jnp.concatenate([nears[pair][:HALO], weights_ref[0, pair]], axis=0), g_stack[pair]) for pair in PAIRS
    ]
    up_inter = each(lambda grad, state: nt(only(carried, grad), state), grads, states)
    far = each(lambda gw: jnp.where(causal, gw[HALO:], 0.0).astype(BF), grad_weights)
    up = each(tn, far, k_both)
    s_stack = each(stack_heads, q_scaled)
    dfeat = each(nn, far, s_stack)
    near_wide = each(lambda near: near.astype(F32), nears)
    inner = each(lambda near, gw: near * gw, near_wide, grad_weights)
    dscores = each(
        lambda near, inner: (inner - near * jnp.sum(inner, axis=0, keepdims=True)).astype(BF),
        near_wide,
        inner,
    )
    up = each(lambda up, inter: pick_heads(up) + inter, up, up_inter)
    q_first = each(lambda q: jnp.where(q > 0, q + 1.0, jnp.exp(jnp.minimum(q, 0.0))), [q.astype(F32) for q in qs])
    inverse_total = [total_ref[:, pair_lanes(pair)] for pair in PAIRS]
    mean_one = each(
        lambda q, up, total: nn((q.astype(BF).astype(F32) * up[:, :128]).astype(BF), ones_diag) * total,
        q_first,
        up,
        inverse_total,
    )
    window = [jnp.concatenate([prev[:, pair_lanes(pair)], ks[pair]], axis=0) for pair in PAIRS]
    q_stack = each(lambda q: stack_heads(q * 0.125), qs)
    gq_near = each(tn, dscores, window)
    dk = each(nn, dscores, q_stack)
    back_low = each(lambda back: back.astype(BF), backs)
    dv_far = each(lambda k, back: nn(only(member, k), back), k_both, back_low)
    dfeat_far = each(lambda v, back: nt(only(member, v), back), vs, back_low)
    added = each(lambda q, grad: tn(only(carried, q), grad), q_scaled, grads)
    weighted = each(lambda mean, q: (mean * q[:, :128].astype(F32)).astype(BF), mean_one, q_scaled)
    mean_back = each(lambda weight: nn(causal_k, weight), weighted)
    for pair in PAIRS:
        lanes, values = pair_lanes(pair), value_lanes(pair)
        up_one, up_two = up[pair][:, :128], up[pair][:, 128:]
        tanh_q = jnp.tanh(qs[pair].astype(F32))
        slope_q = jnp.minimum(q_first[pair], 1.0)
        up_two = up_two * inverse
        grad_one = blends[pair][0] * inverse_total[pair] * (up_one - mean_one[pair] * sums_ref[:, lanes])
        grad_two = blends[pair][1] * up_two
        gq = pick_heads(gq_near[pair]) * 0.125 + grad_one * slope_q + grad_two * (1.0 - tanh_q * tanh_q)
        gq_ref[:, lanes] = gq.astype(BF)
        blend_out_ref[0, pair] += jnp.broadcast_to(
            jnp.sum(mean_one[pair], axis=0, keepdims=True) / 64.0, (8, 128)
        )
        blend_out_ref[1, pair] += jnp.broadcast_to(jnp.sum(tanh_q * up_two, axis=0, keepdims=True), (8, 128))
        dv_own = dv[pair][HALO:] + dv_far[pair]
        dfeat_all = dfeat[pair] + dfeat_far[pair]
        d_one = dfeat_all[:, :128] - mean_back[pair] - jnp.where(member, back_sums[pair], 0.0)
        d_two = dfeat_all[:, 128:]
        wide_k = ks[pair].astype(F32)
        tanh_k = jnp.tanh(wide_k)
        slope_k = jnp.exp(jnp.minimum(wide_k, 0.0))
        gk = dk[pair][HALO:] + d_one * slope_k + d_two * (1.0 - tanh_k * tanh_k)
        gk_ref[: BLOCK - HALO, lanes] = gk[: BLOCK - HALO].astype(BF)
        gk_ref[BLOCK - HALO :, lanes] = (gk[BLOCK - HALO :] + halo_ref[:, lanes]).astype(BF)
        gv_ref[: BLOCK - HALO, lanes] = dv_own[: BLOCK - HALO].astype(BF)
        gv_ref[BLOCK - HALO :, lanes] = (dv_own[BLOCK - HALO :] + halo_ref[:, values]).astype(BF)
        halo_ref[:, lanes] = dk[pair][:HALO]
        halo_ref[:, values] = dv[pair][:HALO]
        back_state_ref[pair] = jnp.where(keep, backs[pair], 0.0) + jnp.where(diag, added[pair], 0.0)
        added_sum = jnp.sum(only(carried, weighted[pair].astype(F32)), axis=0, keepdims=True)
        back_sum_ref[pair] = jnp.broadcast_to(
            jnp.where(keep, back_sums[pair], 0.0) + added_sum, (8, 128)
        )

    @pl.when(first == 0)
    def _():
        for pair in PAIRS:
            slot = (pair + 2) % 4
            pack(packet_ref, slot, back_state_ref[pair], back_sum_ref[pair][0:1])
            pack_halo(packet_ref, 0, slot, halo_ref[:, pair_lanes(pair)].astype(BF))
            pack_halo(packet_ref, 1, slot, halo_ref[:, value_lanes(pair)].astype(BF))


LANES = 256


def layer_kernel(
    blocks,
    parts,
    lengths_ref,
    own_ref,
    other_ref,
    packet_ref,
    blend_own_ref,
    blend_other_ref,
    x_ref,
    cot_ref,
    gain_ref,
    wa_own_ref,
    wa_other_ref,
    wi_own_ref,
    wi_other_ref,
    wo_own_ref,
    wo_other_ref,
    mixed_out_ref,
    state_out_ref,
    prev_out_ref,
    near_ref,
    weights_ref,
    features_ref,
    sums_ref,
    total_ref,
    active_ref,
    branch_ref,
    gmix_ref,
    ggain_ref,
    attn_own_ref,
    attn_sent_ref,
    out_own_ref,
    in_own_ref,
    out_sent_ref,
    in_sent_ref,
    state_ref,
    sum_ref,
    prev_ref,
    mixed_ref,
    y_ref,
    r_ref,
    normed_ref,
    normed_turned_ref,
    grad_ref,
    grad_turned_ref,
    back_ref,
    wi_ref,
    wo_ref,
    stack_ref,
    load_sems,
    store_sems,
):
    step = pl.program_id(0)
    width = x_ref.shape[1]
    heads = wa_own_ref.shape[0]
    units = wo_ref.shape[1]
    chunk_units = units // parts
    loads = [
        pltpu.make_async_copy(source, target, load_sems.at[place])
        for place, (source, target) in enumerate(
            (
                (wi_own_ref, wi_ref.at[0]),
                (wo_own_ref, wo_ref.at[0]),
                (wi_other_ref, wi_ref.at[1]),
                (wo_other_ref, wo_ref.at[1]),
            )
        )
    ]

    @pl.when(step == 0)
    def _():
        for load in loads:
            load.start()
        back_ref[...] = jnp.zeros_like(back_ref)

    @pl.when(step < blocks)
    def _():
        mixed = mixer_forward_block(
            step,
            blocks * BLOCK,
            lengths_ref,
            own_ref,
            other_ref,
            packet_ref,
            blend_own_ref,
            blend_other_ref,
            state_out_ref,
            prev_out_ref,
            near_ref,
            weights_ref,
            features_ref,
            sums_ref,
            total_ref,
            state_ref,
            sum_ref,
            prev_ref,
        )
        here = pl.ds(pl.multiple_of(step * BLOCK, BLOCK), BLOCK)
        mixed_out_ref[...] = mixed
        mixed_ref[here, :] = mixed
        hidden = x_ref[...].astype(F32)
        hidden = hidden + nn(mixed[:, :heads], wa_own_ref[...]) + nn(mixed[:, heads:], wa_other_ref[...])
        r = lax.rsqrt(jnp.mean(hidden * hidden, axis=1, keepdims=True) + EPS)
        y = hidden * r
        y_ref[here, :] = y
        r_ref[here, :] = jnp.broadcast_to(r, (BLOCK, r_ref.shape[1]))
        normed = (y * gain_ref[...]).astype(BF)
        normed_ref[here, :] = normed
        normed_turned_ref[:, here] = normed.T
        grad_ref[here, :] = cot_ref[...]
        grad_turned_ref[:, here] = cot_ref[...].T

    @pl.when(step == blocks)
    def _():
        for load in loads:
            load.wait()

    @pl.when(step >= blocks)
    def _():
        half = (step - blocks) // parts
        place = (step - blocks) % parts
        normed = normed_ref[...]
        grad = grad_ref[...]
        first = pl.multiple_of(place * chunk_units, chunk_units)
        wi = wi_ref[half, :, pl.ds(first, chunk_units)]
        wo = wo_ref[half, pl.ds(first, chunk_units), :]
        spans = [slice(LANES * piece, LANES * piece + LANES) for piece in range(chunk_units // LANES)]
        us = [nn(normed, wi[:, span]) for span in spans]
        gacts = [nt(grad, wo[span, :]) for span in spans]
        gpres = []
        for piece, span in enumerate(spans):
            u = us[piece]
            square = u * u
            t = jnp.tanh(u * (GELU_A + (GELU_A * GELU_B) * square))
            gate = 0.5 + 0.5 * t
            active = (u * gate).astype(BF)
            active_ref[:, span] = active
            slope = gate + (u * (0.5 - 0.5 * t * t)) * (GELU_A + (3.0 * GELU_A * GELU_B) * square)
            gpre = (gacts[piece] * slope).astype(BF)
            gpres.append(gpre)
            gout = nn(grad_turned_ref[...], active).astype(BF).T
            spot = len(spans) * place + piece
            for side in range(width // LANES):
                row = pl.multiple_of(units * side + LANES * spot, LANES)
                stack_ref[half, 0, pl.ds(row, LANES), :] = gout[:, LANES * side : LANES * side + LANES]
            row = pl.multiple_of(width * spot, LANES)
            stack_ref[half, 1, pl.ds(row, width), :] = nn(normed_turned_ref[...], gpre).astype(BF)
        back_ref[...] += nt(jnp.concatenate(gpres, axis=1), wi)

    stores = []
    for late in range(2 * parts):
        half, place = late // parts, late % parts
        out_target, in_target = ((out_own_ref, in_own_ref), (out_sent_ref, in_sent_ref))[half]
        spots = [(0, out_target, units * side + chunk_units * place, chunk_units) for side in range(width // LANES)]
        rows = width * chunk_units // LANES
        spots.append((1, in_target, rows * place, rows))
        stores.append(
            [
                pltpu.make_async_copy(
                    stack_ref.at[half, kind, pl.ds(row, count), :],
                    target.at[pl.ds(row, count), :],
                    store_sems.at[late, number],
                )
                for number, (kind, target, row, count) in enumerate(spots)
            ]
        )

    for late in range(2 * parts):

        @pl.when(step == blocks + late)
        def _(late=late):
            for store in stores[late]:
                store.start()

    @pl.when(step == blocks + 2 * parts - 1)
    def _():
        back, y = back_ref[...], y_ref[...]
        scaled = back * gain_ref[...]
        mean = jnp.mean(scaled * y, axis=1, keepdims=True)
        ghid = grad_ref[...].astype(F32) + r_ref[:, :1] * (scaled - y * mean)
        branch = ghid.astype(BF)
        branch_ref[...] = branch
        gmix_ref[:, :heads] = nt(branch, wa_own_ref[...]).astype(BF)
        gmix_ref[:, heads:] = nt(branch, wa_other_ref[...]).astype(BF)
        ggain_ref[...] = jnp.broadcast_to(jnp.sum(back * y, axis=0, keepdims=True), ggain_ref.shape)
        gattn = tn(mixed_ref[...], branch).astype(BF)
        for half, ref in enumerate((attn_own_ref, attn_sent_ref)):
            for side in range(width // LANES):
                lanes = slice(LANES * side, LANES * side + LANES)
                ref[heads * side : heads * side + heads] = gattn[heads * half : heads * half + heads, lanes]
        for some in stores:
            for store in some:
                store.wait()


def output_kernel(x_ref, mixed_ref, active_ref, wa_own_ref, wa_other_ref, wo_own_ref, wo_other_ref, out_ref):
    heads = wa_own_ref.shape[0]
    units = wo_own_ref.shape[0]
    total = x_ref[...].astype(F32)
    total = total + (nn(mixed_ref[:, :heads], wa_own_ref[...]) + nn(mixed_ref[:, heads:], wa_other_ref[...]))
    total = total + (nn(active_ref[:, :units], wo_own_ref[...]) + nn(active_ref[:, units:], wo_other_ref[...]))
    out_ref[...] = total.astype(BF)


def finish_kernel(
    lengths_ref,
    own_ref,
    other_ref,
    normed_ref,
    packet_ref,
    gblend_ref,
    ggain_ref,
    gain_ref,
    w_own_ref,
    w_other_ref,
    attn_own_ref,
    attn_sent_ref,
    *refs,
):
    gq_ref, gk_ref, gv_ref, gproj_ref, wgrad_own_ref, wgrad_sent_ref = refs

    rows = own_ref.shape[0]
    live = lax.axis_index("tensor") == 0
    member_from = start_at(document_ends(lengths_ref, rows), rows - 1)
    member = (iota((rows, 1), 0) >= member_from) & live
    diag = pair_diag(256, 128)
    for pair in range(4):
        src = own_ref if pair < 2 else other_ref
        col = 128 * (pair % 2)
        lanes = slice(128 * pair, 128 * pair + 128)
        base = 768 * (pair // 2) + col
        k = src[:, 256 + col : 384 + col].astype(F32)
        v = src[:, 512 + col : 640 + col]
        back, back_sum = unpack(packet_ref, pair, diag)
        back, back_sum = back.astype(BF), back_sum[0:1]
        t = jnp.tanh(k)
        slope = jnp.exp(jnp.minimum(k, 0.0))
        k_both = jnp.concatenate([first_feature(k), t.astype(BF)], axis=1)
        dfeat = nt(v, back)
        extra_k = (dfeat[:, :128] - back_sum) * slope + dfeat[:, 128:] * (1.0 - t * t)
        extra_v = nn(k_both, back)
        gk = gk_ref[:, lanes].astype(F32) + jnp.where(member, extra_k, 0.0)
        gv = gv_ref[:, lanes].astype(F32) + jnp.where(member, extra_v, 0.0)
        halo_k = jnp.where(live, unpack_halo(packet_ref, 0, pair).astype(F32), 0.0)
        halo_v = jnp.where(live, unpack_halo(packet_ref, 1, pair).astype(F32), 0.0)
        cut = rows - HALO
        gproj_ref[:, base : base + 128] = gq_ref[:, lanes]
        gproj_ref[:cut, base + 256 : base + 384] = gk[:cut].astype(BF)
        gproj_ref[cut:, base + 256 : base + 384] = (gk[cut:] + halo_k).astype(BF)
        gproj_ref[:cut, base + 512 : base + 640] = gv[:cut].astype(BF)
        gproj_ref[cut:, base + 512 : base + 640] = (gv[cut:] + halo_v).astype(BF)
    width = normed_ref.shape[1]
    cols = w_own_ref.shape[2]
    normed = normed_ref[...]
    ones = jnp.ones((1, cols), F32)
    gain_grad = jnp.zeros((1, width), F32)
    for half, (wgrad_ref, w_ref) in enumerate(((wgrad_own_ref, w_own_ref), (wgrad_sent_ref, w_other_ref))):
        for kind in range(3):
            first = 3 * cols * half + cols * kind
            wgrad = tn(normed, gproj_ref[:, first : first + cols])
            wgrad_ref[width * kind : width * kind + width] = wgrad.astype(BF)
            products = wgrad * w_ref[kind].astype(F32)
            high = products.astype(BF)
            low = (products - high.astype(F32)).astype(BF)
            gain_grad = gain_grad + nt(ones.astype(BF), high) + nt(ones.astype(BF), low)
    gain_grad = gain_grad / gain_ref[...]
    for half, wgrad_ref in enumerate((wgrad_own_ref, wgrad_sent_ref)):
        blends = [
            jnp.concatenate([gblend_ref[kind, 2 * half + pair][0:1] for pair in range(2)], axis=1)
            for kind in range(2)
        ]
        gains = [gain_grad[:, :256], gain_grad[:, 256:], ggain_ref[0:1, :256], ggain_ref[0:1, 256:]]
        extra = jnp.concatenate(blends + gains + [jnp.zeros((10, 256), F32)], axis=0)
        attn_ref = (attn_own_ref, attn_sent_ref)[half]
        wgrad_ref[3 * width : 3 * width + attn_ref.shape[0]] = attn_ref[...]
        base = 3 * width + attn_ref.shape[0]
        wgrad_ref[base : base + 16] = extra.astype(BF)
        wgrad_ref[base + 16 :] = jnp.zeros((EXTRA - 16, 256), BF)


def input_grad_kernel(gproj_ref, x_ref, branch_ref, gain_ref, w_own_ref, w_other_ref, out_ref):
    cols = w_own_ref.shape[2]
    gnormed = None
    for half, w_ref in enumerate((w_own_ref, w_other_ref)):
        for kind in range(3):
            first = 3 * cols * half + cols * kind
            term = nt(gproj_ref[:, first : first + cols], w_ref[kind])
            gnormed = term if gnormed is None else gnormed + term
    x = x_ref[...].astype(F32)
    r = lax.rsqrt(jnp.mean(x * x, axis=1, keepdims=True) + EPS)
    y = x * r
    scaled = gnormed * gain_ref[...]
    grad = branch_ref[...].astype(F32) + r * (scaled - y * jnp.mean(scaled * y, axis=1, keepdims=True))
    out_ref[...] = grad.astype(BF)


def merged(low, mine, got):
    return jnp.where(low, mine, got), jnp.where(low, got, mine)


def put_rows(ref, first_row, lane, parts, first, count):
    rows = parts[0].shape[0]
    lanes = parts[0].shape[1]
    for place, part in enumerate(parts):
        low, high = max(first, rows * place), min(first + count, rows * place + rows)
        if low < high:
            values = part[low - rows * place : high - rows * place].astype(F32)
            ref[first_row + low - first : first_row + high - first, lane : lane + lanes] = values


def feed_output_kernel(bits_ref, out_mine_ref, out_got_ref, in_mine_ref, in_got_ref, wo_ref, wi_ref):
    units, width = wo_ref.shape
    outs = merged(bits_ref[0] == 0, out_mine_ref[...], out_got_ref[...])
    for side in range(width // LANES):
        put_rows(wo_ref, 0, LANES * side, outs, units * side, units)
    ins = merged(bits_ref[1] == 0, in_mine_ref[...], in_got_ref[...])
    for place in range(units // LANES):
        put_rows(wi_ref, 0, LANES * place, ins, width * place, width)


def attention_output_kernel(
    bits_ref, a_mine_ref, a_got_ref, b_mine_ref, b_got_ref, wq_ref, wa_ref, gain_one_ref, gain_two_ref, blend_ref
):
    heads, width = wa_ref.shape
    parts = merged(bits_ref[0] == 0, a_mine_ref[...], a_got_ref[...])
    parts += merged(bits_ref[1] == 0, b_mine_ref[...], b_got_ref[...])
    rows = a_mine_ref.shape[0]
    put_rows(wq_ref, 0, 0, parts, 0, 3 * width)
    for side in range(width // LANES):
        put_rows(wa_ref, 0, LANES * side, parts, 3 * width + heads * side, heads)
    rest = parts[3][rows - EXTRA : rows - EXTRA + 16].astype(F32)
    gain_one_ref[...] = jnp.concatenate([rest[2:3], rest[3:4]], axis=1)
    gain_two_ref[...] = jnp.concatenate([rest[4:5], rest[5:6]], axis=1)
    sums = [jnp.sum(rest[:2, 64 * head : 64 * head + 64], axis=1, keepdims=True) for head in range(4)]
    blend_ref[...] = jnp.concatenate(sums, axis=1)


def flip(values, count, stride):
    return lax.ppermute(values, "dp", [(src, src ^ stride) for src in range(count)])


def strides_of(count):
    strides = []
    stride = 1
    while stride < count:
        strides.append(stride)
        stride *= 2
    return strides


class Reduction:
    def __init__(self, stacks, count, whole_late=False):
        self.stacks = [[(term, 0) for term in terms] for terms in stacks]
        self.rows = [terms[0].shape[0] for terms in stacks]
        self.count = count
        strides = strides_of(count)
        self.orders = [strides, strides[1::-1] + strides[2:]]
        self.steps = len(strides)
        self.taken = 0
        self.halved = min(2, self.steps) if whole_late else self.steps
        self.place = lax.axis_index("dp")
        self.held = None

    def bit(self, stride):
        return (self.place // stride) % 2

    def after(self, *tokens):
        if self.held is not None:
            *self.gots, first, second = tie(*self.gots, *self.held)
            self.held = [first, second]
            return tokens
        news = [terms[-1][0] for terms in self.stacks]
        if news[0] is news[1]:
            news = news[:1]
        tied = tie(*news, *tokens)
        for stack in range(2):
            offset = self.stacks[stack][-1][1]
            self.stacks[stack][-1] = (tied[min(stack, len(news) - 1)], offset)
        return tied[len(news) :]

    def cut(self, stack, rows, skip):
        total = None
        for term, offset in self.stacks[stack]:
            part = lax.dynamic_slice_in_dim(term, offset + skip, rows, 0).astype(F32)
            total = part if total is None else total + part
        return total.astype(BF)

    def outgoing(self):
        cuts = []
        for stack in range(2):
            if self.taken < self.halved:
                self.rows[stack] //= 2
                bit = self.bit(self.orders[stack][self.taken])
                cuts.append(self.cut(stack, self.rows[stack], (1 - bit) * self.rows[stack]))
            else:
                cuts.append(self.cut(stack, self.rows[stack], 0))
        return cuts if self.taken < 2 else [jnp.concatenate(cuts, axis=0)]

    def send(self, cuts):
        gots = [flip(cut, self.count, self.orders[stack][self.taken]) for stack, cut in enumerate(cuts)]
        for stack in range(2):
            skip = self.rows[0] if stack == 1 and len(cuts) == 1 else 0
            got = gots[min(stack, len(cuts) - 1)]
            if self.taken < self.halved:
                bit = self.bit(self.orders[stack][self.taken])
                kept = [(term, offset + bit * self.rows[stack]) for term, offset in self.stacks[stack]]
            else:
                kept = [(cuts[0], skip)]
            self.stacks[stack] = kept + [(got, skip)]
        self.taken += 1

    def start_gather(self):
        self.held = [self.cut(stack, self.rows[stack], 0) for stack in range(2)]

    def gather_outgoing(self):
        return list(self.held) if self.halved <= 2 else [jnp.concatenate(self.held, axis=0)]

    def gather_send(self, cuts):
        step = self.halved - 1
        gots = [flip(cut, self.count, self.orders[stack][step]) for stack, cut in enumerate(cuts)]
        if len(gots) == 1:
            first = self.held[0].shape[0]
            gots = [gots[0][:first], gots[0][first:]]
        self.gots = gots
        self.halved = step

    def finished(self):
        return self.taken == self.steps and (self.steps == 0 or (self.held is not None and self.halved == 0))

    def next_cuts(self):
        if self.taken < self.steps:
            return self.outgoing()
        if self.held is None:
            self.start_gather()
        return self.gather_outgoing()

    def next_send(self, cuts):
        if self.held is None:
            self.send(cuts)
        else:
            self.gather_send(cuts)

    def next_take(self):
        if self.held is not None and self.halved > 0:
            self.gather_take()

    def last_bits(self):
        return jnp.stack([self.bit(order[0]) if order else 0 * self.place for order in self.orders])

    def parts(self):
        if self.steps > 0:
            return [self.held[0], self.gots[0], self.held[1], self.gots[1]]
        halves = []
        for held in [self.cut(stack, self.rows[stack], 0) for stack in range(2)]:
            middle = held.shape[0] // 2
            halves += [held[:middle], held[middle:]]
        return halves

    def gather_take(self):
        for stack in range(2):
            low = self.bit(self.orders[stack][self.halved]) == 0
            mine, got = self.held[stack], self.gots[stack]
            self.held[stack] = jnp.concatenate([jnp.where(low, mine, got), jnp.where(low, got, mine)], axis=0)


def swap(values):
    return lax.ppermute(values, "tensor", [(0, 1), (1, 0)])


def body(count, tokens, lengths, w_qkv, w_attn, w_in, w_out, gain_attn, gain_mlp, blend, cotangent):
    rows, width = tokens.shape
    blocks = rows // BLOCK

    wq_own = w_qkv.transpose(1, 0, 2)
    wq_other = swap(wq_own)
    wa_other, wi_other, wo_other = swap(w_attn), swap(w_in), swap(w_out)
    blend_other = swap(blend)
    gain_one = gain_attn.reshape(1, width)
    gain_two = gain_mlp.reshape(1, width)
    smem = pl.BlockSpec(memory_space=pltpu.SMEM)

    def row_block(size, cols):
        return pl.BlockSpec((size, cols), lambda i: (i, 0))

    own_cols = 3 * wq_own.shape[2]
    normed, own = pl.pallas_call(
        norm_project_kernel,
        grid=(4,),
        in_specs=[row_block(rows // 4, width), whole((1, width)), whole(wq_own.shape)],
        out_specs=[row_block(rows // 4, width), row_block(rows // 4, own_cols)],
        out_shape=[jax.ShapeDtypeStruct((rows, width), BF), jax.ShapeDtypeStruct((rows, own_cols), BF)],
        compiler_params=params(60),
        cost_estimate=cost(5),
        name="norm_project",
    )(tokens, gain_one, wq_own)
    other, packet = pl.pallas_call(
        project_state_kernel,
        in_specs=[smem] + [pl.BlockSpec(memory_space=pltpu.VMEM)] * 3,
        out_shape=[
            jax.ShapeDtypeStruct((rows, own_cols), BF),
            jax.ShapeDtypeStruct((PACKET, 128), BF),
        ],
        compiler_params=params(60),
        cost_estimate=cost(5),
        name="project_state",
    )(lengths, normed, wq_other, own)
    packet = swap(packet)

    units = w_out.shape[0]
    tall = rows // 4
    parts = units // (2 * LANES)
    vmem = pl.BlockSpec(memory_space=pltpu.VMEM)
    stack_rows = units * width // LANES
    attn_rows = w_attn.shape[0] * width // LANES
    anywhere = pl.BlockSpec(memory_space=pl.ANY)

    def early(*shape):
        return pl.BlockSpec(shape, lambda i: (jnp.minimum(i, blocks - 1),) + (0,) * (len(shape) - 1))

    kept_blocks = [
        ((blocks, 4, 256, 128), BF),
        ((blocks, HALO, 1024), BF),
        ((blocks, 4, BLOCK + HALO, 256), BF),
        ((blocks, 4, BLOCK, 256), BF),
        ((blocks, 4, 2, BLOCK, 256), BF),
    ]
    mixed, *outs = pl.pallas_call(
        partial(layer_kernel, blocks, parts),
        grid=(blocks + 2 * parts,),
        in_specs=[
            smem,
            early(BLOCK, own_cols),
            early(BLOCK, own_cols),
            whole((PACKET, 128)),
            smem,
            smem,
            early(BLOCK, width),
            early(BLOCK, width),
            whole((1, width)),
            whole(w_attn.shape),
            whole(w_attn.shape),
        ]
        + [anywhere] * 4,
        out_specs=[early(BLOCK, width)]
        + [early(1, *shape[1:]) for shape, _ in kept_blocks]
        + [early(BLOCK, width)] * 2
        + [
            pl.BlockSpec((rows, units // parts), lambda i: (0, jnp.maximum(i - blocks, 0))),
            whole((rows, width)),
            whole((rows, width)),
            whole((8, width)),
            whole((attn_rows, LANES)),
            whole((attn_rows, LANES)),
        ]
        + [anywhere] * 4,
        out_shape=[jax.ShapeDtypeStruct((rows, width), BF)]
        + [jax.ShapeDtypeStruct(shape, kind) for shape, kind in kept_blocks]
        + [jax.ShapeDtypeStruct((rows, width), F32)] * 2
        + [
            jax.ShapeDtypeStruct((rows, 2 * units), BF),
            jax.ShapeDtypeStruct((rows, width), BF),
            jax.ShapeDtypeStruct((rows, width), BF),
            jax.ShapeDtypeStruct((8, width), F32),
            jax.ShapeDtypeStruct((attn_rows, LANES), BF),
            jax.ShapeDtypeStruct((attn_rows, LANES), BF),
        ]
        + [jax.ShapeDtypeStruct((stack_rows, LANES), BF)] * 4,
        scratch_shapes=[
            pltpu.VMEM((4, 256, 128), F32),
            pltpu.VMEM((4, 8, 128), F32),
            pltpu.VMEM((HALO, 1024), BF),
            pltpu.VMEM((rows, width), BF),
            pltpu.VMEM((rows, width), F32),
            pltpu.VMEM((rows, 128), F32),
            pltpu.VMEM((rows, width), BF),
            pltpu.VMEM((width, rows), BF),
            pltpu.VMEM((rows, width), BF),
            pltpu.VMEM((width, rows), BF),
            pltpu.VMEM((rows, width), F32),
            pltpu.VMEM((2,) + w_in.shape, BF),
            pltpu.VMEM((2,) + w_out.shape, BF),
            pltpu.VMEM((2, 2, stack_rows, LANES), BF),
            pltpu.SemaphoreType.DMA((4,)),
            pltpu.SemaphoreType.DMA((2 * parts, 1 + width // LANES)),
        ],
        compiler_params=params(60),
        cost_estimate=cost(30),
        name="layer",
    )(
        lengths,
        own,
        other,
        packet,
        blend,
        blend_other,
        tokens,
        cotangent,
        gain_two,
        w_attn,
        wa_other,
        w_in,
        wi_other,
        w_out,
        wo_other,
    )
    kept, outs = outs[:7], outs[7:]
    active, branch, gmix, ggain_mlp, *attn_grads = outs[:6]
    out_own, in_own, out_sent, in_sent = outs[6:]

    feed_sum = Reduction([[out_own, swap(out_sent)], [in_own, swap(in_sent)]], count)
    wanted = feed_sum.steps
    if wanted > 0:
        cuts = feed_sum.outgoing()
        gmix, *cuts = tie(gmix, *cuts)
        feed_sum.send(cuts)

    def back_block(*shape):
        return pl.BlockSpec(shape, lambda i: (blocks - 1 - i,) + (0,) * (len(shape) - 1))

    gq, gk, gv, packet_back, gblend = pl.pallas_call(
        partial(mixer_backward_kernel, rows),
        grid=(blocks,),
        in_specs=[
            smem,
            back_block(BLOCK, own_cols),
            back_block(BLOCK, own_cols),
            back_block(1, 4, 256, 128),
            back_block(1, HALO, 1024),
            back_block(1, 4, BLOCK + HALO, 256),
            back_block(1, 4, BLOCK, 256),
            back_block(1, 4, 2, BLOCK, 256),
            back_block(BLOCK, width),
            back_block(BLOCK, width),
            smem,
            smem,
            back_block(BLOCK, width),
        ],
        out_specs=[back_block(BLOCK, width)] * 3 + [whole((PACKET, 128)), whole((2, 4, 8, 128))],
        out_shape=[jax.ShapeDtypeStruct((rows, width), BF)] * 3
        + [jax.ShapeDtypeStruct((PACKET, 128), BF), jax.ShapeDtypeStruct((2, 4, 8, 128), F32)],
        scratch_shapes=[
            pltpu.VMEM((HALO, 1024), F32),
            pltpu.VMEM((4, 256, 128), F32),
            pltpu.VMEM((4, 8, 128), F32),
        ],
        compiler_params=params(60),
        cost_estimate=cost(20),
        name="mixer_backward",
    )(lengths, own, other, *kept, blend, blend_other, gmix)
    if wanted > 1:
        (packet_back,) = feed_sum.after(packet_back)
    packet_got = swap(packet_back)
    if wanted > 1:
        cuts = feed_sum.outgoing()
        packet_got, *cuts = tie(packet_got, *cuts)
        feed_sum.send(cuts)

    gproj, wq_mine, wq_sent = pl.pallas_call(
        finish_kernel,
        in_specs=[smem] + [pl.BlockSpec(memory_space=pltpu.VMEM)] * 14,
        out_shape=[
            jax.ShapeDtypeStruct((rows, 2 * own_cols), BF),
            jax.ShapeDtypeStruct((3 * width + attn_rows + EXTRA, own_cols // 3), BF),
            jax.ShapeDtypeStruct((3 * width + attn_rows + EXTRA, own_cols // 3), BF),
        ],
        compiler_params=params(60),
        cost_estimate=cost(8),
        name="finish",
    )(
        lengths,
        own,
        other,
        normed,
        packet_got,
        gblend,
        ggain_mlp,
        gain_one,
        wq_own,
        wq_other,
        *attn_grads,
        gq,
        gk,
        gv,
    )
    def layer_output(active):
        return pl.pallas_call(
            output_kernel,
            grid=(4,),
            in_specs=[row_block(tall, width), row_block(tall, width), row_block(tall, 2 * units)]
            + [whole(w_attn.shape)] * 2
            + [whole(w_out.shape)] * 2,
            out_specs=row_block(tall, width),
            out_shape=jax.ShapeDtypeStruct((rows, width), BF),
            compiler_params=params(60),
            cost_estimate=cost(5),
            name="layer_output",
        )(tokens, mixed, active, w_attn, wa_other, w_out, wo_other)

    def input_gradient(gproj):
        return pl.pallas_call(
            input_grad_kernel,
            grid=(4,),
            in_specs=[
                row_block(tall, 2 * own_cols),
                row_block(tall, width),
                row_block(tall, width),
                whole((1, width)),
                whole(wq_own.shape),
                whole(wq_own.shape),
            ],
            out_specs=row_block(tall, width),
            out_shape=jax.ShapeDtypeStruct((rows, width), BF),
            compiler_params=params(60),
            cost_estimate=cost(7),
            name="input_grad",
        )(gproj, tokens, branch, gain_one, wq_own, wq_other)

    if wanted > 1:
        (wq_sent,) = feed_sum.after(wq_sent)
    wq_got = swap(wq_sent)
    cut = wq_got.shape[0] // 2
    wq_sum = Reduction([[wq_mine[:cut], wq_got[:cut]], [wq_mine[cut:], wq_got[cut:]]], count, True)
    beside = {0: lambda: input_gradient(gproj), 3: lambda: layer_output(active)}
    done = {}
    step = 0
    while not (feed_sum.finished() and wq_sum.finished()):
        running = [reduction for reduction in (wq_sum, feed_sum) if not reduction.finished()]
        cuts = [reduction.next_cuts() for reduction in running]
        flat = list(tie(*[cut for some in cuts for cut in some], gproj, active))
        active, gproj = flat.pop(), flat.pop()
        for reduction, some in zip(running, cuts):
            reduction.next_send([flat.pop(0) for _ in some])
        if step in beside:
            done[step] = beside[step]()
            for reduction in running:
                (done[step],) = reduction.after(done[step])
        for reduction in running:
            reduction.next_take()
        step += 1
    for step in beside:
        if step not in done:
            done[step] = beside[step]()
    grad_input, output = done[0], done[3]

    wo_grad, wi_grad = pl.pallas_call(
        feed_output_kernel,
        in_specs=[smem] + [vmem] * 4,
        out_shape=[jax.ShapeDtypeStruct(w_out.shape, F32), jax.ShapeDtypeStruct(w_in.shape, F32)],
        compiler_params=params(60),
        cost_estimate=cost(3),
        name="feed_output",
    )(feed_sum.last_bits(), *feed_sum.parts())
    wq_grad, wa_grad, ggain_one, ggain_two, gblend_all = pl.pallas_call(
        attention_output_kernel,
        in_specs=[smem] + [vmem] * 4,
        out_shape=[
            jax.ShapeDtypeStruct((3 * width, own_cols // 3), F32),
            jax.ShapeDtypeStruct(w_attn.shape, F32),
            jax.ShapeDtypeStruct((1, width), F32),
            jax.ShapeDtypeStruct((1, width), F32),
            jax.ShapeDtypeStruct(blend.shape, F32),
        ],
        compiler_params=params(60),
        cost_estimate=cost(3),
        name="attention_output",
    )(wq_sum.last_bits(), *wq_sum.parts())

    return (
        output,
        grad_input,
        wq_grad.reshape(wq_own.shape).transpose(1, 0, 2),
        wa_grad,
        wi_grad,
        wo_grad,
        ggain_one.reshape(width),
        ggain_two.reshape(width),
        gblend_all,
    )


def solution(mesh):
    return jax.shard_map(
        partial(body, mesh.shape["dp"]),
        mesh=mesh,
        in_specs=(
            P(("dp", "tensor"), None),
            P("dp", None),
            P(None, None, "tensor"),
            P("tensor", None),
            P(None, "tensor"),
            P("tensor", None),
            P(),
            P(),
            P(None, "tensor"),
            P(("dp", "tensor"), None),
        ),
        out_specs=(
            P(("dp", "tensor"), None),
            P(("dp", "tensor"), None),
            P(None, None, "tensor"),
            P("tensor", None),
            P(None, "tensor"),
            P("tensor", None),
            P(),
            P(),
            P(None, "tensor"),
        ),
        check_vma=False,
    )
```

```python
from functools import partial

import jax
import jax.numpy as jnp
from jax import lax
from jax.experimental import pallas as pl
from jax.experimental.pallas import tpu as pltpu
from jax.sharding import PartitionSpec as P

BAND = 30
HALO = 32
EXTRA = 64
BLOCK = 128
EPS = 1e-06
BF = jnp.bfloat16
F32 = jnp.float32
GELU_A = 0.7978845608028654
GELU_B = 0.044715


def nn(left, right):
    return lax.dot_general(left, right, (((1,), (0,)), ((), ())), preferred_element_type=F32)


def nt(left, right):
    return lax.dot_general(left, right, (((1,), (1,)), ((), ())), preferred_element_type=F32)


def tn(left, right):
    return lax.dot_general(left, right, (((0,), (0,)), ((), ())), preferred_element_type=F32)


def iota(shape, dim):
    return lax.broadcasted_iota(jnp.int32, shape, dim)


def whole(shape):
    return pl.BlockSpec(shape, lambda *_: (0,) * len(shape))


def params(mebibytes):
    return pltpu.CompilerParams(vmem_limit_bytes=mebibytes << 20)


def cost(micros):
    return pl.CostEstimate(flops=int(micros * 1e7), bytes_accessed=1 << 20, transcendentals=0)


def tie(*values):
    return lax.optimization_barrier(values)


class Copies:
    def __init__(self, sems):
        self.sems = sems
        self.used = 0

    def make(self, source, target):
        self.used += 1
        return pltpu.make_async_copy(source, target, self.sems.at[self.used - 1])


def document_ends(lengths_ref, rows):
    end = -lax.axis_index("tensor") * rows
    ends = [end]
    for doc in range(lengths_ref.shape[1]):
        end = end + lengths_ref[0, doc]
        ends.append(end)
    return ends[1:] + ends[:1]


def starts_of(ends, places):
    start = jnp.full(places.shape, ends[-1], jnp.int32)
    for end in ends[:-1]:
        start = jnp.where(places >= end, jnp.maximum(start, end), start)
    return start


def start_at(ends, place):
    start = ends[-1]
    for end in ends[:-1]:
        start = jnp.where(place >= end, jnp.maximum(start, end), start)
    return start


def norm_project_kernel(x_ref, gain_ref, w_ref, normed_ref, out_ref):
    x = x_ref[...].astype(F32)
    r = lax.rsqrt(jnp.mean(x * x, axis=1, keepdims=True) + EPS)
    normed = (x * r * gain_ref[...]).astype(BF)
    normed_ref[...] = normed
    project(normed, w_ref, out_ref)


def project(normed, w_ref, out_ref):
    cols = w_ref.shape[2]
    for kind in range(3):
        out_ref[:, cols * kind : cols * kind + cols] = nn(normed, w_ref[kind]).astype(BF)


PACKET = 4 * (128 + 16) + 8 * HALO


def packed_state(state):
    return jnp.concatenate([state[:64] + state[64:128], state[128:192] + state[192:]], axis=0).astype(BF)


def unpacked_state(packed, diag):
    one, two = packed[:64], packed[64:]
    state = jnp.concatenate([one, one, two, two], axis=0)
    return jnp.where(diag, state, jnp.zeros_like(state))


def pack(packet_ref, pair, state, total):
    base = 144 * pair
    packet_ref[base : base + 128] = packed_state(state)
    packet_ref[base + 128 : base + 144] = jnp.broadcast_to(total, (16, 128)).astype(BF)


def pack_halo(packet_ref, kind, pair, rows):
    base = 576 + HALO * (4 * kind + pair)
    packet_ref[base : base + HALO] = rows


def unpack(packet_ref, pair, diag):
    base = 144 * pair
    state = unpacked_state(packet_ref[base : base + 128].astype(F32), diag)
    return state, packet_ref[base + 128 : base + 136].astype(F32)


def unpack_halo(packet_ref, kind, pair):
    base = 576 + HALO * (4 * kind + pair)
    return packet_ref[base : base + HALO]


def first_feature(values):
    return jnp.where(values > 0, values + 1.0, jnp.exp(jnp.minimum(values, 0.0))).astype(BF)


def second_feature(values):
    return jnp.tanh(values).astype(BF)


def pair_diag(rows, cols):
    row = iota((rows, cols), 0)
    col = iota((rows, cols), 1)
    return ((row // 64) % 2) == ((col // 64) % 2)


def project_state_kernel(lengths_ref, normed_ref, w_ref, own_ref, out_ref, packet_ref):
    rows = normed_ref.shape[0]
    project(normed_ref[...], w_ref, out_ref)
    member_from = start_at(document_ends(lengths_ref, rows), rows - 1)
    member = iota((rows, 1), 0) >= member_from
    ks, vs = [heads_of(own_ref, out_ref, kind) for kind in (1, 2)]
    wide = [jnp.where(member, k.astype(F32), 0.0) for k in ks]
    ones = [jnp.where(member, first_feature(k).astype(F32), 0.0) for k in wide]
    features = each(lambda k, one: jnp.concatenate([one.astype(BF), second_feature(k)], axis=1), wide, ones)
    states = each(tn, features, vs)
    diag = pair_diag(256, 128)
    for pair in PAIRS:
        slot = (pair + 2) % 4
        pack(packet_ref, slot, jnp.where(diag, states[pair], 0.0), jnp.sum(ones[pair], axis=0, keepdims=True))
        pack_halo(packet_ref, 0, slot, ks[pair][rows - HALO :])
        pack_halo(packet_ref, 1, slot, vs[pair][rows - HALO :])


def block_masks(ends, first):
    row_places = first + iota((1, 256), 1) % BLOCK
    start_row = starts_of(ends, row_places)
    window_places = first - HALO + iota((BLOCK + HALO, 256), 0)
    banded = (window_places <= row_places) & (
        window_places >= jnp.maximum(start_row, row_places - (BAND - 1))
    )
    key_places = first + iota((BLOCK, 256), 0)
    causal = (key_places <= row_places) & (key_places >= start_row)
    col_places = first + iota((BLOCK, 1), 0)
    start_col = starts_of(ends, col_places)
    key_lane = first + iota((BLOCK, BLOCK), 1)
    causal_q = ((key_lane <= col_places) & (key_lane >= start_col)).astype(F32).astype(BF)
    count = (col_places - start_col + 1).astype(F32)
    carried = start_col < first
    member_from = start_at(ends, first + BLOCK - 1)
    member = col_places >= member_from
    keep = member_from < first
    return banded, causal, causal_q, count, carried, member, keep


def stack_heads(values):
    lane = iota(values.shape, 1) % 128
    zero = jnp.zeros_like(values)
    return jnp.concatenate(
        [jnp.where(lane < 64, values, zero), jnp.where(lane >= 64, values, zero)], axis=0
    )


def pick_heads(values):
    half = values.shape[0] // 2
    lane = iota((half, values.shape[1]), 1) % 128
    return jnp.where(lane < 64, values[:half], values[half:])


def ones_diagonal():
    return pair_diag(128, 128).astype(F32).astype(BF)


def only(mask, values):
    return jnp.where(mask, values, jnp.zeros_like(values))


def each(function, *lists):
    return [function(*values) for values in zip(*lists)]


class Front:
    def __init__(self, qs, ks, prev_ks, blends, carries, masks, ones_diag):
        banded, causal, causal_q, count, carried, member, keep = masks
        self.q_stack = each(lambda q: stack_heads(q * 0.125), qs)
        self.window = each(lambda prev, k: jnp.concatenate([prev, k], axis=0), prev_ks, ks)
        scores = each(nt, self.window, self.q_stack)
        self.k_one = each(lambda k: first_feature(k.astype(F32)), ks)
        products = each(lambda k_one: nn(causal_q, k_one), self.k_one)
        self.q_one = each(lambda q: first_feature(q.astype(F32)), qs)
        self.sums = each(lambda product, carry: product + jnp.where(carried, carry, 0.0), products, carries)
        self.total = each(
            lambda q_one, sums: nn((q_one.astype(F32) * sums).astype(BF), ones_diag), self.q_one, self.sums
        )
        self.q_two = each(lambda q: second_feature(q.astype(F32)), qs)
        self.k_both = each(
            lambda k_one, k: jnp.concatenate([k_one, second_feature(k.astype(F32))], axis=1), self.k_one, ks
        )
        scores = each(lambda score: jnp.where(banded, score, -1e30), scores)
        raised = each(lambda score: jnp.exp(score - jnp.max(score, axis=0, keepdims=True)), scores)
        self.near = each(lambda r: r * (1.0 / jnp.sum(r, axis=0, keepdims=True)), raised)
        inverse = 1.0 / count
        self.ratio_one = each(lambda blend, total: blend[0] / total, blends, self.total)
        self.ratio_two = each(lambda blend: blend[1] * inverse, blends)
        self.q_scaled = each(
            lambda q_one, q_two, one, two: jnp.concatenate(
                [(q_one.astype(F32) * one).astype(BF), (q_two.astype(F32) * two).astype(BF)], axis=1
            ),
            self.q_one,
            self.q_two,
            self.ratio_one,
            self.ratio_two,
        )
        self.s_stack = each(stack_heads, self.q_scaled)
        far = each(nt, self.k_both, self.s_stack)
        self.weights = each(
            lambda near, far: jnp.concatenate(
                [near[:HALO].astype(BF), (near[HALO:] + jnp.where(causal, far, 0.0)).astype(BF)], axis=0
            ),
            self.near,
            far,
        )


PAIRS = range(4)


def pair_lanes(pair):
    return slice(128 * pair, 128 * pair + 128)


def value_lanes(pair):
    return slice(512 + 128 * pair, 640 + 128 * pair)


def heads_of(own_ref, other_ref, kind):
    first = own_ref.shape[1] // 3 * kind
    return [
        (own_ref if pair < 2 else other_ref)[:, first + 128 * (pair % 2) : first + 128 * (pair % 2) + 128]
        for pair in PAIRS
    ]


def pair_blends(own_ref, other_ref):
    first_head = iota((1, 128), 1) < 64
    rows = []
    for pair in PAIRS:
        ref = own_ref if pair < 2 else other_ref
        head = 2 * (pair % 2)
        rows.append([jnp.where(first_head, ref[kind, head], ref[kind, head + 1]) for kind in range(2)])
    return rows


def mixer_forward_block(
    index,
    total_rows,
    lengths_ref,
    own_ref,
    other_ref,
    blend_own_ref,
    blend_other_ref,
    state_out_ref,
    prev_out_ref,
    near_ref,
    weights_ref,
    sums_ref,
    total_ref,
    state_ref,
    sum_ref,
    prev_ref,
):
    first = index * BLOCK

    masks = block_masks(document_ends(lengths_ref, total_rows), first)
    banded, causal, causal_q, count, carried, member, keep = masks
    diag = pair_diag(256, 128)
    qs, ks, vs = [heads_of(own_ref, other_ref, kind) for kind in range(3)]
    prev = prev_ref[...]
    states = [state_ref[pair] for pair in PAIRS]
    sums_in = [sum_ref[pair] for pair in PAIRS]
    blends = pair_blends(blend_own_ref, blend_other_ref)
    front = Front(
        qs,
        ks,
        [prev[:, pair_lanes(pair)] for pair in PAIRS],
        blends,
        [total[0:1] for total in sums_in],
        masks,
        ones_diagonal(),
    )
    state_low = each(lambda state: state.astype(BF), states)
    inter = each(lambda q, state: nn(only(carried, q), state), front.q_scaled, state_low)
    added = each(lambda k, v: tn(only(member, k), v), front.k_both, vs)
    outs = [
        tn(front.weights[pair], jnp.concatenate([prev[:, value_lanes(pair)], vs[pair]], axis=0))
        for pair in PAIRS
    ]
    outs = each(lambda out, term: pick_heads(out) + term, outs, inter)
    for pair in PAIRS:
        state_out_ref[0, pair] = packed_state(states[pair])
        near_ref[0, pair] = front.near[pair].astype(BF)
        weights_ref[0, pair] = front.weights[pair][HALO:]
        sums_ref[:, pair_lanes(pair)] = front.sums[pair].astype(BF)
        total_ref[:, pair_lanes(pair)] = (1.0 / front.total[pair]).astype(BF)
        state_ref[pair] = jnp.where(keep, states[pair], 0.0) + jnp.where(diag, added[pair], 0.0)
        sum_ref[pair] = jnp.broadcast_to(front.sums[pair][BLOCK - 1 : BLOCK], (8, 128))
        prev_ref[:, pair_lanes(pair)] = ks[pair][BLOCK - HALO :]
        prev_ref[:, value_lanes(pair)] = vs[pair][BLOCK - HALO :]
    prev_out_ref[0] = prev
    return jnp.concatenate(outs, axis=1).astype(BF)


def mixer_backward_block(
    index,
    total_rows,
    lengths_ref,
    blend_own_ref,
    blend_other_ref,
    own_ref,
    other_ref,
    state_ref,
    prev_ref,
    near_ref,
    weights_ref,
    sums_ref,
    total_ref,
    grad_ref,
    gq_ref,
    gk_ref,
    gv_ref,
    blend_out_ref,
    halo_ref,
    back_state_ref,
    back_sum_ref,
):
    first = index * BLOCK
    ends = document_ends(lengths_ref, total_rows)
    blends = pair_blends(blend_own_ref, blend_other_ref)
    row_places = first + iota((1, 256), 1) % BLOCK
    key_places = first + iota((BLOCK, 256), 0)
    causal = (key_places <= row_places) & (key_places >= starts_of(ends, row_places))
    causal_k = causal[:, :BLOCK].astype(F32).astype(BF)
    col_places = first + iota((BLOCK, 1), 0)
    start_col = starts_of(ends, col_places)
    inverse = 1.0 / (col_places - start_col + 1).astype(F32)
    carried = start_col < first
    member_from = start_at(ends, first + BLOCK - 1)
    member = col_places >= member_from
    keep = member_from < first
    diag = pair_diag(256, 128)
    ones_diag = ones_diagonal()
    qs, ks, vs = [heads_of(own_ref, other_ref, kind) for kind in range(3)]
    prev = prev_ref[0]
    grads = [grad_ref[:, pair_lanes(pair)] for pair in PAIRS]
    states = [unpacked_state(state_ref[0, pair], diag) for pair in PAIRS]
    backs = [back_state_ref[pair] for pair in PAIRS]
    back_sums = [back_sum_ref[pair][0:1] for pair in PAIRS]
    nears = [near_ref[0, pair] for pair in PAIRS]
    wide_ks = [k.astype(F32) for k in ks]
    wide_qs = [q.astype(F32) for q in qs]
    raised_k = [jnp.exp(jnp.minimum(k, 0.0)) for k in wide_ks]
    raised_q = [jnp.exp(jnp.minimum(q, 0.0)) for q in wide_qs]
    tanh_ks = [jnp.tanh(k) for k in wide_ks]
    tanh_qs = [jnp.tanh(q) for q in wide_qs]
    k_both = each(
        lambda k, raised, t: jnp.concatenate(
            [jnp.where(k > 0, k + 1.0, raised).astype(BF), t.astype(BF)], axis=1
        ),
        wide_ks,
        raised_k,
        tanh_ks,
    )
    q_one = each(lambda q, raised: jnp.where(q > 0, q + 1.0, raised).astype(BF).astype(F32), wide_qs, raised_q)
    inverse_total = [total_ref[:, pair_lanes(pair)].astype(F32) for pair in PAIRS]
    ratio_one = each(lambda blend, total: blend[0] * total, blends, inverse_total)
    ratio_two = [blend[1] * inverse for blend in blends]
    q_scaled = each(
        lambda one, ratio, t, other: jnp.concatenate(
            [(one * ratio).astype(BF), (t.astype(BF).astype(F32) * other).astype(BF)], axis=1
        ),
        q_one,
        ratio_one,
        tanh_qs,
        ratio_two,
    )
    g_stack = each(stack_heads, grads)
    v_window = [jnp.concatenate([prev[:, value_lanes(pair)], vs[pair]], axis=0) for pair in PAIRS]
    grad_weights = each(nt, v_window, g_stack)
    dv = [
        nn(jnp.concatenate([nears[pair][:HALO], weights_ref[0, pair]], axis=0), g_stack[pair]) for pair in PAIRS
    ]
    up_inter = each(lambda grad, state: nt(only(carried, grad), state), grads, states)
    far = each(lambda gw: jnp.where(causal, gw[HALO:], 0.0).astype(BF), grad_weights)
    up = each(tn, far, k_both)
    s_stack = each(stack_heads, q_scaled)
    dfeat = each(nn, far, s_stack)
    near_wide = each(lambda near: near.astype(F32), nears)
    inner = each(lambda near, gw: near * gw, near_wide, grad_weights)
    dscores = each(
        lambda near, inner: (inner - near * jnp.sum(inner, axis=0, keepdims=True)).astype(BF),
        near_wide,
        inner,
    )
    up = each(lambda up, inter: pick_heads(up) + inter, up, up_inter)
    mean_one = each(
        lambda q, up, total: nn((q * up[:, :128]).astype(BF), ones_diag) * total,
        q_one,
        up,
        inverse_total,
    )
    window = [jnp.concatenate([prev[:, pair_lanes(pair)], ks[pair]], axis=0) for pair in PAIRS]
    q_stack = each(lambda q: stack_heads(q * 0.125), qs)
    gq_near = each(tn, dscores, window)
    dk = each(nn, dscores, q_stack)
    back_low = each(lambda back: back.astype(BF), backs)
    dv_far = each(lambda k, back: nn(only(member, k), back), k_both, back_low)
    dfeat_far = each(lambda v, back: nt(only(member, v), back), vs, back_low)
    added = each(lambda q, grad: tn(only(carried, q), grad), q_scaled, grads)
    weighted = each(lambda mean, q: (mean * q[:, :128].astype(F32)).astype(BF), mean_one, q_scaled)
    mean_back = each(lambda weight: nn(causal_k, weight), weighted)
    for pair in PAIRS:
        lanes, values = pair_lanes(pair), value_lanes(pair)
        up_one, up_two = up[pair][:, :128], up[pair][:, 128:]
        tanh_q, slope_q = tanh_qs[pair], raised_q[pair]
        up_two = up_two * inverse
        grad_one = ratio_one[pair] * (up_one - mean_one[pair] * sums_ref[:, lanes].astype(F32))
        grad_two = blends[pair][1] * up_two
        gq = pick_heads(gq_near[pair]) * 0.125 + grad_one * slope_q + grad_two * (1.0 - tanh_q * tanh_q)
        gq_ref[:, lanes] = gq.astype(BF)
        blend_out_ref[0, pair] += jnp.broadcast_to(
            jnp.sum(mean_one[pair], axis=0, keepdims=True) / 64.0, (8, 128)
        )
        blend_out_ref[1, pair] += jnp.broadcast_to(jnp.sum(tanh_q * up_two, axis=0, keepdims=True), (8, 128))
        dv_own = dv[pair][HALO:] + dv_far[pair]
        dfeat_all = dfeat[pair] + dfeat_far[pair]
        d_one = dfeat_all[:, :128] - mean_back[pair] - jnp.where(member, back_sums[pair], 0.0)
        d_two = dfeat_all[:, 128:]
        tanh_k, slope_k = tanh_ks[pair], raised_k[pair]
        gk = dk[pair][HALO:] + d_one * slope_k + d_two * (1.0 - tanh_k * tanh_k)
        gk_ref[: BLOCK - HALO, lanes] = gk[: BLOCK - HALO].astype(BF)
        gk_ref[BLOCK - HALO :, lanes] = (gk[BLOCK - HALO :] + halo_ref[:, lanes]).astype(BF)
        gv_ref[: BLOCK - HALO, lanes] = dv_own[: BLOCK - HALO].astype(BF)
        gv_ref[BLOCK - HALO :, lanes] = (dv_own[BLOCK - HALO :] + halo_ref[:, values]).astype(BF)
        halo_ref[:, lanes] = dk[pair][:HALO]
        halo_ref[:, values] = dv[pair][:HALO]
        back_state_ref[pair] = jnp.where(keep, backs[pair], 0.0) + jnp.where(diag, added[pair], 0.0)
        added_sum = jnp.sum(only(carried, weighted[pair].astype(F32)), axis=0, keepdims=True)
        back_sum_ref[pair] = jnp.broadcast_to(
            jnp.where(keep, back_sums[pair], 0.0) + added_sum, (8, 128)
        )


STEP_BLOCKS = 2


def mixer_backward_kernel(lengths_ref, blend_own_ref, blend_other_ref, *refs):
    inputs, outputs = refs[:9], refs[9:12]
    packet_ref, blend_out_ref, halo_ref, back_state_ref, back_sum_ref = refs[12:]
    step = pl.program_id(0)
    steps = pl.num_programs(0)

    @pl.when(step == 0)
    def _():
        for ref in (halo_ref, back_state_ref, back_sum_ref, blend_out_ref):
            ref[...] = jnp.zeros_like(ref)

    for sub in reversed(range(STEP_BLOCKS)):
        views = []
        for ref in inputs + outputs:
            unit = ref.shape[0] // STEP_BLOCKS
            views.append(ref.at[sub * unit : sub * unit + unit])
        mixer_backward_block(
            (steps - 1 - step) * STEP_BLOCKS + sub,
            steps * STEP_BLOCKS * BLOCK,
            lengths_ref,
            blend_own_ref,
            blend_other_ref,
            *views,
            blend_out_ref,
            halo_ref,
            back_state_ref,
            back_sum_ref,
        )

    @pl.when(step == steps - 1)
    def _():
        for pair in PAIRS:
            slot = (pair + 2) % 4
            pack(packet_ref, slot, back_state_ref[pair], back_sum_ref[pair][0:1])
            pack_halo(packet_ref, 0, slot, halo_ref[:, pair_lanes(pair)].astype(BF))
            pack_halo(packet_ref, 1, slot, halo_ref[:, value_lanes(pair)].astype(BF))


LANES = 256


def layer_kernel(
    blocks,
    parts,
    lengths_ref,
    blend_own_ref,
    blend_other_ref,
    packet_ref,
    gain_ref,
    wa_own_ref,
    wa_other_ref,
    own_hbm,
    other_hbm,
    x_hbm,
    cot_hbm,
    wi_own_hbm,
    wi_other_hbm,
    wo_own_hbm,
    wo_other_hbm,
    branch_ref,
    gmix_ref,
    ggain_ref,
    attn_own_ref,
    attn_sent_ref,
    mixed_hbm,
    state_hbm,
    prev_hbm,
    near_hbm,
    weights_hbm,
    sums_hbm,
    total_hbm,
    active_hbm,
    out_own_hbm,
    in_own_hbm,
    out_sent_hbm,
    in_sent_hbm,
    own_ref,
    other_ref,
    x_ref,
    grad_ref,
    wi_ref,
    wo_ref,
    mixed_ref,
    state_out_ref,
    prev_out_ref,
    near_ref,
    weights_ref,
    sums_ref,
    total_ref,
    active_ref,
    stack_ref,
    state_ref,
    sum_ref,
    prev_ref,
    y_ref,
    r_ref,
    normed_ref,
    normed_turned_ref,
    grad_turned_ref,
    back_ref,
    sems,
):
    copies = Copies(sems)
    rows, width = x_ref.shape
    heads = wa_own_ref.shape[0]
    units = wo_ref.shape[1]
    chunk_units = units // parts
    tokens = ((own_hbm, own_ref), (other_hbm, other_ref), (x_hbm, x_ref), (cot_hbm, grad_ref))
    first_loads = [copies.make(source.at[:BLOCK], target.at[:BLOCK]) for source, target in tokens]
    later_loads = [copies.make(source.at[BLOCK:], target.at[BLOCK:]) for source, target in tokens]
    weight_loads = [
        copies.make(source, target)
        for source, target in (
            (wi_own_hbm, wi_ref.at[0]),
            (wo_own_hbm, wo_ref.at[0]),
            (wi_other_hbm, wi_ref.at[1]),
            (wo_other_hbm, wo_ref.at[1]),
        )
    ]
    for load in first_loads + later_loads + weight_loads:
        load.start()
    for pair in PAIRS:
        state_ref[pair], sum_ref[pair] = unpack(packet_ref, pair, pair_diag(256, 128))
        prev_ref[:, pair_lanes(pair)] = unpack_halo(packet_ref, 0, pair)
        prev_ref[:, value_lanes(pair)] = unpack_halo(packet_ref, 1, pair)
    back_ref[...] = jnp.zeros_like(back_ref)
    for load in first_loads:
        load.wait()

    def block(step, _):
        @pl.when(step == 1)
        def _():
            for load in later_loads:
                load.wait()

        here = pl.ds(pl.multiple_of(step * BLOCK, BLOCK), BLOCK)
        only_here = pl.ds(step, 1)
        mixed = mixer_forward_block(
            step,
            rows,
            lengths_ref,
            own_ref.at[here],
            other_ref.at[here],
            blend_own_ref,
            blend_other_ref,
            state_out_ref.at[only_here],
            prev_out_ref.at[only_here],
            near_ref.at[only_here],
            weights_ref.at[only_here],
            sums_ref.at[here],
            total_ref.at[here],
            state_ref,
            sum_ref,
            prev_ref,
        )
        mixed_ref[here, :] = mixed
        hidden = x_ref[here, :].astype(F32)
        hidden = hidden + nn(mixed[:, :heads], wa_own_ref[...]) + nn(mixed[:, heads:], wa_other_ref[...])
        r = lax.rsqrt(jnp.mean(hidden * hidden, axis=1, keepdims=True) + EPS)
        y = hidden * r
        y_ref[here, :] = y
        r_ref[here, :] = jnp.broadcast_to(r, (BLOCK, r_ref.shape[1]))
        normed = (y * gain_ref[...]).astype(BF)
        normed_ref[here, :] = normed
        normed_turned_ref[:, here] = normed.T
        grad_turned_ref[:, here] = grad_ref[here, :].T
        return 0

    def some_blocks(step, _):
        for sub in range(STEP_BLOCKS):
            block(step * STEP_BLOCKS + sub, 0)
        return 0

    lax.fori_loop(0, blocks // STEP_BLOCKS, some_blocks, 0)
    stores = [
        copies.make(source, target)
        for source, target in (
            (mixed_ref, mixed_hbm),
            (state_out_ref, state_hbm),
            (prev_out_ref, prev_hbm),
            (near_ref, near_hbm),
            (weights_ref, weights_hbm),
            (sums_ref, sums_hbm),
            (total_ref, total_hbm),
        )
    ]
    for store in stores:
        store.start()
    for load in weight_loads:
        load.wait()
    chunk_stores = []
    for late in range(2 * parts):
        half, place = late // parts, late % parts
        out_target, in_target = ((out_own_hbm, in_own_hbm), (out_sent_hbm, in_sent_hbm))[half]
        spots = [(0, out_target, units * side + chunk_units * place, chunk_units) for side in range(width // LANES)]
        count = width * chunk_units // LANES
        spots.append((1, in_target, count * place, count))
        columns = pl.ds(late * chunk_units, chunk_units)
        chunk_stores.append(
            [
                copies.make(stack_ref.at[half, kind, pl.ds(row, count), :], target.at[pl.ds(row, count), :])
                for kind, target, row, count in spots
            ]
            + [copies.make(active_ref.at[:, columns], active_hbm.at[:, columns])]
        )

    def chunk(late, _):
        half, place = late // parts, late % parts
        normed = normed_ref[...]
        grad = grad_ref[...]
        first = pl.multiple_of(place * chunk_units, chunk_units)
        wi = wi_ref[half, :, pl.ds(first, chunk_units)]
        wo = wo_ref[half, pl.ds(first, chunk_units), :]
        spans = [slice(LANES * piece, LANES * piece + LANES) for piece in range(chunk_units // LANES)]
        us = [nn(normed, wi[:, span]) for span in spans]
        gacts = [nt(grad, wo[span, :]) for span in spans]
        gpres = []
        for piece in range(len(spans)):
            u = us[piece]
            square = u * u
            t = jnp.tanh(u * (GELU_A + (GELU_A * GELU_B) * square))
            gate = 0.5 + 0.5 * t
            active = (u * gate).astype(BF)
            column = pl.multiple_of(late * chunk_units + LANES * piece, LANES)
            active_ref[:, pl.ds(column, LANES)] = active
            slope = gate + (u * (0.5 - 0.5 * t * t)) * (GELU_A + (3.0 * GELU_A * GELU_B) * square)
            gpre = (gacts[piece] * slope).astype(BF)
            gpres.append(gpre)
            gout = nn(grad_turned_ref[...], active).astype(BF).T
            spot = len(spans) * place + piece
            for side in range(width // LANES):
                row = pl.multiple_of(units * side + LANES * spot, LANES)
                stack_ref[half, 0, pl.ds(row, LANES), :] = gout[:, LANES * side : LANES * side + LANES]
            row = pl.multiple_of(width * spot, LANES)
            stack_ref[half, 1, pl.ds(row, width), :] = nn(normed_turned_ref[...], gpre).astype(BF)
        back_ref[...] += nt(jnp.concatenate(gpres, axis=1), wi)
        for number, some in enumerate(chunk_stores):

            @pl.when(late == number)
            def _(some=some):
                for store in some:
                    store.start()

        return 0

    lax.fori_loop(0, 2 * parts, chunk, 0)
    back, y = back_ref[...], y_ref[...]
    scaled = back * gain_ref[...]
    mean = jnp.mean(scaled * y, axis=1, keepdims=True)
    ghid = grad_ref[...].astype(F32) + r_ref[:, :1] * (scaled - y * mean)
    branch = ghid.astype(BF)
    branch_ref[...] = branch
    gmix_ref[:, :heads] = nt(branch, wa_own_ref[...]).astype(BF)
    gmix_ref[:, heads:] = nt(branch, wa_other_ref[...]).astype(BF)
    ggain_ref[...] = jnp.broadcast_to(jnp.sum(back * y, axis=0, keepdims=True), ggain_ref.shape)
    gattn = tn(mixed_ref[...], branch).astype(BF)
    for half, ref in enumerate((attn_own_ref, attn_sent_ref)):
        for side in range(width // LANES):
            lanes = slice(LANES * side, LANES * side + LANES)
            ref[heads * side : heads * side + heads] = gattn[heads * half : heads * half + heads, lanes]
    for store in stores + [store for some in chunk_stores for store in some]:
        store.wait()


def output_kernel(x_ref, mixed_ref, active_ref, wa_own_ref, wa_other_ref, wo_own_ref, wo_other_ref, out_ref):
    heads = wa_own_ref.shape[0]
    units = wo_own_ref.shape[0]
    total = x_ref[...].astype(F32)
    total = total + (nn(mixed_ref[:, :heads], wa_own_ref[...]) + nn(mixed_ref[:, heads:], wa_other_ref[...]))
    total = total + (nn(active_ref[:, :units], wo_own_ref[...]) + nn(active_ref[:, units:], wo_other_ref[...]))
    out_ref[...] = total.astype(BF)


def finish_kernel(
    lengths_ref,
    gblend_ref,
    ggain_ref,
    gain_ref,
    packet_hbm,
    own_hbm,
    other_hbm,
    gk_hbm,
    gv_hbm,
    gq_hbm,
    normed_hbm,
    w_own_hbm,
    w_other_hbm,
    attn_own_hbm,
    attn_sent_hbm,
    gkv_hbm,
    wgrad_own_hbm,
    wgrad_sent_hbm,
    packet_ref,
    own_ref,
    other_ref,
    gk_ref,
    gv_ref,
    gq_ref,
    normed_ref,
    w_own_ref,
    w_other_ref,
    gkv_ref,
    wgrad_own_ref,
    wgrad_sent_ref,
    sems,
):
    copies = Copies(sems)
    rows, width = normed_ref.shape
    cols = w_own_ref.shape[2]
    wgrads = (wgrad_own_ref, wgrad_sent_ref)
    attn_rows = attn_own_hbm.shape[0]
    keys_values = slice(cols, 3 * cols)
    loads = [
        copies.make(source, target)
        for source, target in (
            (packet_hbm, packet_ref),
            (own_hbm.at[:, keys_values], own_ref),
            (gk_hbm, gk_ref),
            (gv_hbm, gv_ref),
            (other_hbm.at[:, keys_values], other_ref),
            (normed_hbm, normed_ref),
            (gq_hbm, gq_ref),
            (w_own_hbm, w_own_ref),
            (w_other_hbm, w_other_ref),
            (attn_own_hbm, wgrad_own_ref.at[3 * width : 3 * width + attn_rows]),
            (attn_sent_hbm, wgrad_sent_ref.at[3 * width : 3 * width + attn_rows]),
        )
    ]
    gkv_stores, wgrad_stores = [], []
    for half, target in enumerate((wgrad_own_hbm, wgrad_sent_hbm)):
        lanes = slice(2 * cols * half, 2 * cols * half + 2 * cols)
        gkv_stores.append(copies.make(gkv_ref.at[:, lanes], gkv_hbm.at[:, lanes]))
        spans = [slice(width * kind, width * kind + width) for kind in range(3)]
        spans.append(slice(3 * width, wgrads[half].shape[0]))
        wgrad_stores.append([copies.make(wgrads[half].at[span], target.at[span]) for span in spans])
    for load in loads:
        load.start()
    live = lax.axis_index("tensor") == 0
    member_from = start_at(document_ends(lengths_ref, rows), rows - 1)
    member = (iota((rows, 1), 0) >= member_from) & live
    diag = pair_diag(256, 128)
    cut = rows - HALO
    for load in loads[:4]:
        load.wait()
    for pair in PAIRS:
        if pair == 2:
            loads[4].wait()
        src = own_ref if pair < 2 else other_ref
        col = 128 * (pair % 2)
        lanes = pair_lanes(pair)
        k = src[:, col : col + 128].astype(F32)
        v = src[:, cols + col : cols + col + 128]
        back, back_sum = unpack(packet_ref, pair, diag)
        back, back_sum = back.astype(BF), back_sum[0:1]
        t = jnp.tanh(k)
        raised = jnp.exp(jnp.minimum(k, 0.0))
        k_both = jnp.concatenate([jnp.where(k > 0, k + 1.0, raised).astype(BF), t.astype(BF)], axis=1)
        dfeat = nt(v, back)
        extra_k = (dfeat[:, :128] - back_sum) * raised + dfeat[:, 128:] * (1.0 - t * t)
        extra_v = nn(k_both, back)
        for kind, (grad_ref, extra) in enumerate(((gk_ref, extra_k), (gv_ref, extra_v))):
            grad = grad_ref[:, lanes].astype(F32) + jnp.where(member, extra, 0.0)
            halo = jnp.where(live, unpack_halo(packet_ref, kind, pair).astype(F32), 0.0)
            base = cols * (2 * (pair // 2) + kind) + col
            gkv_ref[:cut, base : base + 128] = grad[:cut].astype(BF)
            gkv_ref[cut:, base : base + 128] = (grad[cut:] + halo).astype(BF)
        if pair % 2 == 1:
            gkv_stores[pair // 2].start()
    for load in loads[5:]:
        load.wait()
    normed = normed_ref[...].T
    ones = jnp.ones((1, cols), BF)
    gain_grad = jnp.zeros((1, width), F32)
    for half, (wgrad_ref, w_ref) in enumerate(zip(wgrads, (w_own_ref, w_other_ref))):
        for kind in range(3):
            if kind == 0:
                grad = gq_ref[:, cols * half : cols * half + cols]
            else:
                first = cols * (2 * half + kind - 1)
                grad = gkv_ref[:, first : first + cols]
            wgrad = nn(normed, grad)
            wgrad_ref[width * kind : width * kind + width] = wgrad.astype(BF)
            wgrad_stores[half][kind].start()
            products = wgrad * w_ref[kind].astype(F32)
            high = products.astype(BF)
            low = (products - high.astype(F32)).astype(BF)
            gain_grad = gain_grad + nt(ones, high) + nt(ones, low)
    gain_grad = gain_grad / gain_ref[...]
    for half, wgrad_ref in enumerate(wgrads):
        blends = [
            jnp.concatenate([gblend_ref[kind, 2 * half + pair][0:1] for pair in range(2)], axis=1)
            for kind in range(2)
        ]
        gains = [gain_grad[:, :256], gain_grad[:, 256:], ggain_ref[0:1, :256], ggain_ref[0:1, 256:]]
        extra = jnp.concatenate(blends + gains + [jnp.zeros((10, 256), F32)], axis=0)
        base = 3 * width + attn_rows
        wgrad_ref[base : base + 16] = extra.astype(BF)
        wgrad_ref[base + 16 :] = jnp.zeros((EXTRA - 16, 256), BF)
        wgrad_stores[half][3].start()
    for store in gkv_stores + wgrad_stores[0] + wgrad_stores[1]:
        store.wait()


def input_grad_kernel(gq_ref, gkv_ref, x_ref, branch_ref, gain_ref, w_own_ref, w_other_ref, out_ref):
    cols = w_own_ref.shape[2]
    gnormed = None
    for half, w_ref in enumerate((w_own_ref, w_other_ref)):
        for kind in range(3):
            if kind == 0:
                grad = gq_ref[:, cols * half : cols * half + cols]
            else:
                first = cols * (2 * half + kind - 1)
                grad = gkv_ref[:, first : first + cols]
            term = nt(grad, w_ref[kind])
            gnormed = term if gnormed is None else gnormed + term
    x = x_ref[...].astype(F32)
    r = lax.rsqrt(jnp.mean(x * x, axis=1, keepdims=True) + EPS)
    y = x * r
    scaled = gnormed * gain_ref[...]
    grad = branch_ref[...].astype(F32) + r * (scaled - y * jnp.mean(scaled * y, axis=1, keepdims=True))
    out_ref[...] = grad.astype(BF)


def merged(low, mine, got):
    return jnp.where(low, mine, got), jnp.where(low, got, mine)


def put_part_kernel(parts_ref, out_part_ref, in_part_ref, wo_ref, wi_ref):
    wo_ref[...] = out_part_ref[...].astype(F32)
    width = wi_ref.shape[0]
    for side in range(wi_ref.shape[1] // LANES):
        wi_ref[:, LANES * side : LANES * side + LANES] = in_part_ref[width * side : width * side + width].astype(F32)


def put_rows(ref, first_row, lane, parts, first, count):
    rows = parts[0].shape[0]
    lanes = parts[0].shape[1]
    for place, part in enumerate(parts):
        low, high = max(first, rows * place), min(first + count, rows * place + rows)
        if low < high:
            values = part[low - rows * place : high - rows * place].astype(F32)
            ref[first_row + low - first : first_row + high - first, lane : lane + lanes] = values


def last_output_kernel(
    bits_ref,
    out_part_hbm,
    in_part_hbm,
    a_mine_hbm,
    a_got_hbm,
    b_mine_hbm,
    b_got_hbm,
    wo_before_hbm,
    wi_before_hbm,
    wo_hbm,
    wi_hbm,
    wq_ref,
    wa_ref,
    gain_one_ref,
    gain_two_ref,
    blend_ref,
    out_part_ref,
    in_part_ref,
    a_mine_ref,
    a_got_ref,
    b_mine_ref,
    b_got_ref,
    wo_ref,
    wi_ref,
    sems,
):
    copies = Copies(sems)
    loads = [
        copies.make(source, target)
        for source, target in (
            (out_part_hbm, out_part_ref),
            (in_part_hbm, in_part_ref),
            (a_mine_hbm, a_mine_ref),
            (a_got_hbm, a_got_ref),
            (b_mine_hbm, b_mine_ref),
            (b_got_hbm, b_got_ref),
        )
    ]
    for load in loads:
        load.start()
    wo_column = pl.multiple_of((1 - bits_ref[0]) * wo_ref.shape[1], LANES)
    wi_column = pl.multiple_of((1 - bits_ref[1]) * wi_ref.shape[1], LANES)
    middle = wo_ref.shape[0] // 2
    stores = [
        copies.make(wo_ref.at[span], wo_hbm.at[span, pl.ds(wo_column, wo_ref.shape[1])])
        for span in (slice(0, middle), slice(middle, 2 * middle))
    ]
    for side in range(wi_ref.shape[1] // LANES):
        lanes = slice(LANES * side, LANES * side + LANES)
        target = wi_hbm.at[:, pl.ds(pl.multiple_of(wi_column + LANES * side, LANES), LANES)]
        stores.append(copies.make(wi_ref.at[:, lanes], target))
    for load in loads[:2]:
        load.wait()
    wo_ref[...] = out_part_ref[...].astype(F32)
    for store in stores[:2]:
        store.start()
    width = wi_ref.shape[0]
    for side in range(wi_ref.shape[1] // LANES):
        wi_ref[:, LANES * side : LANES * side + LANES] = in_part_ref[width * side : width * side + width].astype(F32)
        stores[2 + side].start()
    for load in loads[2:]:
        load.wait()
    heads = wa_ref.shape[0]
    parts = merged(bits_ref[0] == 0, a_mine_ref[...], a_got_ref[...])
    parts += merged(bits_ref[1] == 0, b_mine_ref[...], b_got_ref[...])
    rows = a_mine_ref.shape[0]
    put_rows(wq_ref, 0, 0, parts, 0, 3 * width)
    for side in range(width // LANES):
        put_rows(wa_ref, 0, LANES * side, parts, 3 * width + heads * side, heads)
    rest = parts[3][rows - EXTRA : rows - EXTRA + 16].astype(F32)
    gain_one_ref[...] = jnp.concatenate([rest[2:3], rest[3:4]], axis=1)
    gain_two_ref[...] = jnp.concatenate([rest[4:5], rest[5:6]], axis=1)
    sums = [jnp.sum(rest[:2, 64 * head : 64 * head + 64], axis=1, keepdims=True) for head in range(4)]
    blend_ref[...] = jnp.concatenate(sums, axis=1)
    for store in stores:
        store.wait()


def flip(values, count, stride):
    return lax.ppermute(values, "dp", [(src, src ^ stride) for src in range(count)])


def strides_of(count):
    strides = []
    stride = 1
    while stride < count:
        strides.append(stride)
        stride *= 2
    return strides


class Reduction:
    def __init__(self, stacks, count, whole_late=False):
        self.stacks = [[(term, first) for term in terms] for terms, first, _ in stacks]
        self.rows = [rows for _, _, rows in stacks]
        self.count = count
        strides = strides_of(count)
        self.orders = [strides, strides[1::-1] + strides[2:]]
        self.steps = len(strides)
        self.taken = 0
        self.halved = min(2, self.steps) if whole_late else self.steps
        self.place = lax.axis_index("dp")
        self.held = None

    def bit(self, stride):
        return (self.place // stride) % 2

    def after(self, *tokens):
        if self.held is not None:
            *self.gots, first, second = tie(*self.gots, *self.held)
            self.held = [first, second]
            return tokens
        news = [terms[-1][0] for terms in self.stacks]
        if news[0] is news[1]:
            news = news[:1]
        tied = tie(*news, *tokens)
        for stack in range(2):
            offset = self.stacks[stack][-1][1]
            self.stacks[stack][-1] = (tied[min(stack, len(news) - 1)], offset)
        return tied[len(news) :]

    def cut(self, stack, rows, skip):
        total = None
        for term, offset in self.stacks[stack]:
            part = lax.dynamic_slice_in_dim(term, offset + skip, rows, 0).astype(F32)
            total = part if total is None else total + part
        return total.astype(BF)

    def outgoing(self):
        cuts = []
        for stack in range(2):
            if self.taken < self.halved:
                self.rows[stack] //= 2
                bit = self.bit(self.orders[stack][self.taken])
                cuts.append(self.cut(stack, self.rows[stack], (1 - bit) * self.rows[stack]))
            else:
                cuts.append(self.cut(stack, self.rows[stack], 0))
        return cuts if self.taken < 2 else [jnp.concatenate(cuts, axis=0)]

    def send(self, cuts):
        gots = [flip(cut, self.count, self.orders[stack][self.taken]) for stack, cut in enumerate(cuts)]
        for stack in range(2):
            skip = self.rows[0] if stack == 1 and len(cuts) == 1 else 0
            got = gots[min(stack, len(cuts) - 1)]
            if self.taken < self.halved:
                bit = self.bit(self.orders[stack][self.taken])
                kept = [(term, offset + bit * self.rows[stack]) for term, offset in self.stacks[stack]]
            else:
                kept = [(cuts[0], skip)]
            self.stacks[stack] = kept + [(got, skip)]
        self.taken += 1

    def start_gather(self):
        self.held = [self.cut(stack, self.rows[stack], 0) for stack in range(2)]

    def gather_outgoing(self):
        return list(self.held) if self.halved <= 2 else [jnp.concatenate(self.held, axis=0)]

    def gather_send(self, cuts):
        step = self.halved - 1
        gots = [flip(cut, self.count, self.orders[stack][step]) for stack, cut in enumerate(cuts)]
        if len(gots) == 1:
            first = self.held[0].shape[0]
            gots = [gots[0][:first], gots[0][first:]]
        self.gots = gots
        self.halved = step

    def finished(self):
        return self.taken == self.steps and (self.steps == 0 or (self.held is not None and self.halved == 0))

    def next_cuts(self):
        if self.taken < self.steps:
            return self.outgoing()
        if self.held is None:
            self.start_gather()
        return self.gather_outgoing()

    def next_send(self, cuts):
        if self.held is None:
            self.send(cuts)
        else:
            self.gather_send(cuts)

    def next_take(self):
        if self.held is not None and self.halved > 0:
            self.gather_take()

    def last_bits(self):
        return jnp.stack([self.bit(order[0]) if order else 0 * self.place for order in self.orders])

    def parts(self):
        if self.steps > 0:
            return [self.held[0], self.gots[0], self.held[1], self.gots[1]]
        halves = []
        for held in [self.cut(stack, self.rows[stack], 0) for stack in range(2)]:
            middle = held.shape[0] // 2
            halves += [held[:middle], held[middle:]]
        return halves

    def gather_take(self):
        for stack in range(2):
            low = self.bit(self.orders[stack][self.halved]) == 0
            mine, got = self.held[stack], self.gots[stack]
            self.held[stack] = jnp.concatenate([jnp.where(low, mine, got), jnp.where(low, got, mine)], axis=0)


def swap(values):
    return lax.ppermute(values, "tensor", [(0, 1), (1, 0)])


def body(count, tokens, lengths, w_qkv, w_attn, w_in, w_out, gain_attn, gain_mlp, blend, cotangent):
    rows, width = tokens.shape
    blocks = rows // BLOCK

    wq_own = w_qkv.transpose(1, 0, 2)
    wq_other = swap(wq_own)
    wa_other, wi_other, wo_other = swap(w_attn), swap(w_in), swap(w_out)
    blend_other = swap(blend)
    gain_one = gain_attn.reshape(1, width)
    gain_two = gain_mlp.reshape(1, width)
    smem = pl.BlockSpec(memory_space=pltpu.SMEM)

    def row_block(size, cols):
        return pl.BlockSpec((size, cols), lambda i: (i, 0))

    own_cols = 3 * wq_own.shape[2]
    normed, own = pl.pallas_call(
        norm_project_kernel,
        grid=(4,),
        in_specs=[row_block(rows // 4, width), whole((1, width)), whole(wq_own.shape)],
        out_specs=[row_block(rows // 4, width), row_block(rows // 4, own_cols)],
        out_shape=[jax.ShapeDtypeStruct((rows, width), BF), jax.ShapeDtypeStruct((rows, own_cols), BF)],
        compiler_params=params(60),
        cost_estimate=cost(5),
        name="norm_project",
    )(tokens, gain_one, wq_own)
    normed, wi_other, wo_other, wa_other = tie(normed, wi_other, wo_other, wa_other)
    other, packet = pl.pallas_call(
        project_state_kernel,
        in_specs=[smem] + [pl.BlockSpec(memory_space=pltpu.VMEM)] * 3,
        out_shape=[
            jax.ShapeDtypeStruct((rows, own_cols), BF),
            jax.ShapeDtypeStruct((PACKET, 128), BF),
        ],
        compiler_params=params(60),
        cost_estimate=cost(5),
        name="project_state",
    )(lengths, normed, wq_other, own)
    packet = swap(packet)

    units = w_out.shape[0]
    tall = rows // 4
    parts = units // (2 * LANES)
    vmem = pl.BlockSpec(memory_space=pltpu.VMEM)
    stack_rows = units * width // LANES
    attn_rows = w_attn.shape[0] * width // LANES
    anywhere = pl.BlockSpec(memory_space=pltpu.HBM)

    kept_shapes = [
        ((blocks, 4, 128, 128), BF),
        ((blocks, HALO, 1024), BF),
        ((blocks, 4, BLOCK + HALO, 256), BF),
        ((blocks, 4, BLOCK, 256), BF),
        ((rows, width), BF),
        ((rows, width), BF),
    ]
    stored_shapes = [((rows, width), BF)] + kept_shapes + [((rows, 2 * units), BF)]
    branch, gmix, ggain_mlp, *outs = pl.pallas_call(
        partial(layer_kernel, blocks, parts),
        in_specs=[smem] * 3 + [vmem] * 4 + [anywhere] * 8,
        out_specs=[vmem] * 5 + [anywhere] * 12,
        out_shape=[
            jax.ShapeDtypeStruct((rows, width), BF),
            jax.ShapeDtypeStruct((rows, width), BF),
            jax.ShapeDtypeStruct((8, width), F32),
            jax.ShapeDtypeStruct((attn_rows, LANES), BF),
            jax.ShapeDtypeStruct((attn_rows, LANES), BF),
        ]
        + [jax.ShapeDtypeStruct(shape, kind) for shape, kind in stored_shapes]
        + [jax.ShapeDtypeStruct((stack_rows, LANES), BF)] * 4,
        scratch_shapes=[
            pltpu.VMEM((rows, own_cols), BF),
            pltpu.VMEM((rows, own_cols), BF),
            pltpu.VMEM((rows, width), BF),
            pltpu.VMEM((rows, width), BF),
            pltpu.VMEM((2,) + w_in.shape, BF),
            pltpu.VMEM((2,) + w_out.shape, BF),
        ]
        + [pltpu.VMEM(shape, kind) for shape, kind in stored_shapes]
        + [
            pltpu.VMEM((2, 2, stack_rows, LANES), BF),
            pltpu.VMEM((4, 256, 128), F32),
            pltpu.VMEM((4, 8, 128), F32),
            pltpu.VMEM((HALO, 1024), BF),
            pltpu.VMEM((rows, width), F32),
            pltpu.VMEM((rows, 128), F32),
            pltpu.VMEM((rows, width), BF),
            pltpu.VMEM((width, rows), BF),
            pltpu.VMEM((width, rows), BF),
            pltpu.VMEM((rows, width), F32),
            pltpu.SemaphoreType.DMA((64,)),
        ],
        compiler_params=params(62),
        cost_estimate=cost(30),
        name="layer",
    )(
        lengths,
        blend,
        blend_other,
        packet,
        gain_two,
        w_attn,
        wa_other,
        own,
        other,
        tokens,
        cotangent,
        w_in,
        wi_other,
        w_out,
        wo_other,
    )
    attn_grads, outs = outs[:2], outs[2:]
    mixed, *kept = outs[:7]
    active, out_own, in_own, out_sent, in_sent = outs[7:]

    feed_sum = Reduction(
        [([out_own, swap(out_sent)], 0, stack_rows), ([in_own, swap(in_sent)], 0, stack_rows)], count
    )
    wanted = feed_sum.steps
    if wanted > 0:
        cuts = feed_sum.outgoing()
        gmix, *cuts = tie(gmix, *cuts)
        feed_sum.send(cuts)

    steps = blocks // STEP_BLOCKS

    def back_block(*shape):
        return pl.BlockSpec(
            (shape[0] * STEP_BLOCKS,) + shape[1:], lambda i: (steps - 1 - i,) + (0,) * (len(shape) - 1)
        )

    gq, gk, gv, packet_back, gblend = pl.pallas_call(
        mixer_backward_kernel,
        grid=(steps,),
        in_specs=[
            smem,
            smem,
            smem,
            back_block(BLOCK, own_cols),
            back_block(BLOCK, own_cols),
            back_block(1, 4, 128, 128),
            back_block(1, HALO, 1024),
            back_block(1, 4, BLOCK + HALO, 256),
            back_block(1, 4, BLOCK, 256),
            back_block(BLOCK, width),
            back_block(BLOCK, width),
            back_block(BLOCK, width),
        ],
        out_specs=[back_block(BLOCK, width)] * 3 + [whole((PACKET, 128)), whole((2, 4, 8, 128))],
        out_shape=[jax.ShapeDtypeStruct((rows, width), BF)] * 3
        + [jax.ShapeDtypeStruct((PACKET, 128), BF), jax.ShapeDtypeStruct((2, 4, 8, 128), F32)],
        scratch_shapes=[
            pltpu.VMEM((HALO, 1024), F32),
            pltpu.VMEM((4, 256, 128), F32),
            pltpu.VMEM((4, 8, 128), F32),
        ],
        compiler_params=params(60),
        cost_estimate=cost(20),
        name="mixer_backward",
    )(lengths, blend, blend_other, own, other, *kept, gmix)
    if wanted > 1:
        (packet_back,) = feed_sum.after(packet_back)
    packet_got = swap(packet_back)
    if wanted > 1:
        cuts = feed_sum.outgoing()
        packet_got, *cuts = tie(packet_got, *cuts)
        feed_sum.send(cuts)

    wq_shape = (3 * width + attn_rows + EXTRA, own_cols // 3)
    kv_cols = 2 * own_cols // 3
    gproj, wq_mine, wq_sent = pl.pallas_call(
        finish_kernel,
        in_specs=[smem] + [vmem] * 3 + [anywhere] * 11,
        out_specs=[anywhere] * 3,
        out_shape=[
            jax.ShapeDtypeStruct((rows, 2 * kv_cols), BF),
            jax.ShapeDtypeStruct(wq_shape, BF),
            jax.ShapeDtypeStruct(wq_shape, BF),
        ],
        scratch_shapes=[
            pltpu.VMEM((PACKET, 128), BF),
            pltpu.VMEM((rows, kv_cols), BF),
            pltpu.VMEM((rows, kv_cols), BF),
        ]
        + [pltpu.VMEM((rows, width), BF)] * 4
        + [pltpu.VMEM(wq_own.shape, BF)] * 2
        + [
            pltpu.VMEM((rows, 2 * kv_cols), BF),
            pltpu.VMEM(wq_shape, BF),
            pltpu.VMEM(wq_shape, BF),
            pltpu.SemaphoreType.DMA((24,)),
        ],
        compiler_params=params(60),
        cost_estimate=cost(8),
        name="finish",
    )(
        lengths,
        gblend,
        ggain_mlp,
        gain_one,
        packet_got,
        own,
        other,
        gk,
        gv,
        gq,
        normed,
        wq_own,
        wq_other,
        *attn_grads,
    )

    def layer_output(active):
        return pl.pallas_call(
            output_kernel,
            grid=(4,),
            in_specs=[row_block(tall, width), row_block(tall, width), row_block(tall, 2 * units)]
            + [whole(w_attn.shape)] * 2
            + [whole(w_out.shape)] * 2,
            out_specs=row_block(tall, width),
            out_shape=jax.ShapeDtypeStruct((rows, width), BF),
            compiler_params=params(60),
            cost_estimate=cost(5),
            name="layer_output",
        )(tokens, mixed, active, w_attn, wa_other, w_out, wo_other)

    def input_gradient(gproj):
        return pl.pallas_call(
            input_grad_kernel,
            grid=(4,),
            in_specs=[
                row_block(tall, width),
                row_block(tall, 2 * kv_cols),
                row_block(tall, width),
                row_block(tall, width),
                whole((1, width)),
                whole(wq_own.shape),
                whole(wq_own.shape),
            ],
            out_specs=row_block(tall, width),
            out_shape=jax.ShapeDtypeStruct((rows, width), BF),
            compiler_params=params(60),
            cost_estimate=cost(7),
            name="input_grad",
        )(gq, gproj, tokens, branch, gain_one, wq_own, wq_other)

    if wanted > 1:
        (wq_sent,) = feed_sum.after(wq_sent)
    wq_got = swap(wq_sent)
    cut = wq_got.shape[0] // 2
    wq_sum = Reduction([([wq_mine, wq_got], 0, cut), ([wq_mine, wq_got], cut, cut)], count, True)
    beside = {0: lambda: input_gradient(gproj), 3: lambda: layer_output(active)}
    done = {}
    step = 0
    while not (feed_sum.finished() and wq_sum.finished()):
        running = [reduction for reduction in (wq_sum, feed_sum) if not reduction.finished()]
        cuts = [reduction.next_cuts() for reduction in running]
        flat = list(tie(*[cut for some in cuts for cut in some], gproj, active))
        active, gproj = flat.pop(), flat.pop()
        for reduction, some in zip(running, cuts):
            reduction.next_send([flat.pop(0) for _ in some])
        if step in beside:
            done[step] = beside[step]()
            for reduction in running:
                (done[step],) = reduction.after(done[step])
        for reduction in running:
            reduction.next_take()
        step += 1
    for step in beside:
        if step not in done:
            done[step] = beside[step]()
    grad_input, output = done[0], done[3]

    out_mine, out_got, in_mine, in_got = feed_sum.parts()
    bits = feed_sum.last_bits()
    if wanted > 1:
        out_mine, in_mine, *wq_sum.held = tie(out_mine, in_mine, *wq_sum.held)
    grad_shapes = [jax.ShapeDtypeStruct(w_out.shape, F32), jax.ShapeDtypeStruct(w_in.shape, F32)]
    wo_grad, wi_grad = pl.pallas_call(
        put_part_kernel,
        grid_spec=pltpu.PrefetchScalarGridSpec(
            num_scalar_prefetch=1,
            grid=(1,),
            in_specs=[whole(out_mine.shape), whole(in_mine.shape)],
            out_specs=[
                pl.BlockSpec((units, LANES), lambda i, places: (0, places[0])),
                pl.BlockSpec((width, units // 2), lambda i, places: (0, places[1])),
            ],
        ),
        out_shape=grad_shapes,
        compiler_params=params(60),
        cost_estimate=cost(2),
        name="put_part",
    )(bits, out_mine, in_mine)
    if wanted > 1:
        wo_grad, wi_grad, out_got, in_got = tie(wo_grad, wi_grad, out_got, in_got)
        (wi_grad,) = wq_sum.after(wi_grad)
    wq_parts = wq_sum.parts()
    last_inputs = [out_got, in_got] + wq_parts
    wo_grad, wi_grad, wq_grad, wa_grad, ggain_one, ggain_two, gblend_all = pl.pallas_call(
        last_output_kernel,
        in_specs=[smem] + [anywhere] * 8,
        out_specs=[anywhere] * 2 + [vmem] * 5,
        out_shape=grad_shapes
        + [
            jax.ShapeDtypeStruct((3 * width, own_cols // 3), F32),
            jax.ShapeDtypeStruct(w_attn.shape, F32),
            jax.ShapeDtypeStruct((1, width), F32),
            jax.ShapeDtypeStruct((1, width), F32),
            jax.ShapeDtypeStruct(blend.shape, F32),
        ],
        scratch_shapes=[pltpu.VMEM(part.shape, BF) for part in last_inputs]
        + [
            pltpu.VMEM((units, LANES), F32),
            pltpu.VMEM((width, units // 2), F32),
            pltpu.SemaphoreType.DMA((16,)),
        ],
        input_output_aliases={7: 0, 8: 1},
        compiler_params=params(60),
        cost_estimate=cost(3),
        name="last_output",
    )(bits, *last_inputs, wo_grad, wi_grad)

    return (
        output,
        grad_input,
        wq_grad.reshape(wq_own.shape).transpose(1, 0, 2),
        wa_grad,
        wi_grad,
        wo_grad,
        ggain_one.reshape(width),
        ggain_two.reshape(width),
        gblend_all,
    )


def solution(mesh):
    return jax.shard_map(
        partial(body, mesh.shape["dp"]),
        mesh=mesh,
        in_specs=(
            P(("dp", "tensor"), None),
            P("dp", None),
            P(None, None, "tensor"),
            P("tensor", None),
            P(None, "tensor"),
            P("tensor", None),
            P(),
            P(),
            P(None, "tensor"),
            P(("dp", "tensor"), None),
        ),
        out_specs=(
            P(("dp", "tensor"), None),
            P(("dp", "tensor"), None),
            P(None, None, "tensor"),
            P("tensor", None),
            P(None, "tensor"),
            P("tensor", None),
            P(),
            P(),
            P(None, "tensor"),
        ),
        check_vma=False,
    )
```

```python
from functools import partial

import jax
import jax.numpy as jnp
from jax import lax
from jax.experimental import pallas as pl
from jax.experimental.pallas import tpu as pltpu
from jax.sharding import PartitionSpec as P

BAND = 30
HALO = 32
EXTRA = 64
LATE_TURN = 1
BLOCK = 128
EPS = 1e-06
BF = jnp.bfloat16
F32 = jnp.float32
GELU_A = 0.7978845608028654
GELU_B = 0.044715


def nn(left, right):
    return lax.dot_general(left, right, (((1,), (0,)), ((), ())), preferred_element_type=F32)


def nt(left, right):
    return lax.dot_general(left, right, (((1,), (1,)), ((), ())), preferred_element_type=F32)


def tn(left, right):
    return lax.dot_general(left, right, (((0,), (0,)), ((), ())), preferred_element_type=F32)


def iota(shape, dim):
    return lax.broadcasted_iota(jnp.int32, shape, dim)


def whole(shape):
    return pl.BlockSpec(shape, lambda *_: (0,) * len(shape))


def params(mebibytes):
    return pltpu.CompilerParams(vmem_limit_bytes=mebibytes << 20)


def cost(micros):
    return pl.CostEstimate(flops=int(micros * 1e7), bytes_accessed=1 << 20, transcendentals=0)


def tie(*values):
    return lax.optimization_barrier(values)


class Copies:
    def __init__(self, sems):
        self.sems = sems
        self.used = 0

    def make(self, source, target):
        self.used += 1
        return pltpu.make_async_copy(source, target, self.sems.at[self.used - 1])


def document_ends(lengths_ref, rows):
    end = -lax.axis_index("tensor") * rows
    ends = [end]
    for doc in range(lengths_ref.shape[1]):
        end = end + lengths_ref[0, doc]
        ends.append(end)
    return ends[1:] + ends[:1]


def starts_of(ends, places):
    start = jnp.full(places.shape, ends[-1], jnp.int32)
    for end in ends[:-1]:
        start = jnp.where(places >= end, jnp.maximum(start, end), start)
    return start


def start_at(ends, place):
    start = ends[-1]
    for end in ends[:-1]:
        start = jnp.where(place >= end, jnp.maximum(start, end), start)
    return start


def norm_project_kernel(x_ref, gain_ref, w_ref, normed_ref, out_ref):
    x = x_ref[...].astype(F32)
    r = lax.rsqrt(jnp.mean(x * x, axis=1, keepdims=True) + EPS)
    normed = (x * r * gain_ref[...]).astype(BF)
    normed_ref[...] = normed
    project(normed, w_ref, out_ref)


def project(normed, w_ref, out_ref):
    cols = w_ref.shape[2]
    for kind in range(3):
        out_ref[:, cols * kind : cols * kind + cols] = nn(normed, w_ref[kind]).astype(BF)


PACKET = 4 * (128 + 16) + 8 * HALO


def packed_state(state):
    return jnp.concatenate([state[:64] + state[64:128], state[128:192] + state[192:]], axis=0).astype(BF)


def unpacked_state(packed, diag):
    one, two = packed[:64], packed[64:]
    state = jnp.concatenate([one, one, two, two], axis=0)
    return jnp.where(diag, state, jnp.zeros_like(state))


def pack(packet_ref, pair, state, total):
    base = 144 * pair
    packet_ref[base : base + 128] = packed_state(state)
    packet_ref[base + 128 : base + 144] = jnp.broadcast_to(total, (16, 128)).astype(BF)


def pack_halo(packet_ref, kind, pair, rows):
    base = 576 + HALO * (4 * kind + pair)
    packet_ref[base : base + HALO] = rows


def unpack(packet_ref, pair, diag):
    base = 144 * pair
    state = unpacked_state(packet_ref[base : base + 128].astype(F32), diag)
    return state, packet_ref[base + 128 : base + 136].astype(F32)


def unpack_halo(packet_ref, kind, pair):
    base = 576 + HALO * (4 * kind + pair)
    return packet_ref[base : base + HALO]


def first_feature(values):
    return jnp.where(values > 0, values + 1.0, jnp.exp(jnp.minimum(values, 0.0))).astype(BF)


def second_feature(values):
    return jnp.tanh(values).astype(BF)


def pair_diag(rows, cols):
    row = iota((rows, cols), 0)
    col = iota((rows, cols), 1)
    return ((row // 64) % 2) == ((col // 64) % 2)


def project_state_kernel(lengths_ref, normed_ref, w_ref, own_ref, out_ref, packet_ref):
    rows = normed_ref.shape[0]
    project(normed_ref[...], w_ref, out_ref)
    member_from = start_at(document_ends(lengths_ref, rows), rows - 1)
    member = iota((rows, 1), 0) >= member_from
    ks, vs = [heads_of(own_ref, out_ref, kind) for kind in (1, 2)]
    wide = [jnp.where(member, k.astype(F32), 0.0) for k in ks]
    ones = [jnp.where(member, first_feature(k).astype(F32), 0.0) for k in wide]
    features = each(lambda k, one: jnp.concatenate([one.astype(BF), second_feature(k)], axis=1), wide, ones)
    states = each(tn, features, vs)
    diag = pair_diag(256, 128)
    for pair in PAIRS:
        slot = (pair + 2) % 4
        pack(packet_ref, slot, jnp.where(diag, states[pair], 0.0), jnp.sum(ones[pair], axis=0, keepdims=True))
        pack_halo(packet_ref, 0, slot, ks[pair][rows - HALO :])
        pack_halo(packet_ref, 1, slot, vs[pair][rows - HALO :])


def block_masks(ends, first):
    row_places = first + iota((1, 256), 1) % BLOCK
    start_row = starts_of(ends, row_places)
    window_places = first - HALO + iota((BLOCK + HALO, 256), 0)
    banded = (window_places <= row_places) & (
        window_places >= jnp.maximum(start_row, row_places - (BAND - 1))
    )
    key_places = first + iota((BLOCK, 256), 0)
    causal = (key_places <= row_places) & (key_places >= start_row)
    col_places = first + iota((BLOCK, 1), 0)
    start_col = starts_of(ends, col_places)
    key_lane = first + iota((BLOCK, BLOCK), 1)
    causal_q = ((key_lane <= col_places) & (key_lane >= start_col)).astype(F32).astype(BF)
    count = (col_places - start_col + 1).astype(F32)
    carried = start_col < first
    member_from = start_at(ends, first + BLOCK - 1)
    member = col_places >= member_from
    keep = member_from < first
    return banded, causal, causal_q, count, carried, member, keep


def stack_heads(values):
    lane = iota(values.shape, 1) % 128
    zero = jnp.zeros_like(values)
    return jnp.concatenate(
        [jnp.where(lane < 64, values, zero), jnp.where(lane >= 64, values, zero)], axis=0
    )


def pick_heads(values):
    half = values.shape[0] // 2
    lane = iota((half, values.shape[1]), 1) % 128
    return jnp.where(lane < 64, values[:half], values[half:])


def ones_diagonal():
    return pair_diag(128, 128).astype(F32).astype(BF)


def only(mask, values):
    return jnp.where(mask, values, jnp.zeros_like(values))


def each(function, *lists):
    return [function(*values) for values in zip(*lists)]


class Front:
    def __init__(self, qs, ks, prev_ks, blends, carries, masks, ones_diag):
        banded, causal, causal_q, count, carried, member, keep = masks
        self.q_stack = each(lambda q: stack_heads(q * 0.125), qs)
        self.window = each(lambda prev, k: jnp.concatenate([prev, k], axis=0), prev_ks, ks)
        scores = each(nt, self.window, self.q_stack)
        self.k_one = each(lambda k: first_feature(k.astype(F32)), ks)
        products = each(lambda k_one: nn(causal_q, k_one), self.k_one)
        self.q_one = each(lambda q: first_feature(q.astype(F32)), qs)
        self.sums = each(lambda product, carry: product + jnp.where(carried, carry, 0.0), products, carries)
        self.total = each(
            lambda q_one, sums: nn((q_one.astype(F32) * sums).astype(BF), ones_diag), self.q_one, self.sums
        )
        self.q_two = each(lambda q: second_feature(q.astype(F32)), qs)
        self.k_both = each(
            lambda k_one, k: jnp.concatenate([k_one, second_feature(k.astype(F32))], axis=1), self.k_one, ks
        )
        scores = each(lambda score: jnp.where(banded, score, -1e30), scores)
        raised = each(lambda score: jnp.exp(score - jnp.max(score, axis=0, keepdims=True)), scores)
        self.near = each(lambda r: r * (1.0 / jnp.sum(r, axis=0, keepdims=True)), raised)
        inverse = 1.0 / count
        self.ratio_one = each(lambda blend, total: blend[0] / total, blends, self.total)
        self.ratio_two = each(lambda blend: blend[1] * inverse, blends)
        self.q_scaled = each(
            lambda q_one, q_two, one, two: jnp.concatenate(
                [(q_one.astype(F32) * one).astype(BF), (q_two.astype(F32) * two).astype(BF)], axis=1
            ),
            self.q_one,
            self.q_two,
            self.ratio_one,
            self.ratio_two,
        )
        self.s_stack = each(stack_heads, self.q_scaled)
        far = each(nt, self.k_both, self.s_stack)
        self.weights = each(
            lambda near, far: jnp.concatenate(
                [near[:HALO].astype(BF), (near[HALO:] + jnp.where(causal, far, 0.0)).astype(BF)], axis=0
            ),
            self.near,
            far,
        )


PAIRS = range(4)


def pair_lanes(pair):
    return slice(128 * pair, 128 * pair + 128)


def value_lanes(pair):
    return slice(512 + 128 * pair, 640 + 128 * pair)


def heads_of(own_ref, other_ref, kind):
    first = own_ref.shape[1] // 3 * kind
    return [
        (own_ref if pair < 2 else other_ref)[:, first + 128 * (pair % 2) : first + 128 * (pair % 2) + 128]
        for pair in PAIRS
    ]


def pair_blends(own_ref, other_ref):
    first_head = iota((1, 128), 1) < 64
    rows = []
    for pair in PAIRS:
        ref = own_ref if pair < 2 else other_ref
        head = 2 * (pair % 2)
        rows.append([jnp.where(first_head, ref[kind, head], ref[kind, head + 1]) for kind in range(2)])
    return rows


def mixer_forward_block(
    index,
    total_rows,
    lengths_ref,
    own_ref,
    other_ref,
    blend_own_ref,
    blend_other_ref,
    state_out_ref,
    prev_out_ref,
    near_ref,
    weights_ref,
    sums_ref,
    total_ref,
    state_ref,
    sum_ref,
    prev_ref,
):
    first = index * BLOCK

    masks = block_masks(document_ends(lengths_ref, total_rows), first)
    banded, causal, causal_q, count, carried, member, keep = masks
    diag = pair_diag(256, 128)
    qs, ks, vs = [heads_of(own_ref, other_ref, kind) for kind in range(3)]
    prev = prev_ref[...]
    states = [state_ref[pair] for pair in PAIRS]
    sums_in = [sum_ref[pair] for pair in PAIRS]
    blends = pair_blends(blend_own_ref, blend_other_ref)
    front = Front(
        qs,
        ks,
        [prev[:, pair_lanes(pair)] for pair in PAIRS],
        blends,
        [total[0:1] for total in sums_in],
        masks,
        ones_diagonal(),
    )
    state_low = each(lambda state: state.astype(BF), states)
    inter = each(lambda q, state: nn(only(carried, q), state), front.q_scaled, state_low)
    added = each(lambda k, v: tn(only(member, k), v), front.k_both, vs)
    outs = [
        tn(front.weights[pair], jnp.concatenate([prev[:, value_lanes(pair)], vs[pair]], axis=0))
        for pair in PAIRS
    ]
    outs = each(lambda out, term: pick_heads(out) + term, outs, inter)
    for pair in PAIRS:
        state_out_ref[0, pair] = packed_state(states[pair])
        near_ref[0, pair] = front.near[pair].astype(BF)
        weights_ref[0, pair] = front.weights[pair][HALO:]
        sums_ref[:, pair_lanes(pair)] = front.sums[pair].astype(BF)
        total_ref[:, pair_lanes(pair)] = (1.0 / front.total[pair]).astype(BF)
        state_ref[pair] = jnp.where(keep, states[pair], 0.0) + jnp.where(diag, added[pair], 0.0)
        sum_ref[pair] = jnp.broadcast_to(front.sums[pair][BLOCK - 1 : BLOCK], (8, 128))
        prev_ref[:, pair_lanes(pair)] = ks[pair][BLOCK - HALO :]
        prev_ref[:, value_lanes(pair)] = vs[pair][BLOCK - HALO :]
    prev_out_ref[0] = prev
    return jnp.concatenate(outs, axis=1).astype(BF)


def mixer_backward_block(
    index,
    total_rows,
    lengths_ref,
    blend_own_ref,
    blend_other_ref,
    own_ref,
    other_ref,
    state_ref,
    prev_ref,
    near_ref,
    weights_ref,
    sums_ref,
    total_ref,
    grad_ref,
    gq_ref,
    gk_ref,
    gv_ref,
    blend_out_ref,
    halo_ref,
    back_state_ref,
    back_sum_ref,
):
    first = index * BLOCK
    ends = document_ends(lengths_ref, total_rows)
    blends = pair_blends(blend_own_ref, blend_other_ref)
    row_places = first + iota((1, 256), 1) % BLOCK
    key_places = first + iota((BLOCK, 256), 0)
    causal = (key_places <= row_places) & (key_places >= starts_of(ends, row_places))
    causal_k = causal[:, :BLOCK].astype(F32).astype(BF)
    col_places = first + iota((BLOCK, 1), 0)
    start_col = starts_of(ends, col_places)
    inverse = 1.0 / (col_places - start_col + 1).astype(F32)
    carried = start_col < first
    member_from = start_at(ends, first + BLOCK - 1)
    member = col_places >= member_from
    keep = member_from < first
    diag = pair_diag(256, 128)
    ones_diag = ones_diagonal()
    qs, ks, vs = [heads_of(own_ref, other_ref, kind) for kind in range(3)]
    prev = prev_ref[0]
    grads = [grad_ref[:, pair_lanes(pair)] for pair in PAIRS]
    states = [unpacked_state(state_ref[0, pair], diag) for pair in PAIRS]
    backs = [back_state_ref[pair] for pair in PAIRS]
    back_sums = [back_sum_ref[pair][0:1] for pair in PAIRS]
    nears = [near_ref[0, pair] for pair in PAIRS]
    wide_ks = [k.astype(F32) for k in ks]
    wide_qs = [q.astype(F32) for q in qs]
    raised_k = [jnp.exp(jnp.minimum(k, 0.0)) for k in wide_ks]
    raised_q = [jnp.exp(jnp.minimum(q, 0.0)) for q in wide_qs]
    tanh_ks = [jnp.tanh(k) for k in wide_ks]
    tanh_qs = [jnp.tanh(q) for q in wide_qs]
    k_both = each(
        lambda k, raised, t: jnp.concatenate(
            [jnp.where(k > 0, k + 1.0, raised).astype(BF), t.astype(BF)], axis=1
        ),
        wide_ks,
        raised_k,
        tanh_ks,
    )
    q_one = each(lambda q, raised: jnp.where(q > 0, q + 1.0, raised).astype(BF).astype(F32), wide_qs, raised_q)
    inverse_total = [total_ref[:, pair_lanes(pair)].astype(F32) for pair in PAIRS]
    ratio_one = each(lambda blend, total: blend[0] * total, blends, inverse_total)
    ratio_two = [blend[1] * inverse for blend in blends]
    q_scaled = each(
        lambda one, ratio, t, other: jnp.concatenate(
            [(one * ratio).astype(BF), (t.astype(BF).astype(F32) * other).astype(BF)], axis=1
        ),
        q_one,
        ratio_one,
        tanh_qs,
        ratio_two,
    )
    g_stack = each(stack_heads, grads)
    v_window = [jnp.concatenate([prev[:, value_lanes(pair)], vs[pair]], axis=0) for pair in PAIRS]
    grad_weights = each(nt, v_window, g_stack)
    dv = [
        nn(jnp.concatenate([nears[pair][:HALO], weights_ref[0, pair]], axis=0), g_stack[pair]) for pair in PAIRS
    ]
    up_inter = each(lambda grad, state: nt(only(carried, grad), state), grads, states)
    far = each(lambda gw: jnp.where(causal, gw[HALO:], 0.0).astype(BF), grad_weights)
    up = each(tn, far, k_both)
    s_stack = each(stack_heads, q_scaled)
    dfeat = each(nn, far, s_stack)
    near_wide = each(lambda near: near.astype(F32), nears)
    inner = each(lambda near, gw: near * gw, near_wide, grad_weights)
    dscores = each(
        lambda near, inner: (inner - near * jnp.sum(inner, axis=0, keepdims=True)).astype(BF),
        near_wide,
        inner,
    )
    up = each(lambda up, inter: pick_heads(up) + inter, up, up_inter)
    mean_one = each(
        lambda q, up, total: nn((q * up[:, :128]).astype(BF), ones_diag) * total,
        q_one,
        up,
        inverse_total,
    )
    window = [jnp.concatenate([prev[:, pair_lanes(pair)], ks[pair]], axis=0) for pair in PAIRS]
    q_stack = each(lambda q: stack_heads(q * 0.125), qs)
    gq_near = each(tn, dscores, window)
    dk = each(nn, dscores, q_stack)
    back_low = each(lambda back: back.astype(BF), backs)
    dv_far = each(lambda k, back: nn(only(member, k), back), k_both, back_low)
    dfeat_far = each(lambda v, back: nt(only(member, v), back), vs, back_low)
    added = each(lambda q, grad: tn(only(carried, q), grad), q_scaled, grads)
    weighted = each(lambda mean, q: (mean * q[:, :128].astype(F32)).astype(BF), mean_one, q_scaled)
    mean_back = each(lambda weight: nn(causal_k, weight), weighted)
    for pair in PAIRS:
        lanes, values = pair_lanes(pair), value_lanes(pair)
        up_one, up_two = up[pair][:, :128], up[pair][:, 128:]
        tanh_q, slope_q = tanh_qs[pair], raised_q[pair]
        up_two = up_two * inverse
        grad_one = ratio_one[pair] * (up_one - mean_one[pair] * sums_ref[:, lanes].astype(F32))
        grad_two = blends[pair][1] * up_two
        gq = pick_heads(gq_near[pair]) * 0.125 + grad_one * slope_q + grad_two * (1.0 - tanh_q * tanh_q)
        gq_ref[:, lanes] = gq.astype(BF)
        blend_out_ref[0, pair] += jnp.broadcast_to(
            jnp.sum(mean_one[pair], axis=0, keepdims=True) / 64.0, (8, 128)
        )
        blend_out_ref[1, pair] += jnp.broadcast_to(jnp.sum(tanh_q * up_two, axis=0, keepdims=True), (8, 128))
        dv_own = dv[pair][HALO:] + dv_far[pair]
        dfeat_all = dfeat[pair] + dfeat_far[pair]
        d_one = dfeat_all[:, :128] - mean_back[pair] - jnp.where(member, back_sums[pair], 0.0)
        d_two = dfeat_all[:, 128:]
        tanh_k, slope_k = tanh_ks[pair], raised_k[pair]
        gk = dk[pair][HALO:] + d_one * slope_k + d_two * (1.0 - tanh_k * tanh_k)
        gk_ref[: BLOCK - HALO, lanes] = gk[: BLOCK - HALO].astype(BF)
        gk_ref[BLOCK - HALO :, lanes] = (gk[BLOCK - HALO :] + halo_ref[:, lanes]).astype(BF)
        gv_ref[: BLOCK - HALO, lanes] = dv_own[: BLOCK - HALO].astype(BF)
        gv_ref[BLOCK - HALO :, lanes] = (dv_own[BLOCK - HALO :] + halo_ref[:, values]).astype(BF)
        halo_ref[:, lanes] = dk[pair][:HALO]
        halo_ref[:, values] = dv[pair][:HALO]
        back_state_ref[pair] = jnp.where(keep, backs[pair], 0.0) + jnp.where(diag, added[pair], 0.0)
        added_sum = jnp.sum(only(carried, weighted[pair].astype(F32)), axis=0, keepdims=True)
        back_sum_ref[pair] = jnp.broadcast_to(
            jnp.where(keep, back_sums[pair], 0.0) + added_sum, (8, 128)
        )


STEP_BLOCKS = 2


def mixer_backward_kernel(lengths_ref, blend_own_ref, blend_other_ref, *refs):
    inputs, outputs = refs[:9], refs[9:12]
    packet_ref, blend_out_ref, halo_ref, back_state_ref, back_sum_ref = refs[12:]
    step = pl.program_id(0)
    steps = pl.num_programs(0)

    @pl.when(step == 0)
    def _():
        for ref in (halo_ref, back_state_ref, back_sum_ref, blend_out_ref):
            ref[...] = jnp.zeros_like(ref)

    for sub in reversed(range(STEP_BLOCKS)):
        views = []
        for ref in inputs + outputs:
            unit = ref.shape[0] // STEP_BLOCKS
            views.append(ref.at[sub * unit : sub * unit + unit])
        mixer_backward_block(
            (steps - 1 - step) * STEP_BLOCKS + sub,
            steps * STEP_BLOCKS * BLOCK,
            lengths_ref,
            blend_own_ref,
            blend_other_ref,
            *views,
            blend_out_ref,
            halo_ref,
            back_state_ref,
            back_sum_ref,
        )

    @pl.when(step == steps - 1)
    def _():
        for pair in PAIRS:
            slot = (pair + 2) % 4
            pack(packet_ref, slot, back_state_ref[pair], back_sum_ref[pair][0:1])
            pack_halo(packet_ref, 0, slot, halo_ref[:, pair_lanes(pair)].astype(BF))
            pack_halo(packet_ref, 1, slot, halo_ref[:, value_lanes(pair)].astype(BF))


LANES = 256


def layer_kernel(
    blocks,
    parts,
    lengths_ref,
    blend_own_ref,
    blend_other_ref,
    packet_ref,
    gain_ref,
    wa_own_ref,
    wa_other_ref,
    own_hbm,
    other_hbm,
    x_hbm,
    cot_hbm,
    wi_own_hbm,
    wi_other_hbm,
    wo_own_hbm,
    wo_other_hbm,
    branch_ref,
    gmix_ref,
    ggain_ref,
    attn_own_ref,
    attn_sent_ref,
    mixed_hbm,
    state_hbm,
    prev_hbm,
    near_hbm,
    weights_hbm,
    sums_hbm,
    total_hbm,
    active_hbm,
    out_own_hbm,
    in_own_hbm,
    out_sent_hbm,
    in_sent_hbm,
    own_ref,
    other_ref,
    x_ref,
    grad_ref,
    wi_ref,
    wo_ref,
    mixed_ref,
    state_out_ref,
    prev_out_ref,
    near_ref,
    weights_ref,
    sums_ref,
    total_ref,
    active_ref,
    stack_ref,
    state_ref,
    sum_ref,
    prev_ref,
    y_ref,
    r_ref,
    normed_ref,
    normed_turned_ref,
    grad_turned_ref,
    back_ref,
    sems,
):
    copies = Copies(sems)
    rows, width = x_ref.shape
    heads = wa_own_ref.shape[0]
    units = wo_ref.shape[1]
    chunk_units = units // parts
    tokens = ((own_hbm, own_ref), (other_hbm, other_ref), (x_hbm, x_ref), (cot_hbm, grad_ref))
    first_loads = [copies.make(source.at[:BLOCK], target.at[:BLOCK]) for source, target in tokens]
    later_loads = [copies.make(source.at[BLOCK:], target.at[BLOCK:]) for source, target in tokens]
    weight_loads = [
        copies.make(source, target)
        for source, target in (
            (wi_own_hbm, wi_ref.at[0]),
            (wo_own_hbm, wo_ref.at[0]),
            (wi_other_hbm, wi_ref.at[1]),
            (wo_other_hbm, wo_ref.at[1]),
        )
    ]
    for load in first_loads + later_loads + weight_loads:
        load.start()
    for pair in PAIRS:
        state_ref[pair], sum_ref[pair] = unpack(packet_ref, pair, pair_diag(256, 128))
        prev_ref[:, pair_lanes(pair)] = unpack_halo(packet_ref, 0, pair)
        prev_ref[:, value_lanes(pair)] = unpack_halo(packet_ref, 1, pair)
    back_ref[...] = jnp.zeros_like(back_ref)
    for load in first_loads:
        load.wait()

    def block(step, _):
        @pl.when(step == 1)
        def _():
            for load in later_loads:
                load.wait()

        here = pl.ds(pl.multiple_of(step * BLOCK, BLOCK), BLOCK)
        only_here = pl.ds(step, 1)
        mixed = mixer_forward_block(
            step,
            rows,
            lengths_ref,
            own_ref.at[here],
            other_ref.at[here],
            blend_own_ref,
            blend_other_ref,
            state_out_ref.at[only_here],
            prev_out_ref.at[only_here],
            near_ref.at[only_here],
            weights_ref.at[only_here],
            sums_ref.at[here],
            total_ref.at[here],
            state_ref,
            sum_ref,
            prev_ref,
        )
        mixed_ref[here, :] = mixed
        hidden = x_ref[here, :].astype(F32)
        hidden = hidden + nn(mixed[:, :heads], wa_own_ref[...]) + nn(mixed[:, heads:], wa_other_ref[...])
        r = lax.rsqrt(jnp.mean(hidden * hidden, axis=1, keepdims=True) + EPS)
        y = hidden * r
        y_ref[here, :] = y
        r_ref[here, :] = jnp.broadcast_to(r, (BLOCK, r_ref.shape[1]))
        normed = (y * gain_ref[...]).astype(BF)
        normed_ref[here, :] = normed
        normed_turned_ref[:, here] = normed.T
        grad_turned_ref[:, here] = grad_ref[here, :].T
        return 0

    def some_blocks(step, _):
        for sub in range(STEP_BLOCKS):
            block(step * STEP_BLOCKS + sub, 0)
        return 0

    lax.fori_loop(0, blocks // STEP_BLOCKS, some_blocks, 0)
    stores = [
        copies.make(source, target)
        for source, target in (
            (mixed_ref, mixed_hbm),
            (state_out_ref, state_hbm),
            (prev_out_ref, prev_hbm),
            (near_ref, near_hbm),
            (weights_ref, weights_hbm),
            (sums_ref, sums_hbm),
            (total_ref, total_hbm),
        )
    ]
    for store in stores:
        store.start()
    for load in weight_loads:
        load.wait()
    chunk_stores = []
    for late in range(2 * parts):
        half, place = late // parts, late % parts
        out_target, in_target = ((out_own_hbm, in_own_hbm), (out_sent_hbm, in_sent_hbm))[half]
        spots = [(0, out_target, units * side + chunk_units * place, chunk_units) for side in range(width // LANES)]
        count = width * chunk_units // LANES
        spots.append((1, in_target, count * place, count))
        columns = pl.ds(late * chunk_units, chunk_units)
        chunk_stores.append(
            [
                copies.make(stack_ref.at[half, kind, pl.ds(row, count), :], target.at[pl.ds(row, count), :])
                for kind, target, row, count in spots
            ]
            + [copies.make(active_ref.at[:, columns], active_hbm.at[:, columns])]
        )

    def chunk(late, _):
        half, place = late // parts, late % parts
        normed = normed_ref[...]
        grad = grad_ref[...]
        first = pl.multiple_of(place * chunk_units, chunk_units)
        wi = wi_ref[half, :, pl.ds(first, chunk_units)]
        wo = wo_ref[half, pl.ds(first, chunk_units), :]
        spans = [slice(LANES * piece, LANES * piece + LANES) for piece in range(chunk_units // LANES)]
        us = [nn(normed, wi[:, span]) for span in spans]
        gacts = [nt(grad, wo[span, :]) for span in spans]
        gpres = []
        for piece in range(len(spans)):
            u = us[piece]
            square = u * u
            t = jnp.tanh(u * (GELU_A + (GELU_A * GELU_B) * square))
            gate = 0.5 + 0.5 * t
            active = (u * gate).astype(BF)
            column = pl.multiple_of(late * chunk_units + LANES * piece, LANES)
            active_ref[:, pl.ds(column, LANES)] = active
            slope = gate + (u * (0.5 - 0.5 * t * t)) * (GELU_A + (3.0 * GELU_A * GELU_B) * square)
            gpre = (gacts[piece] * slope).astype(BF)
            gpres.append(gpre)
            gout = nn(grad_turned_ref[...], active).astype(BF).T
            spot = len(spans) * place + piece
            for side in range(width // LANES):
                row = pl.multiple_of(units * side + LANES * spot, LANES)
                stack_ref[half, 0, pl.ds(row, LANES), :] = gout[:, LANES * side : LANES * side + LANES]
            row = pl.multiple_of(width * spot, LANES)
            stack_ref[half, 1, pl.ds(row, width), :] = nn(normed_turned_ref[...], gpre).astype(BF)
        back_ref[...] += nt(jnp.concatenate(gpres, axis=1), wi)
        for number, some in enumerate(chunk_stores):

            @pl.when(late == number)
            def _(some=some):
                for store in some:
                    store.start()

        return 0

    lax.fori_loop(0, 2 * parts, chunk, 0)
    back, y = back_ref[...], y_ref[...]
    scaled = back * gain_ref[...]
    mean = jnp.mean(scaled * y, axis=1, keepdims=True)
    ghid = grad_ref[...].astype(F32) + r_ref[:, :1] * (scaled - y * mean)
    branch = ghid.astype(BF)
    branch_ref[...] = branch
    gmix_ref[:, :heads] = nt(branch, wa_own_ref[...]).astype(BF)
    gmix_ref[:, heads:] = nt(branch, wa_other_ref[...]).astype(BF)
    ggain_ref[...] = jnp.broadcast_to(jnp.sum(back * y, axis=0, keepdims=True), ggain_ref.shape)
    gattn = tn(mixed_ref[...], branch).astype(BF)
    for half, ref in enumerate((attn_own_ref, attn_sent_ref)):
        for side in range(width // LANES):
            lanes = slice(LANES * side, LANES * side + LANES)
            ref[heads * side : heads * side + heads] = gattn[heads * half : heads * half + heads, lanes]
    for store in stores + [store for some in chunk_stores for store in some]:
        store.wait()


def output_kernel(x_ref, mixed_ref, active_ref, wa_own_ref, wa_other_ref, wo_own_ref, wo_other_ref, out_ref):
    heads = wa_own_ref.shape[0]
    units = wo_own_ref.shape[0]
    total = x_ref[...].astype(F32)
    total = total + (nn(mixed_ref[:, :heads], wa_own_ref[...]) + nn(mixed_ref[:, heads:], wa_other_ref[...]))
    total = total + (nn(active_ref[:, :units], wo_own_ref[...]) + nn(active_ref[:, units:], wo_other_ref[...]))
    out_ref[...] = total.astype(BF)


def finish_kernel(
    lengths_ref,
    gblend_ref,
    ggain_ref,
    gain_ref,
    packet_hbm,
    own_hbm,
    other_hbm,
    gk_hbm,
    gv_hbm,
    gq_hbm,
    normed_hbm,
    w_own_hbm,
    w_other_hbm,
    attn_own_hbm,
    attn_sent_hbm,
    gkv_hbm,
    wgrad_own_hbm,
    wgrad_sent_hbm,
    packet_ref,
    own_ref,
    other_ref,
    gk_ref,
    gv_ref,
    gq_ref,
    normed_ref,
    w_own_ref,
    w_other_ref,
    gkv_ref,
    wgrad_own_ref,
    wgrad_sent_ref,
    sems,
):
    copies = Copies(sems)
    rows, width = normed_ref.shape
    cols = w_own_ref.shape[2]
    wgrads = (wgrad_own_ref, wgrad_sent_ref)
    attn_rows = attn_own_hbm.shape[0]
    keys_values = slice(cols, 3 * cols)
    loads = [
        copies.make(source, target)
        for source, target in (
            (packet_hbm, packet_ref),
            (own_hbm.at[:, keys_values], own_ref),
            (gk_hbm, gk_ref),
            (gv_hbm, gv_ref),
            (other_hbm.at[:, keys_values], other_ref),
            (normed_hbm, normed_ref),
            (gq_hbm, gq_ref),
            (w_own_hbm, w_own_ref),
            (w_other_hbm, w_other_ref),
            (attn_own_hbm, wgrad_own_ref.at[3 * width : 3 * width + attn_rows]),
            (attn_sent_hbm, wgrad_sent_ref.at[3 * width : 3 * width + attn_rows]),
        )
    ]
    gkv_stores, wgrad_stores = [], []
    for half, target in enumerate((wgrad_own_hbm, wgrad_sent_hbm)):
        lanes = slice(2 * cols * half, 2 * cols * half + 2 * cols)
        gkv_stores.append(copies.make(gkv_ref.at[:, lanes], gkv_hbm.at[:, lanes]))
        spans = [slice(width * kind, width * kind + width) for kind in range(3)]
        spans.append(slice(3 * width, wgrads[half].shape[0]))
        wgrad_stores.append([copies.make(wgrads[half].at[span], target.at[span]) for span in spans])
    for load in loads:
        load.start()
    live = lax.axis_index("tensor") == 0
    member_from = start_at(document_ends(lengths_ref, rows), rows - 1)
    member = (iota((rows, 1), 0) >= member_from) & live
    diag = pair_diag(256, 128)
    cut = rows - HALO
    for load in loads[:4]:
        load.wait()
    for pair in PAIRS:
        if pair == 2:
            loads[4].wait()
        src = own_ref if pair < 2 else other_ref
        col = 128 * (pair % 2)
        lanes = pair_lanes(pair)
        k = src[:, col : col + 128].astype(F32)
        v = src[:, cols + col : cols + col + 128]
        back, back_sum = unpack(packet_ref, pair, diag)
        back, back_sum = back.astype(BF), back_sum[0:1]
        t = jnp.tanh(k)
        raised = jnp.exp(jnp.minimum(k, 0.0))
        k_both = jnp.concatenate([jnp.where(k > 0, k + 1.0, raised).astype(BF), t.astype(BF)], axis=1)
        dfeat = nt(v, back)
        extra_k = (dfeat[:, :128] - back_sum) * raised + dfeat[:, 128:] * (1.0 - t * t)
        extra_v = nn(k_both, back)
        for kind, (grad_ref, extra) in enumerate(((gk_ref, extra_k), (gv_ref, extra_v))):
            grad = grad_ref[:, lanes].astype(F32) + jnp.where(member, extra, 0.0)
            halo = jnp.where(live, unpack_halo(packet_ref, kind, pair).astype(F32), 0.0)
            base = cols * (2 * (pair // 2) + kind) + col
            gkv_ref[:cut, base : base + 128] = grad[:cut].astype(BF)
            gkv_ref[cut:, base : base + 128] = (grad[cut:] + halo).astype(BF)
        if pair % 2 == 1:
            gkv_stores[pair // 2].start()
    for load in loads[5:]:
        load.wait()
    normed = normed_ref[...].T
    ones = jnp.ones((1, cols), BF)
    gain_grad = jnp.zeros((1, width), F32)
    for half, (wgrad_ref, w_ref) in enumerate(zip(wgrads, (w_own_ref, w_other_ref))):
        for kind in range(3):
            if kind == 0:
                grad = gq_ref[:, cols * half : cols * half + cols]
            else:
                first = cols * (2 * half + kind - 1)
                grad = gkv_ref[:, first : first + cols]
            wgrad = nn(normed, grad)
            wgrad_ref[width * kind : width * kind + width] = wgrad.astype(BF)
            wgrad_stores[half][kind].start()
            products = wgrad * w_ref[kind].astype(F32)
            high = products.astype(BF)
            low = (products - high.astype(F32)).astype(BF)
            gain_grad = gain_grad + nt(ones, high) + nt(ones, low)
    gain_grad = gain_grad / gain_ref[...]
    for half, wgrad_ref in enumerate(wgrads):
        blends = [
            jnp.concatenate([gblend_ref[kind, 2 * half + pair][0:1] for pair in range(2)], axis=1)
            for kind in range(2)
        ]
        gains = [gain_grad[:, :256], gain_grad[:, 256:], ggain_ref[0:1, :256], ggain_ref[0:1, 256:]]
        extra = jnp.concatenate(blends + gains + [jnp.zeros((10, 256), F32)], axis=0)
        base = 3 * width + attn_rows
        wgrad_ref[base : base + 16] = extra.astype(BF)
        wgrad_ref[base + 16 :] = jnp.zeros((EXTRA - 16, 256), BF)
        wgrad_stores[half][3].start()
    for store in gkv_stores + wgrad_stores[0] + wgrad_stores[1]:
        store.wait()


def input_grad_kernel(gq_ref, gkv_ref, x_ref, branch_ref, gain_ref, w_own_ref, w_other_ref, out_ref):
    cols = w_own_ref.shape[2]
    gnormed = None
    for half, w_ref in enumerate((w_own_ref, w_other_ref)):
        for kind in range(3):
            if kind == 0:
                grad = gq_ref[:, cols * half : cols * half + cols]
            else:
                first = cols * (2 * half + kind - 1)
                grad = gkv_ref[:, first : first + cols]
            term = nt(grad, w_ref[kind])
            gnormed = term if gnormed is None else gnormed + term
    x = x_ref[...].astype(F32)
    r = lax.rsqrt(jnp.mean(x * x, axis=1, keepdims=True) + EPS)
    y = x * r
    scaled = gnormed * gain_ref[...]
    grad = branch_ref[...].astype(F32) + r * (scaled - y * jnp.mean(scaled * y, axis=1, keepdims=True))
    out_ref[...] = grad.astype(BF)


def merged(low, mine, got):
    return jnp.where(low, mine, got), jnp.where(low, got, mine)


def put_rows(ref, first_row, lane, parts, first, count):
    rows = parts[0].shape[0]
    lanes = parts[0].shape[1]
    for place, part in enumerate(parts):
        low, high = max(first, rows * place), min(first + count, rows * place + rows)
        if low < high:
            values = part[low - rows * place : high - rows * place].astype(F32)
            ref[first_row + low - first : first_row + high - first, lane : lane + lanes] = values


def feed_output_kernel(
    bits_ref,
    out_mine_hbm,
    in_mine_hbm,
    out_got_hbm,
    in_got_hbm,
    wo_hbm,
    wi_hbm,
    out_mine_ref,
    in_mine_ref,
    out_got_ref,
    in_got_ref,
    wo_ref,
    wi_ref,
    sems,
):
    copies = Copies(sems)
    parts = ((out_mine_ref, in_mine_ref), (out_got_ref, in_got_ref))
    loads = [
        copies.make(source, target)
        for source, target in (
            (out_mine_hbm, out_mine_ref),
            (in_mine_hbm, in_mine_ref),
            (out_got_hbm, out_got_ref),
            (in_got_hbm, in_got_ref),
        )
    ]
    for load in loads:
        load.start()
    units, wide = wo_ref.shape[1], wo_ref.shape[2]
    width, span = wi_ref.shape[1], wi_ref.shape[2]
    middle = units // 2
    stores = []
    for place, (out_part_ref, in_part_ref) in enumerate(parts):
        wo_first = bits_ref[0] if place == 0 else 1 - bits_ref[0]
        wi_first = bits_ref[1] if place == 0 else 1 - bits_ref[1]
        loads[2 * place].wait()
        wo_ref[place] = out_part_ref[...].astype(F32)
        column = pl.multiple_of(wo_first * wide, LANES)
        for rows in (slice(0, middle), slice(middle, units)):
            stores.append(copies.make(wo_ref.at[place, rows], wo_hbm.at[rows, pl.ds(column, wide)]))
            stores[-1].start()
        loads[2 * place + 1].wait()
        for side in range(span // LANES):
            lanes = slice(LANES * side, LANES * side + LANES)
            wi_ref[place, :, lanes] = in_part_ref[width * side : width * side + width].astype(F32)
            column = pl.multiple_of(wi_first * span + LANES * side, LANES)
            stores.append(copies.make(wi_ref.at[place, :, lanes], wi_hbm.at[:, pl.ds(column, LANES)]))
            stores[-1].start()
    for store in stores:
        store.wait()


def last_output_kernel(
    bits_ref,
    a_mine_hbm,
    b_mine_hbm,
    a_got_hbm,
    b_got_hbm,
    wq_ref,
    wa_ref,
    gain_one_ref,
    gain_two_ref,
    blend_ref,
    a_mine_ref,
    b_mine_ref,
    a_got_ref,
    b_got_ref,
    sems,
):
    copies = Copies(sems)
    loads = [
        copies.make(source, target)
        for source, target in (
            (a_mine_hbm, a_mine_ref),
            (b_mine_hbm, b_mine_ref),
            (a_got_hbm, a_got_ref),
            (b_got_hbm, b_got_ref),
        )
    ]
    for load in loads:
        load.start()
    for load in loads:
        load.wait()
    heads, width = wa_ref.shape
    parts = merged(bits_ref[0] == 0, a_mine_ref[...], a_got_ref[...])
    parts += merged(bits_ref[1] == 0, b_mine_ref[...], b_got_ref[...])
    rows = a_mine_ref.shape[0]
    put_rows(wq_ref, 0, 0, parts, 0, 3 * width)
    for side in range(width // LANES):
        put_rows(wa_ref, 0, LANES * side, parts, 3 * width + heads * side, heads)
    rest = parts[3][rows - EXTRA : rows - EXTRA + 16].astype(F32)
    gain_one_ref[...] = jnp.concatenate([rest[2:3], rest[3:4]], axis=1)
    gain_two_ref[...] = jnp.concatenate([rest[4:5], rest[5:6]], axis=1)
    sums = [jnp.sum(rest[:2, 64 * head : 64 * head + 64], axis=1, keepdims=True) for head in range(4)]
    blend_ref[...] = jnp.concatenate(sums, axis=1)


def steps_of(count, late_sizes):
    steps = []
    stride = 1
    while stride < count:
        left = count // stride
        size = next(size for size in ((2,) if len(steps) < 2 else late_sizes) if left % size == 0)
        steps.append((stride, size))
        stride *= size
    return steps


def flip(values, count, step):
    stride, _ = step
    pairs = [(src, src + stride * (1 - 2 * ((src // stride) % 2))) for src in range(count)]
    return lax.ppermute(values, "dp", pairs)


def trade(values, count, step):
    stride, size = step
    groups = [
        [first + stride * digit for digit in range(size)]
        for first in range(count)
        if (first // stride) % size == 0
    ]
    return lax.all_to_all(
        values, "dp", split_axis=0, concat_axis=0, axis_index_groups=groups, tiled=True
    )


class Reduction:
    def __init__(self, stacks, count, whole_late=False):
        self.stacks = [[(term, first) for term in terms] for terms, first, _ in stacks]
        self.rows = [rows for _, _, rows in stacks]
        self.count = count
        steps = steps_of(count, (2,) if whole_late else (4, 2))
        self.orders = [steps, steps[1::-1] + steps[2:]]
        self.whole_late = whole_late
        self.left = min(2, len(steps)) if whole_late else len(steps)
        self.taken = 0
        self.place = lax.axis_index("dp")
        self.held = None
        self.gots = []

    def digit(self, step):
        return (self.place // step[0]) % step[1]

    def cut(self, stack, first, rows):
        total = None
        for term, offset in self.stacks[stack]:
            part = lax.dynamic_slice_in_dim(term, offset + first, rows, 0).astype(F32)
            total = part if total is None else total + part
        return total.astype(BF)

    def after(self, *tokens):
        count = len(self.gots)
        tied = tie(*self.gots, *tokens)
        self.gots = list(tied[:count])
        return tied[count:]

    def gathering(self):
        return self.taken == len(self.orders[0])

    def level(self):
        return self.left - 1 if self.gathering() else self.taken

    def cuts(self):
        if self.gathering():
            if self.held is None:
                self.held = [self.cut(stack, 0, self.rows[stack]) for stack in range(2)]
            if self.level() < 2:
                return list(self.held)
            both = jnp.concatenate(self.held, axis=0)
            return [jnp.broadcast_to(both[None], (self.orders[0][self.level()][1],) + both.shape)]
        if self.level() < 2:
            cuts = []
            for stack in range(2):
                step = self.orders[stack][self.level()]
                rows = self.rows[stack] // 2
                cuts.append(self.cut(stack, (1 - self.digit(step)) * rows, rows))
            return cuts
        size = self.orders[0][self.level()][1]
        wholes = [self.cut(stack, 0, self.rows[stack]) for stack in range(2)]
        if self.whole_late:
            self.sent = jnp.concatenate(wholes, axis=0)
            return [self.sent]
        return [jnp.concatenate([part.reshape(size, -1, part.shape[1]) for part in wholes], axis=1)]

    def send(self, cuts):
        steps = [order[self.level()] for order in self.orders]
        if self.level() < 2:
            self.gots = [flip(cut, self.count, step) for cut, step in zip(cuts, steps)]
        elif self.whole_late:
            self.sent = cuts[0]
            self.gots = [flip(cuts[0], self.count, steps[0])]
        else:
            self.gots = [trade(cuts[0], self.count, steps[0])]

    def take(self):
        steps = [order[self.level()] for order in self.orders]
        size = steps[0][1]
        if self.gathering():
            if self.level() < 2:
                for stack in range(2):
                    low = self.digit(steps[stack]) == 0
                    mine, got = self.held[stack], self.gots[stack]
                    self.held[stack] = jnp.concatenate(
                        [jnp.where(low, mine, got), jnp.where(low, got, mine)], axis=0
                    )
            else:
                first = self.held[0].shape[0]
                (got,) = self.gots
                self.held = [part.reshape(-1, part.shape[2]) for part in (got[:, :first], got[:, first:])]
            self.left -= 1
            self.gots = []
            return
        if self.level() < 2:
            for stack in range(2):
                self.rows[stack] //= 2
                offset = self.digit(steps[stack]) * self.rows[stack]
                terms = [(term, first + offset) for term, first in self.stacks[stack]]
                self.stacks[stack] = terms + [(self.gots[stack], 0)]
        elif self.whole_late:
            (got,) = self.gots
            self.stacks = [[(self.sent, skip), (got, skip)] for skip in (0, self.rows[0])]
        else:
            (got,) = self.gots
            self.rows = [rows // size for rows in self.rows]
            flat = got.reshape(-1, got.shape[2])
            for stack in range(2):
                skip = self.rows[0] * stack
                self.stacks[stack] = [(flat, sum(self.rows) * piece + skip) for piece in range(size)]
        self.taken += 1
        self.gots = []

    def last(self):
        return self.gathering() and self.left <= 1

    def last_bits(self):
        return jnp.stack([self.digit(order[0]) if order else 0 * self.place for order in self.orders])

    def parts(self):
        if self.orders[0]:
            return [self.held[0], self.gots[0], self.held[1], self.gots[1]]
        halves = []
        for held in [self.cut(stack, 0, self.rows[stack]) for stack in range(2)]:
            middle = held.shape[0] // 2
            halves += [held[:middle], held[middle:]]
        return halves


def swap(values):
    return lax.ppermute(values, "tensor", [(0, 1), (1, 0)])


def body(count, tokens, lengths, w_qkv, w_attn, w_in, w_out, gain_attn, gain_mlp, blend, cotangent):
    rows, width = tokens.shape
    blocks = rows // BLOCK

    wq_own = w_qkv.transpose(1, 0, 2)
    wq_other = swap(wq_own)
    wa_other, wi_other, wo_other = swap(w_attn), swap(w_in), swap(w_out)
    blend_other = swap(blend)
    gain_one = gain_attn.reshape(1, width)
    gain_two = gain_mlp.reshape(1, width)
    smem = pl.BlockSpec(memory_space=pltpu.SMEM)

    def row_block(size, cols):
        return pl.BlockSpec((size, cols), lambda i: (i, 0))

    own_cols = 3 * wq_own.shape[2]
    normed, own = pl.pallas_call(
        norm_project_kernel,
        grid=(4,),
        in_specs=[row_block(rows // 4, width), whole((1, width)), whole(wq_own.shape)],
        out_specs=[row_block(rows // 4, width), row_block(rows // 4, own_cols)],
        out_shape=[jax.ShapeDtypeStruct((rows, width), BF), jax.ShapeDtypeStruct((rows, own_cols), BF)],
        compiler_params=params(60),
        cost_estimate=cost(5),
        name="norm_project",
    )(tokens, gain_one, wq_own)
    normed, wi_other, wo_other, wa_other = tie(normed, wi_other, wo_other, wa_other)
    other, packet = pl.pallas_call(
        project_state_kernel,
        in_specs=[smem] + [pl.BlockSpec(memory_space=pltpu.VMEM)] * 3,
        out_shape=[
            jax.ShapeDtypeStruct((rows, own_cols), BF),
            jax.ShapeDtypeStruct((PACKET, 128), BF),
        ],
        compiler_params=params(60),
        cost_estimate=cost(5),
        name="project_state",
    )(lengths, normed, wq_other, own)
    packet = swap(packet)

    units = w_out.shape[0]
    tall = rows // 4
    parts = units // (2 * LANES)
    vmem = pl.BlockSpec(memory_space=pltpu.VMEM)
    stack_rows = units * width // LANES
    attn_rows = w_attn.shape[0] * width // LANES
    anywhere = pl.BlockSpec(memory_space=pltpu.HBM)

    kept_shapes = [
        ((blocks, 4, 128, 128), BF),
        ((blocks, HALO, 1024), BF),
        ((blocks, 4, BLOCK + HALO, 256), BF),
        ((blocks, 4, BLOCK, 256), BF),
        ((rows, width), BF),
        ((rows, width), BF),
    ]
    stored_shapes = [((rows, width), BF)] + kept_shapes + [((rows, 2 * units), BF)]
    branch, gmix, ggain_mlp, *outs = pl.pallas_call(
        partial(layer_kernel, blocks, parts),
        in_specs=[smem] * 3 + [vmem] * 4 + [anywhere] * 8,
        out_specs=[vmem] * 5 + [anywhere] * 12,
        out_shape=[
            jax.ShapeDtypeStruct((rows, width), BF),
            jax.ShapeDtypeStruct((rows, width), BF),
            jax.ShapeDtypeStruct((8, width), F32),
            jax.ShapeDtypeStruct((attn_rows, LANES), BF),
            jax.ShapeDtypeStruct((attn_rows, LANES), BF),
        ]
        + [jax.ShapeDtypeStruct(shape, kind) for shape, kind in stored_shapes]
        + [jax.ShapeDtypeStruct((stack_rows, LANES), BF)] * 4,
        scratch_shapes=[
            pltpu.VMEM((rows, own_cols), BF),
            pltpu.VMEM((rows, own_cols), BF),
            pltpu.VMEM((rows, width), BF),
            pltpu.VMEM((rows, width), BF),
            pltpu.VMEM((2,) + w_in.shape, BF),
            pltpu.VMEM((2,) + w_out.shape, BF),
        ]
        + [pltpu.VMEM(shape, kind) for shape, kind in stored_shapes]
        + [
            pltpu.VMEM((2, 2, stack_rows, LANES), BF),
            pltpu.VMEM((4, 256, 128), F32),
            pltpu.VMEM((4, 8, 128), F32),
            pltpu.VMEM((HALO, 1024), BF),
            pltpu.VMEM((rows, width), F32),
            pltpu.VMEM((rows, 128), F32),
            pltpu.VMEM((rows, width), BF),
            pltpu.VMEM((width, rows), BF),
            pltpu.VMEM((width, rows), BF),
            pltpu.VMEM((rows, width), F32),
            pltpu.SemaphoreType.DMA((64,)),
        ],
        compiler_params=params(62),
        cost_estimate=cost(30),
        name="layer",
    )(
        lengths,
        blend,
        blend_other,
        packet,
        gain_two,
        w_attn,
        wa_other,
        own,
        other,
        tokens,
        cotangent,
        w_in,
        wi_other,
        w_out,
        wo_other,
    )
    attn_grads, outs = outs[:2], outs[2:]
    mixed, *kept = outs[:7]
    active, out_own, in_own, out_sent, in_sent = outs[7:]

    feed_sum = Reduction(
        [([out_own, swap(out_sent)], 0, stack_rows), ([in_own, swap(in_sent)], 0, stack_rows)], count
    )
    wanted = len(feed_sum.orders[0])
    if wanted > 0:
        gmix, *cuts = tie(gmix, *feed_sum.cuts())
        feed_sum.send(cuts)

    steps = blocks // STEP_BLOCKS

    def back_block(*shape):
        return pl.BlockSpec(
            (shape[0] * STEP_BLOCKS,) + shape[1:], lambda i: (steps - 1 - i,) + (0,) * (len(shape) - 1)
        )

    gq, gk, gv, packet_back, gblend = pl.pallas_call(
        mixer_backward_kernel,
        grid=(steps,),
        in_specs=[
            smem,
            smem,
            smem,
            back_block(BLOCK, own_cols),
            back_block(BLOCK, own_cols),
            back_block(1, 4, 128, 128),
            back_block(1, HALO, 1024),
            back_block(1, 4, BLOCK + HALO, 256),
            back_block(1, 4, BLOCK, 256),
            back_block(BLOCK, width),
            back_block(BLOCK, width),
            back_block(BLOCK, width),
        ],
        out_specs=[back_block(BLOCK, width)] * 3 + [whole((PACKET, 128)), whole((2, 4, 8, 128))],
        out_shape=[jax.ShapeDtypeStruct((rows, width), BF)] * 3
        + [jax.ShapeDtypeStruct((PACKET, 128), BF), jax.ShapeDtypeStruct((2, 4, 8, 128), F32)],
        scratch_shapes=[
            pltpu.VMEM((HALO, 1024), F32),
            pltpu.VMEM((4, 256, 128), F32),
            pltpu.VMEM((4, 8, 128), F32),
        ],
        compiler_params=params(60),
        cost_estimate=cost(20),
        name="mixer_backward",
    )(lengths, blend, blend_other, own, other, *kept, gmix)
    if wanted > 1:
        (packet_back,) = feed_sum.after(packet_back)
        feed_sum.take()
    packet_got = swap(packet_back)
    if wanted > 1:
        packet_got, *cuts = tie(packet_got, *feed_sum.cuts())
        feed_sum.send(cuts)

    wq_shape = (3 * width + attn_rows + EXTRA, own_cols // 3)
    kv_cols = 2 * own_cols // 3
    gproj, wq_mine, wq_sent = pl.pallas_call(
        finish_kernel,
        in_specs=[smem] + [vmem] * 3 + [anywhere] * 11,
        out_specs=[anywhere] * 3,
        out_shape=[
            jax.ShapeDtypeStruct((rows, 2 * kv_cols), BF),
            jax.ShapeDtypeStruct(wq_shape, BF),
            jax.ShapeDtypeStruct(wq_shape, BF),
        ],
        scratch_shapes=[
            pltpu.VMEM((PACKET, 128), BF),
            pltpu.VMEM((rows, kv_cols), BF),
            pltpu.VMEM((rows, kv_cols), BF),
        ]
        + [pltpu.VMEM((rows, width), BF)] * 4
        + [pltpu.VMEM(wq_own.shape, BF)] * 2
        + [
            pltpu.VMEM((rows, 2 * kv_cols), BF),
            pltpu.VMEM(wq_shape, BF),
            pltpu.VMEM(wq_shape, BF),
            pltpu.SemaphoreType.DMA((24,)),
        ],
        compiler_params=params(60),
        cost_estimate=cost(8),
        name="finish",
    )(
        lengths,
        gblend,
        ggain_mlp,
        gain_one,
        packet_got,
        own,
        other,
        gk,
        gv,
        gq,
        normed,
        wq_own,
        wq_other,
        *attn_grads,
    )

    def layer_output(active):
        return pl.pallas_call(
            output_kernel,
            grid=(4,),
            in_specs=[row_block(tall, width), row_block(tall, width), row_block(tall, 2 * units)]
            + [whole(w_attn.shape)] * 2
            + [whole(w_out.shape)] * 2,
            out_specs=row_block(tall, width),
            out_shape=jax.ShapeDtypeStruct((rows, width), BF),
            compiler_params=params(60),
            cost_estimate=cost(5),
            name="layer_output",
        )(tokens, mixed, active, w_attn, wa_other, w_out, wo_other)

    def input_gradient(gproj):
        return pl.pallas_call(
            input_grad_kernel,
            grid=(4,),
            in_specs=[
                row_block(tall, width),
                row_block(tall, 2 * kv_cols),
                row_block(tall, width),
                row_block(tall, width),
                whole((1, width)),
                whole(wq_own.shape),
                whole(wq_own.shape),
            ],
            out_specs=row_block(tall, width),
            out_shape=jax.ShapeDtypeStruct((rows, width), BF),
            compiler_params=params(60),
            cost_estimate=cost(7),
            name="input_grad",
        )(gq, gproj, tokens, branch, gain_one, wq_own, wq_other)

    if wanted > 1:
        (wq_sent,) = feed_sum.after(wq_sent)
        feed_sum.take()
    wq_got = swap(wq_sent)
    cut = wq_got.shape[0] // 2
    wq_sum = Reduction([([wq_mine, wq_got], 0, cut), ([wq_mine, wq_got], cut, cut)], count, True)
    if wanted == 3:
        feed_cuts, wq_cuts = feed_sum.cuts(), wq_sum.cuts()
        gproj, *cuts = tie(gproj, *wq_cuts, *feed_cuts)
        wq_sum.send(cuts[: len(wq_cuts)])
        feed_sum.send(cuts[len(wq_cuts) :])
        grad_input = input_gradient(gproj)
        (grad_input,) = wq_sum.after(grad_input)
        turns = ((wq_sum,), (feed_sum, wq_sum), (feed_sum, wq_sum), (feed_sum,), (wq_sum,), (wq_sum,))
        for turn, reductions in enumerate(turns):
            if turn == len(turns) - 1:
                wq_sum.gots = list(feed_sum.after(*wq_sum.gots))
            some = []
            for reduction in reductions:
                reduction.take()
                some.append(reduction.cuts())
            active, *cuts = tie(active, *[cut for own_cuts in some for cut in own_cuts])
            for reduction, own_cuts in zip(reductions, some):
                reduction.send([cuts.pop(0) for _ in own_cuts])
            if turn == LATE_TURN:
                output = layer_output(active)
                (output,) = feed_sum.after(output)
                (output,) = wq_sum.after(output)
    else:
        grad_input, output = input_gradient(gproj), layer_output(active)
        for reduction in (feed_sum, wq_sum):
            while reduction.orders[0] and not (reduction.last() and reduction.gots and reduction.held is not None):
                if reduction.gots:
                    reduction.take()
                reduction.send(reduction.cuts())

    out_mine, out_got, in_mine, in_got = feed_sum.parts()
    bits = feed_sum.last_bits()
    feed_parts = [out_mine, in_mine, out_got, in_got]
    wo_grad, wi_grad = pl.pallas_call(
        feed_output_kernel,
        in_specs=[smem] + [anywhere] * 4,
        out_specs=[anywhere] * 2,
        out_shape=[jax.ShapeDtypeStruct(w_out.shape, F32), jax.ShapeDtypeStruct(w_in.shape, F32)],
        scratch_shapes=[pltpu.VMEM(part.shape, BF) for part in feed_parts]
        + [
            pltpu.VMEM((2, units, LANES), F32),
            pltpu.VMEM((2, width, units // 2), F32),
            pltpu.SemaphoreType.DMA((16,)),
        ],
        compiler_params=params(60),
        cost_estimate=cost(3),
        name="feed_output",
    )(bits, *feed_parts)
    if wanted > 1:
        (wi_grad,) = wq_sum.after(wi_grad)
    a_mine, a_got, b_mine, b_got = wq_sum.parts()
    wq_parts = [a_mine, b_mine, a_got, b_got]
    wq_grad, wa_grad, ggain_one, ggain_two, gblend_all = pl.pallas_call(
        last_output_kernel,
        in_specs=[smem] + [anywhere] * 4,
        out_specs=[vmem] * 5,
        out_shape=[
            jax.ShapeDtypeStruct((3 * width, own_cols // 3), F32),
            jax.ShapeDtypeStruct(w_attn.shape, F32),
            jax.ShapeDtypeStruct((1, width), F32),
            jax.ShapeDtypeStruct((1, width), F32),
            jax.ShapeDtypeStruct(blend.shape, F32),
        ],
        scratch_shapes=[pltpu.VMEM(part.shape, BF) for part in wq_parts] + [pltpu.SemaphoreType.DMA((4,))],
        compiler_params=params(60),
        cost_estimate=cost(3),
        name="last_output",
    )(bits, *wq_parts)

    return (
        output,
        grad_input,
        wq_grad.reshape(wq_own.shape).transpose(1, 0, 2),
        wa_grad,
        wi_grad,
        wo_grad,
        ggain_one.reshape(width),
        ggain_two.reshape(width),
        gblend_all,
    )


def solution(mesh):
    return jax.shard_map(
        partial(body, mesh.shape["dp"]),
        mesh=mesh,
        in_specs=(
            P(("dp", "tensor"), None),
            P("dp", None),
            P(None, None, "tensor"),
            P("tensor", None),
            P(None, "tensor"),
            P("tensor", None),
            P(),
            P(),
            P(None, "tensor"),
            P(("dp", "tensor"), None),
        ),
        out_specs=(
            P(("dp", "tensor"), None),
            P(("dp", "tensor"), None),
            P(None, None, "tensor"),
            P("tensor", None),
            P(None, "tensor"),
            P("tensor", None),
            P(),
            P(),
            P(None, "tensor"),
        ),
        check_vma=False,
    )
```

```python
from functools import partial

import jax
import jax.numpy as jnp
from jax import lax
from jax.experimental import pallas as pl
from jax.experimental.pallas import tpu as pltpu
from jax.sharding import PartitionSpec as P

BAND = 30
HALO = 32
EXTRA = 64
LATE_TURN = 2
BLOCK = 128
EPS = 1e-06
BF = jnp.bfloat16
F32 = jnp.float32
GELU_A = 0.7978845608028654
GELU_B = 0.044715


def nn(left, right):
    return lax.dot_general(left, right, (((1,), (0,)), ((), ())), preferred_element_type=F32)


def nt(left, right):
    return lax.dot_general(left, right, (((1,), (1,)), ((), ())), preferred_element_type=F32)


def tn(left, right):
    return lax.dot_general(left, right, (((0,), (0,)), ((), ())), preferred_element_type=F32)


def iota(shape, dim):
    return lax.broadcasted_iota(jnp.int32, shape, dim)


def whole(shape):
    return pl.BlockSpec(shape, lambda *_: (0,) * len(shape))


def params(mebibytes):
    return pltpu.CompilerParams(vmem_limit_bytes=mebibytes << 20)


def cost(micros):
    return pl.CostEstimate(flops=int(micros * 1e7), bytes_accessed=1 << 20, transcendentals=0)


def tie(*values):
    return lax.optimization_barrier(values)


class Copies:
    def __init__(self, sems):
        self.sems = sems
        self.used = 0

    def make(self, source, target):
        self.used += 1
        return pltpu.make_async_copy(source, target, self.sems.at[self.used - 1])


def document_ends(lengths_ref, rows):
    end = -lax.axis_index("tensor") * rows
    ends = [end]
    for doc in range(lengths_ref.shape[1]):
        end = end + lengths_ref[0, doc]
        ends.append(end)
    return ends[1:] + ends[:1]


def starts_of(ends, places):
    start = jnp.full(places.shape, ends[-1], jnp.int32)
    for end in ends[:-1]:
        start = jnp.where(places >= end, jnp.maximum(start, end), start)
    return start


def start_at(ends, place):
    start = ends[-1]
    for end in ends[:-1]:
        start = jnp.where(place >= end, jnp.maximum(start, end), start)
    return start


def norm_project_kernel(x_ref, gain_ref, w_ref, normed_ref, out_ref):
    x = x_ref[...].astype(F32)
    r = lax.rsqrt(jnp.mean(x * x, axis=1, keepdims=True) + EPS)
    normed = (x * r * gain_ref[...]).astype(BF)
    normed_ref[...] = normed
    project(normed, w_ref, out_ref)


def project(normed, w_ref, out_ref):
    cols = w_ref.shape[2]
    for kind in range(3):
        out_ref[:, cols * kind : cols * kind + cols] = nn(normed, w_ref[kind]).astype(BF)


PACKET = 4 * (128 + 16) + 8 * HALO


def packed_state(state):
    return jnp.concatenate([state[:64] + state[64:128], state[128:192] + state[192:]], axis=0).astype(BF)


def unpacked_state(packed, diag):
    one, two = packed[:64], packed[64:]
    state = jnp.concatenate([one, one, two, two], axis=0)
    return jnp.where(diag, state, jnp.zeros_like(state))


def pack(packet_ref, pair, state, total):
    base = 144 * pair
    packet_ref[base : base + 128] = packed_state(state)
    packet_ref[base + 128 : base + 144] = jnp.broadcast_to(total, (16, 128)).astype(BF)


def pack_halo(packet_ref, kind, pair, rows):
    base = 576 + HALO * (4 * kind + pair)
    packet_ref[base : base + HALO] = rows


def unpack(packet_ref, pair, diag):
    base = 144 * pair
    state = unpacked_state(packet_ref[base : base + 128].astype(F32), diag)
    return state, packet_ref[base + 128 : base + 136].astype(F32)


def unpack_halo(packet_ref, kind, pair):
    base = 576 + HALO * (4 * kind + pair)
    return packet_ref[base : base + HALO]


def first_feature(values):
    return jnp.where(values > 0, values + 1.0, jnp.exp(jnp.minimum(values, 0.0))).astype(BF)


def second_feature(values):
    return jnp.tanh(values).astype(BF)


def pair_diag(rows, cols):
    row = iota((rows, cols), 0)
    col = iota((rows, cols), 1)
    return ((row // 64) % 2) == ((col // 64) % 2)


def project_state_kernel(lengths_ref, normed_ref, w_ref, own_ref, out_ref, packet_ref):
    rows = normed_ref.shape[0]
    project(normed_ref[...], w_ref, out_ref)
    member_from = start_at(document_ends(lengths_ref, rows), rows - 1)
    member = iota((rows, 1), 0) >= member_from
    ks, vs = [heads_of(own_ref, out_ref, kind) for kind in (1, 2)]
    wide = [jnp.where(member, k.astype(F32), 0.0) for k in ks]
    ones = [jnp.where(member, first_feature(k).astype(F32), 0.0) for k in wide]
    features = each(lambda k, one: jnp.concatenate([one.astype(BF), second_feature(k)], axis=1), wide, ones)
    states = each(tn, features, vs)
    diag = pair_diag(256, 128)
    for pair in PAIRS:
        slot = (pair + 2) % 4
        pack(packet_ref, slot, jnp.where(diag, states[pair], 0.0), jnp.sum(ones[pair], axis=0, keepdims=True))
        pack_halo(packet_ref, 0, slot, ks[pair][rows - HALO :])
        pack_halo(packet_ref, 1, slot, vs[pair][rows - HALO :])


def block_masks(ends, first):
    row_places = first + iota((1, 256), 1) % BLOCK
    start_row = starts_of(ends, row_places)
    window_places = first - HALO + iota((BLOCK + HALO, 256), 0)
    banded = (window_places <= row_places) & (
        window_places >= jnp.maximum(start_row, row_places - (BAND - 1))
    )
    key_places = first + iota((BLOCK, 256), 0)
    causal = (key_places <= row_places) & (key_places >= start_row)
    col_places = first + iota((BLOCK, 1), 0)
    start_col = starts_of(ends, col_places)
    key_lane = first + iota((BLOCK, BLOCK), 1)
    causal_q = ((key_lane <= col_places) & (key_lane >= start_col)).astype(F32).astype(BF)
    count = (col_places - start_col + 1).astype(F32)
    carried = start_col < first
    member_from = start_at(ends, first + BLOCK - 1)
    member = col_places >= member_from
    keep = member_from < first
    return banded, causal, causal_q, count, carried, member, keep


def stack_heads(values):
    lane = iota(values.shape, 1) % 128
    zero = jnp.zeros_like(values)
    return jnp.concatenate(
        [jnp.where(lane < 64, values, zero), jnp.where(lane >= 64, values, zero)], axis=0
    )


def pick_heads(values):
    half = values.shape[0] // 2
    lane = iota((half, values.shape[1]), 1) % 128
    return jnp.where(lane < 64, values[:half], values[half:])


def ones_diagonal():
    return pair_diag(128, 128).astype(F32).astype(BF)


def only(mask, values):
    return jnp.where(mask, values, jnp.zeros_like(values))


def each(function, *lists):
    return [function(*values) for values in zip(*lists)]


class Front:
    def __init__(self, qs, ks, prev_ks, blends, carries, masks, ones_diag):
        banded, causal, causal_q, count, carried, member, keep = masks
        self.q_stack = each(lambda q: stack_heads(q * 0.125), qs)
        self.window = each(lambda prev, k: jnp.concatenate([prev, k], axis=0), prev_ks, ks)
        scores = each(nt, self.window, self.q_stack)
        self.k_one = each(lambda k: first_feature(k.astype(F32)), ks)
        products = each(lambda k_one: nn(causal_q, k_one), self.k_one)
        self.q_one = each(lambda q: first_feature(q.astype(F32)), qs)
        self.sums = each(lambda product, carry: product + jnp.where(carried, carry, 0.0), products, carries)
        self.total = each(
            lambda q_one, sums: nn((q_one.astype(F32) * sums).astype(BF), ones_diag), self.q_one, self.sums
        )
        self.q_two = each(lambda q: second_feature(q.astype(F32)), qs)
        self.k_both = each(
            lambda k_one, k: jnp.concatenate([k_one, second_feature(k.astype(F32))], axis=1), self.k_one, ks
        )
        scores = each(lambda score: jnp.where(banded, score, -1e30), scores)
        raised = each(lambda score: jnp.exp(score - jnp.max(score, axis=0, keepdims=True)), scores)
        self.near = each(lambda r: r * (1.0 / jnp.sum(r, axis=0, keepdims=True)), raised)
        inverse = 1.0 / count
        self.ratio_one = each(lambda blend, total: blend[0] / total, blends, self.total)
        self.ratio_two = each(lambda blend: blend[1] * inverse, blends)
        self.q_scaled = each(
            lambda q_one, q_two, one, two: jnp.concatenate(
                [(q_one.astype(F32) * one).astype(BF), (q_two.astype(F32) * two).astype(BF)], axis=1
            ),
            self.q_one,
            self.q_two,
            self.ratio_one,
            self.ratio_two,
        )
        self.s_stack = each(stack_heads, self.q_scaled)
        far = each(nt, self.k_both, self.s_stack)
        self.weights = each(
            lambda near, far: jnp.concatenate(
                [near[:HALO].astype(BF), (near[HALO:] + jnp.where(causal, far, 0.0)).astype(BF)], axis=0
            ),
            self.near,
            far,
        )


PAIRS = range(4)


def pair_lanes(pair):
    return slice(128 * pair, 128 * pair + 128)


def value_lanes(pair):
    return slice(512 + 128 * pair, 640 + 128 * pair)


def heads_of(own_ref, other_ref, kind):
    first = own_ref.shape[1] // 3 * kind
    return [
        (own_ref if pair < 2 else other_ref)[:, first + 128 * (pair % 2) : first + 128 * (pair % 2) + 128]
        for pair in PAIRS
    ]


def pair_blends(own_ref, other_ref):
    first_head = iota((1, 128), 1) < 64
    rows = []
    for pair in PAIRS:
        ref = own_ref if pair < 2 else other_ref
        head = 2 * (pair % 2)
        rows.append([jnp.where(first_head, ref[kind, head], ref[kind, head + 1]) for kind in range(2)])
    return rows


def mixer_forward_block(
    index,
    total_rows,
    lengths_ref,
    own_ref,
    other_ref,
    blend_own_ref,
    blend_other_ref,
    state_out_ref,
    prev_out_ref,
    near_ref,
    weights_ref,
    sums_ref,
    total_ref,
    state_ref,
    sum_ref,
    prev_ref,
):
    first = index * BLOCK

    masks = block_masks(document_ends(lengths_ref, total_rows), first)
    banded, causal, causal_q, count, carried, member, keep = masks
    diag = pair_diag(256, 128)
    qs, ks, vs = [heads_of(own_ref, other_ref, kind) for kind in range(3)]
    prev = prev_ref[...]
    states = [state_ref[pair] for pair in PAIRS]
    sums_in = [sum_ref[pair] for pair in PAIRS]
    blends = pair_blends(blend_own_ref, blend_other_ref)
    front = Front(
        qs,
        ks,
        [prev[:, pair_lanes(pair)] for pair in PAIRS],
        blends,
        [total[0:1] for total in sums_in],
        masks,
        ones_diagonal(),
    )
    state_low = each(lambda state: state.astype(BF), states)
    inter = each(lambda q, state: nn(only(carried, q), state), front.q_scaled, state_low)
    added = each(lambda k, v: tn(only(member, k), v), front.k_both, vs)
    outs = [
        tn(front.weights[pair], jnp.concatenate([prev[:, value_lanes(pair)], vs[pair]], axis=0))
        for pair in PAIRS
    ]
    outs = each(lambda out, term: pick_heads(out) + term, outs, inter)
    for pair in PAIRS:
        state_out_ref[0, pair] = packed_state(states[pair])
        near_ref[0, pair] = front.near[pair].astype(BF)
        weights_ref[0, pair] = front.weights[pair][HALO:]
        sums_ref[:, pair_lanes(pair)] = front.sums[pair].astype(BF)
        total_ref[:, pair_lanes(pair)] = (1.0 / front.total[pair]).astype(BF)
        state_ref[pair] = jnp.where(keep, states[pair], 0.0) + jnp.where(diag, added[pair], 0.0)
        sum_ref[pair] = jnp.broadcast_to(front.sums[pair][BLOCK - 1 : BLOCK], (8, 128))
        prev_ref[:, pair_lanes(pair)] = ks[pair][BLOCK - HALO :]
        prev_ref[:, value_lanes(pair)] = vs[pair][BLOCK - HALO :]
    prev_out_ref[0] = prev
    return jnp.concatenate(outs, axis=1).astype(BF)


def mixer_backward_block(
    index,
    total_rows,
    lengths_ref,
    blend_own_ref,
    blend_other_ref,
    own_ref,
    other_ref,
    state_ref,
    prev_ref,
    near_ref,
    weights_ref,
    sums_ref,
    total_ref,
    grad_ref,
    gq_ref,
    gk_ref,
    gv_ref,
    blend_out_ref,
    halo_ref,
    back_state_ref,
    back_sum_ref,
):
    first = index * BLOCK
    ends = document_ends(lengths_ref, total_rows)
    blends = pair_blends(blend_own_ref, blend_other_ref)
    row_places = first + iota((1, 256), 1) % BLOCK
    key_places = first + iota((BLOCK, 256), 0)
    causal = (key_places <= row_places) & (key_places >= starts_of(ends, row_places))
    causal_k = causal[:, :BLOCK].astype(F32).astype(BF)
    col_places = first + iota((BLOCK, 1), 0)
    start_col = starts_of(ends, col_places)
    inverse = 1.0 / (col_places - start_col + 1).astype(F32)
    carried = start_col < first
    member_from = start_at(ends, first + BLOCK - 1)
    member = col_places >= member_from
    keep = member_from < first
    diag = pair_diag(256, 128)
    ones_diag = ones_diagonal()
    qs, ks, vs = [heads_of(own_ref, other_ref, kind) for kind in range(3)]
    prev = prev_ref[0]
    grads = [grad_ref[:, pair_lanes(pair)] for pair in PAIRS]
    states = [unpacked_state(state_ref[0, pair], diag) for pair in PAIRS]
    backs = [back_state_ref[pair] for pair in PAIRS]
    back_sums = [back_sum_ref[pair][0:1] for pair in PAIRS]
    nears = [near_ref[0, pair] for pair in PAIRS]
    wide_ks = [k.astype(F32) for k in ks]
    wide_qs = [q.astype(F32) for q in qs]
    raised_k = [jnp.exp(jnp.minimum(k, 0.0)) for k in wide_ks]
    raised_q = [jnp.exp(jnp.minimum(q, 0.0)) for q in wide_qs]
    tanh_ks = [jnp.tanh(k) for k in wide_ks]
    tanh_qs = [jnp.tanh(q) for q in wide_qs]
    k_both = each(
        lambda k, raised, t: jnp.concatenate(
            [jnp.where(k > 0, k + 1.0, raised).astype(BF), t.astype(BF)], axis=1
        ),
        wide_ks,
        raised_k,
        tanh_ks,
    )
    q_one = each(lambda q, raised: jnp.where(q > 0, q + 1.0, raised).astype(BF).astype(F32), wide_qs, raised_q)
    inverse_total = [total_ref[:, pair_lanes(pair)].astype(F32) for pair in PAIRS]
    ratio_one = each(lambda blend, total: blend[0] * total, blends, inverse_total)
    ratio_two = [blend[1] * inverse for blend in blends]
    q_scaled = each(
        lambda one, ratio, t, other: jnp.concatenate(
            [(one * ratio).astype(BF), (t.astype(BF).astype(F32) * other).astype(BF)], axis=1
        ),
        q_one,
        ratio_one,
        tanh_qs,
        ratio_two,
    )
    g_stack = each(stack_heads, grads)
    v_window = [jnp.concatenate([prev[:, value_lanes(pair)], vs[pair]], axis=0) for pair in PAIRS]
    grad_weights = each(nt, v_window, g_stack)
    dv = [
        nn(jnp.concatenate([nears[pair][:HALO], weights_ref[0, pair]], axis=0), g_stack[pair]) for pair in PAIRS
    ]
    up_inter = each(lambda grad, state: nt(only(carried, grad), state), grads, states)
    far = each(lambda gw: jnp.where(causal, gw[HALO:], 0.0).astype(BF), grad_weights)
    up = each(tn, far, k_both)
    s_stack = each(stack_heads, q_scaled)
    dfeat = each(nn, far, s_stack)
    near_wide = each(lambda near: near.astype(F32), nears)
    inner = each(lambda near, gw: near * gw, near_wide, grad_weights)
    dscores = each(
        lambda near, inner: (inner - near * jnp.sum(inner, axis=0, keepdims=True)).astype(BF),
        near_wide,
        inner,
    )
    up = each(lambda up, inter: pick_heads(up) + inter, up, up_inter)
    mean_one = each(
        lambda q, up, total: nn((q * up[:, :128]).astype(BF), ones_diag) * total,
        q_one,
        up,
        inverse_total,
    )
    window = [jnp.concatenate([prev[:, pair_lanes(pair)], ks[pair]], axis=0) for pair in PAIRS]
    q_stack = each(lambda q: stack_heads(q * 0.125), qs)
    gq_near = each(tn, dscores, window)
    dk = each(nn, dscores, q_stack)
    back_low = each(lambda back: back.astype(BF), backs)
    dv_far = each(lambda k, back: nn(only(member, k), back), k_both, back_low)
    dfeat_far = each(lambda v, back: nt(only(member, v), back), vs, back_low)
    added = each(lambda q, grad: tn(only(carried, q), grad), q_scaled, grads)
    weighted = each(lambda mean, q: (mean * q[:, :128].astype(F32)).astype(BF), mean_one, q_scaled)
    mean_back = each(lambda weight: nn(causal_k, weight), weighted)
    for pair in PAIRS:
        lanes, values = pair_lanes(pair), value_lanes(pair)
        up_one, up_two = up[pair][:, :128], up[pair][:, 128:]
        tanh_q, slope_q = tanh_qs[pair], raised_q[pair]
        up_two = up_two * inverse
        grad_one = ratio_one[pair] * (up_one - mean_one[pair] * sums_ref[:, lanes].astype(F32))
        grad_two = blends[pair][1] * up_two
        gq = pick_heads(gq_near[pair]) * 0.125 + grad_one * slope_q + grad_two * (1.0 - tanh_q * tanh_q)
        gq_ref[:, lanes] = gq.astype(BF)
        blend_out_ref[0, pair] += jnp.broadcast_to(
            jnp.sum(mean_one[pair], axis=0, keepdims=True) / 64.0, (8, 128)
        )
        blend_out_ref[1, pair] += jnp.broadcast_to(jnp.sum(tanh_q * up_two, axis=0, keepdims=True), (8, 128))
        dv_own = dv[pair][HALO:] + dv_far[pair]
        dfeat_all = dfeat[pair] + dfeat_far[pair]
        d_one = dfeat_all[:, :128] - mean_back[pair] - jnp.where(member, back_sums[pair], 0.0)
        d_two = dfeat_all[:, 128:]
        tanh_k, slope_k = tanh_ks[pair], raised_k[pair]
        gk = dk[pair][HALO:] + d_one * slope_k + d_two * (1.0 - tanh_k * tanh_k)
        gk_ref[: BLOCK - HALO, lanes] = gk[: BLOCK - HALO].astype(BF)
        gk_ref[BLOCK - HALO :, lanes] = (gk[BLOCK - HALO :] + halo_ref[:, lanes]).astype(BF)
        gv_ref[: BLOCK - HALO, lanes] = dv_own[: BLOCK - HALO].astype(BF)
        gv_ref[BLOCK - HALO :, lanes] = (dv_own[BLOCK - HALO :] + halo_ref[:, values]).astype(BF)
        halo_ref[:, lanes] = dk[pair][:HALO]
        halo_ref[:, values] = dv[pair][:HALO]
        back_state_ref[pair] = jnp.where(keep, backs[pair], 0.0) + jnp.where(diag, added[pair], 0.0)
        added_sum = jnp.sum(only(carried, weighted[pair].astype(F32)), axis=0, keepdims=True)
        back_sum_ref[pair] = jnp.broadcast_to(
            jnp.where(keep, back_sums[pair], 0.0) + added_sum, (8, 128)
        )


STEP_BLOCKS = 2


def mixer_backward_kernel(lengths_ref, blend_own_ref, blend_other_ref, *refs):
    inputs, outputs = refs[:9], refs[9:12]
    packet_ref, blend_out_ref, halo_ref, back_state_ref, back_sum_ref = refs[12:]
    step = pl.program_id(0)
    steps = pl.num_programs(0)

    @pl.when(step == 0)
    def _():
        for ref in (halo_ref, back_state_ref, back_sum_ref, blend_out_ref):
            ref[...] = jnp.zeros_like(ref)

    for sub in reversed(range(STEP_BLOCKS)):
        views = []
        for ref in inputs + outputs:
            unit = ref.shape[0] // STEP_BLOCKS
            views.append(ref.at[sub * unit : sub * unit + unit])
        mixer_backward_block(
            (steps - 1 - step) * STEP_BLOCKS + sub,
            steps * STEP_BLOCKS * BLOCK,
            lengths_ref,
            blend_own_ref,
            blend_other_ref,
            *views,
            blend_out_ref,
            halo_ref,
            back_state_ref,
            back_sum_ref,
        )

    @pl.when(step == steps - 1)
    def _():
        for pair in PAIRS:
            slot = (pair + 2) % 4
            pack(packet_ref, slot, back_state_ref[pair], back_sum_ref[pair][0:1])
            pack_halo(packet_ref, 0, slot, halo_ref[:, pair_lanes(pair)].astype(BF))
            pack_halo(packet_ref, 1, slot, halo_ref[:, value_lanes(pair)].astype(BF))


LANES = 256


def layer_kernel(
    blocks,
    parts,
    lengths_ref,
    blend_own_ref,
    blend_other_ref,
    packet_ref,
    gain_ref,
    wa_own_ref,
    wa_other_ref,
    own_hbm,
    other_hbm,
    x_hbm,
    cot_hbm,
    wi_own_hbm,
    wi_other_hbm,
    wo_own_hbm,
    wo_other_hbm,
    branch_ref,
    gmix_ref,
    ggain_ref,
    attn_own_ref,
    attn_sent_ref,
    mixed_hbm,
    state_hbm,
    prev_hbm,
    near_hbm,
    weights_hbm,
    sums_hbm,
    total_hbm,
    active_hbm,
    out_own_hbm,
    in_own_hbm,
    out_sent_hbm,
    in_sent_hbm,
    own_ref,
    other_ref,
    x_ref,
    grad_ref,
    wi_ref,
    wo_ref,
    mixed_ref,
    state_out_ref,
    prev_out_ref,
    near_ref,
    weights_ref,
    sums_ref,
    total_ref,
    active_ref,
    stack_ref,
    state_ref,
    sum_ref,
    prev_ref,
    y_ref,
    r_ref,
    normed_ref,
    normed_turned_ref,
    grad_turned_ref,
    back_ref,
    sems,
):
    copies = Copies(sems)
    rows, width = x_ref.shape
    heads = wa_own_ref.shape[0]
    units = wo_ref.shape[1]
    chunk_units = units // parts
    tokens = ((own_hbm, own_ref), (other_hbm, other_ref), (x_hbm, x_ref), (cot_hbm, grad_ref))
    first_loads = [copies.make(source.at[:BLOCK], target.at[:BLOCK]) for source, target in tokens]
    later_loads = [copies.make(source.at[BLOCK:], target.at[BLOCK:]) for source, target in tokens]
    weight_loads = [
        copies.make(source, target)
        for source, target in (
            (wi_own_hbm, wi_ref.at[0]),
            (wo_own_hbm, wo_ref.at[0]),
            (wi_other_hbm, wi_ref.at[1]),
            (wo_other_hbm, wo_ref.at[1]),
        )
    ]
    for load in first_loads + later_loads + weight_loads:
        load.start()
    for pair in PAIRS:
        state_ref[pair], sum_ref[pair] = unpack(packet_ref, pair, pair_diag(256, 128))
        prev_ref[:, pair_lanes(pair)] = unpack_halo(packet_ref, 0, pair)
        prev_ref[:, value_lanes(pair)] = unpack_halo(packet_ref, 1, pair)
    back_ref[...] = jnp.zeros_like(back_ref)
    for load in first_loads:
        load.wait()

    def block(step, _):
        @pl.when(step == 1)
        def _():
            for load in later_loads:
                load.wait()

        here = pl.ds(pl.multiple_of(step * BLOCK, BLOCK), BLOCK)
        only_here = pl.ds(step, 1)
        mixed = mixer_forward_block(
            step,
            rows,
            lengths_ref,
            own_ref.at[here],
            other_ref.at[here],
            blend_own_ref,
            blend_other_ref,
            state_out_ref.at[only_here],
            prev_out_ref.at[only_here],
            near_ref.at[only_here],
            weights_ref.at[only_here],
            sums_ref.at[here],
            total_ref.at[here],
            state_ref,
            sum_ref,
            prev_ref,
        )
        mixed_ref[here, :] = mixed
        hidden = x_ref[here, :].astype(F32)
        hidden = hidden + nn(mixed[:, :heads], wa_own_ref[...]) + nn(mixed[:, heads:], wa_other_ref[...])
        r = lax.rsqrt(jnp.mean(hidden * hidden, axis=1, keepdims=True) + EPS)
        y = hidden * r
        y_ref[here, :] = y
        r_ref[here, :] = jnp.broadcast_to(r, (BLOCK, r_ref.shape[1]))
        normed = (y * gain_ref[...]).astype(BF)
        normed_ref[here, :] = normed
        normed_turned_ref[:, here] = normed.T
        grad_turned_ref[:, here] = grad_ref[here, :].T
        return 0

    def some_blocks(step, _):
        for sub in range(STEP_BLOCKS):
            block(step * STEP_BLOCKS + sub, 0)
        return 0

    lax.fori_loop(0, blocks // STEP_BLOCKS, some_blocks, 0)
    stores = [
        copies.make(source, target)
        for source, target in (
            (mixed_ref, mixed_hbm),
            (state_out_ref, state_hbm),
            (prev_out_ref, prev_hbm),
            (near_ref, near_hbm),
            (weights_ref, weights_hbm),
            (sums_ref, sums_hbm),
            (total_ref, total_hbm),
        )
    ]
    for store in stores:
        store.start()
    for load in weight_loads:
        load.wait()
    chunk_stores = []
    for late in range(2 * parts):
        half, place = late // parts, late % parts
        out_target, in_target = ((out_own_hbm, in_own_hbm), (out_sent_hbm, in_sent_hbm))[half]
        spots = [(0, out_target, units * side + chunk_units * place, chunk_units) for side in range(width // LANES)]
        count = width * chunk_units // LANES
        spots.append((1, in_target, count * place, count))
        columns = pl.ds(late * chunk_units, chunk_units)
        chunk_stores.append(
            [
                copies.make(stack_ref.at[half, kind, pl.ds(row, count), :], target.at[pl.ds(row, count), :])
                for kind, target, row, count in spots
            ]
            + [copies.make(active_ref.at[:, columns], active_hbm.at[:, columns])]
        )

    def chunk(late, _):
        half, place = late // parts, late % parts
        normed = normed_ref[...]
        grad = grad_ref[...]
        first = pl.multiple_of(place * chunk_units, chunk_units)
        wi = wi_ref[half, :, pl.ds(first, chunk_units)]
        wo = wo_ref[half, pl.ds(first, chunk_units), :]
        spans = [slice(LANES * piece, LANES * piece + LANES) for piece in range(chunk_units // LANES)]
        us = [nn(normed, wi[:, span]) for span in spans]
        gacts = [nt(grad, wo[span, :]) for span in spans]
        gpres = []
        for piece in range(len(spans)):
            u = us[piece]
            square = u * u
            t = jnp.tanh(u * (GELU_A + (GELU_A * GELU_B) * square))
            gate = 0.5 + 0.5 * t
            active = (u * gate).astype(BF)
            column = pl.multiple_of(late * chunk_units + LANES * piece, LANES)
            active_ref[:, pl.ds(column, LANES)] = active
            slope = gate + (u * (0.5 - 0.5 * t * t)) * (GELU_A + (3.0 * GELU_A * GELU_B) * square)
            gpre = (gacts[piece] * slope).astype(BF)
            gpres.append(gpre)
            gout = nn(grad_turned_ref[...], active).astype(BF).T
            spot = len(spans) * place + piece
            for side in range(width // LANES):
                row = pl.multiple_of(units * side + LANES * spot, LANES)
                stack_ref[half, 0, pl.ds(row, LANES), :] = gout[:, LANES * side : LANES * side + LANES]
            row = pl.multiple_of(width * spot, LANES)
            stack_ref[half, 1, pl.ds(row, width), :] = nn(normed_turned_ref[...], gpre).astype(BF)
        back_ref[...] += nt(jnp.concatenate(gpres, axis=1), wi)
        for number, some in enumerate(chunk_stores):

            @pl.when(late == number)
            def _(some=some):
                for store in some:
                    store.start()

        return 0

    lax.fori_loop(0, 2 * parts, chunk, 0)
    back, y = back_ref[...], y_ref[...]
    scaled = back * gain_ref[...]
    mean = jnp.mean(scaled * y, axis=1, keepdims=True)
    ghid = grad_ref[...].astype(F32) + r_ref[:, :1] * (scaled - y * mean)
    branch = ghid.astype(BF)
    branch_ref[...] = branch
    gmix_ref[:, :heads] = nt(branch, wa_own_ref[...]).astype(BF)
    gmix_ref[:, heads:] = nt(branch, wa_other_ref[...]).astype(BF)
    ggain_ref[...] = jnp.broadcast_to(jnp.sum(back * y, axis=0, keepdims=True), ggain_ref.shape)
    gattn = tn(mixed_ref[...], branch).astype(BF)
    for half, ref in enumerate((attn_own_ref, attn_sent_ref)):
        for side in range(width // LANES):
            lanes = slice(LANES * side, LANES * side + LANES)
            ref[heads * side : heads * side + heads] = gattn[heads * half : heads * half + heads, lanes]
    for store in stores + [store for some in chunk_stores for store in some]:
        store.wait()


def output_kernel(x_ref, mixed_ref, active_ref, wa_own_ref, wa_other_ref, wo_own_ref, wo_other_ref, out_ref):
    heads = wa_own_ref.shape[0]
    units = wo_own_ref.shape[0]
    total = x_ref[...].astype(F32)
    total = total + (nn(mixed_ref[:, :heads], wa_own_ref[...]) + nn(mixed_ref[:, heads:], wa_other_ref[...]))
    total = total + (nn(active_ref[:, :units], wo_own_ref[...]) + nn(active_ref[:, units:], wo_other_ref[...]))
    out_ref[...] = total.astype(BF)


def finish_kernel(
    lengths_ref,
    gblend_ref,
    ggain_ref,
    gain_ref,
    packet_hbm,
    own_hbm,
    other_hbm,
    gk_hbm,
    gv_hbm,
    gq_hbm,
    normed_hbm,
    w_own_hbm,
    w_other_hbm,
    attn_own_hbm,
    attn_sent_hbm,
    gkv_hbm,
    wgrad_own_hbm,
    wgrad_sent_hbm,
    packet_ref,
    own_ref,
    other_ref,
    gk_ref,
    gv_ref,
    gq_ref,
    normed_ref,
    w_own_ref,
    w_other_ref,
    gkv_ref,
    wgrad_own_ref,
    wgrad_sent_ref,
    sems,
):
    copies = Copies(sems)
    rows, width = normed_ref.shape
    cols = w_own_ref.shape[2]
    wgrads = (wgrad_own_ref, wgrad_sent_ref)
    attn_rows = attn_own_hbm.shape[0]
    keys_values = slice(cols, 3 * cols)
    loads = [
        copies.make(source, target)
        for source, target in (
            (packet_hbm, packet_ref),
            (own_hbm.at[:, keys_values], own_ref),
            (gk_hbm, gk_ref),
            (gv_hbm, gv_ref),
            (other_hbm.at[:, keys_values], other_ref),
            (normed_hbm, normed_ref),
            (gq_hbm, gq_ref),
            (w_own_hbm, w_own_ref),
            (w_other_hbm, w_other_ref),
            (attn_own_hbm, wgrad_own_ref.at[3 * width : 3 * width + attn_rows]),
            (attn_sent_hbm, wgrad_sent_ref.at[3 * width : 3 * width + attn_rows]),
        )
    ]
    gkv_stores, wgrad_stores = [], []
    for half, target in enumerate((wgrad_own_hbm, wgrad_sent_hbm)):
        lanes = slice(2 * cols * half, 2 * cols * half + 2 * cols)
        gkv_stores.append(copies.make(gkv_ref.at[:, lanes], gkv_hbm.at[:, lanes]))
        spans = [slice(width * kind, width * kind + width) for kind in range(3)]
        spans.append(slice(3 * width, wgrads[half].shape[0]))
        wgrad_stores.append([copies.make(wgrads[half].at[span], target.at[span]) for span in spans])
    for load in loads:
        load.start()
    live = lax.axis_index("tensor") == 0
    member_from = start_at(document_ends(lengths_ref, rows), rows - 1)
    member = (iota((rows, 1), 0) >= member_from) & live
    diag = pair_diag(256, 128)
    cut = rows - HALO
    for load in loads[:4]:
        load.wait()
    for pair in PAIRS:
        if pair == 2:
            loads[4].wait()
        src = own_ref if pair < 2 else other_ref
        col = 128 * (pair % 2)
        lanes = pair_lanes(pair)
        k = src[:, col : col + 128].astype(F32)
        v = src[:, cols + col : cols + col + 128]
        back, back_sum = unpack(packet_ref, pair, diag)
        back, back_sum = back.astype(BF), back_sum[0:1]
        t = jnp.tanh(k)
        raised = jnp.exp(jnp.minimum(k, 0.0))
        k_both = jnp.concatenate([jnp.where(k > 0, k + 1.0, raised).astype(BF), t.astype(BF)], axis=1)
        dfeat = nt(v, back)
        extra_k = (dfeat[:, :128] - back_sum) * raised + dfeat[:, 128:] * (1.0 - t * t)
        extra_v = nn(k_both, back)
        for kind, (grad_ref, extra) in enumerate(((gk_ref, extra_k), (gv_ref, extra_v))):
            grad = grad_ref[:, lanes].astype(F32) + jnp.where(member, extra, 0.0)
            halo = jnp.where(live, unpack_halo(packet_ref, kind, pair).astype(F32), 0.0)
            base = cols * (2 * (pair // 2) + kind) + col
            gkv_ref[:cut, base : base + 128] = grad[:cut].astype(BF)
            gkv_ref[cut:, base : base + 128] = (grad[cut:] + halo).astype(BF)
        if pair % 2 == 1:
            gkv_stores[pair // 2].start()
    for load in loads[5:]:
        load.wait()
    normed = normed_ref[...].T
    ones = jnp.ones((1, cols), BF)
    gain_grad = jnp.zeros((1, width), F32)
    for half, (wgrad_ref, w_ref) in enumerate(zip(wgrads, (w_own_ref, w_other_ref))):
        for kind in range(3):
            if kind == 0:
                grad = gq_ref[:, cols * half : cols * half + cols]
            else:
                first = cols * (2 * half + kind - 1)
                grad = gkv_ref[:, first : first + cols]
            wgrad = nn(normed, grad)
            wgrad_ref[width * kind : width * kind + width] = wgrad.astype(BF)
            wgrad_stores[half][kind].start()
            products = wgrad * w_ref[kind].astype(F32)
            high = products.astype(BF)
            low = (products - high.astype(F32)).astype(BF)
            gain_grad = gain_grad + nt(ones, high) + nt(ones, low)
    gain_grad = gain_grad / gain_ref[...]
    for half, wgrad_ref in enumerate(wgrads):
        blends = [
            jnp.concatenate([gblend_ref[kind, 2 * half + pair][0:1] for pair in range(2)], axis=1)
            for kind in range(2)
        ]
        gains = [gain_grad[:, :256], gain_grad[:, 256:], ggain_ref[0:1, :256], ggain_ref[0:1, 256:]]
        extra = jnp.concatenate(blends + gains + [jnp.zeros((10, 256), F32)], axis=0)
        base = 3 * width + attn_rows
        wgrad_ref[base : base + 16] = extra.astype(BF)
        wgrad_ref[base + 16 :] = jnp.zeros((EXTRA - 16, 256), BF)
        wgrad_stores[half][3].start()
    for store in gkv_stores + wgrad_stores[0] + wgrad_stores[1]:
        store.wait()


def input_grad_kernel(gq_ref, gkv_ref, x_ref, branch_ref, gain_ref, w_own_ref, w_other_ref, out_ref):
    cols = w_own_ref.shape[2]
    gnormed = None
    for half, w_ref in enumerate((w_own_ref, w_other_ref)):
        for kind in range(3):
            if kind == 0:
                grad = gq_ref[:, cols * half : cols * half + cols]
            else:
                first = cols * (2 * half + kind - 1)
                grad = gkv_ref[:, first : first + cols]
            term = nt(grad, w_ref[kind])
            gnormed = term if gnormed is None else gnormed + term
    x = x_ref[...].astype(F32)
    r = lax.rsqrt(jnp.mean(x * x, axis=1, keepdims=True) + EPS)
    y = x * r
    scaled = gnormed * gain_ref[...]
    grad = branch_ref[...].astype(F32) + r * (scaled - y * jnp.mean(scaled * y, axis=1, keepdims=True))
    out_ref[...] = grad.astype(BF)


def merged(low, mine, got):
    return jnp.where(low, mine, got), jnp.where(low, got, mine)


def put_rows(ref, first_row, lane, parts, first, count):
    rows = parts[0].shape[0]
    lanes = parts[0].shape[1]
    for place, part in enumerate(parts):
        low, high = max(first, rows * place), min(first + count, rows * place + rows)
        if low < high:
            values = part[low - rows * place : high - rows * place].astype(F32)
            ref[first_row + low - first : first_row + high - first, lane : lane + lanes] = values


def feed_output_kernel(
    bits_ref,
    out_mine_hbm,
    in_mine_hbm,
    out_got_hbm,
    in_got_hbm,
    wo_hbm,
    wi_hbm,
    out_mine_ref,
    in_mine_ref,
    out_got_ref,
    in_got_ref,
    wo_ref,
    wi_ref,
    sems,
):
    copies = Copies(sems)
    parts = ((out_mine_ref, in_mine_ref), (out_got_ref, in_got_ref))
    loads = [
        copies.make(source, target)
        for source, target in (
            (out_mine_hbm, out_mine_ref),
            (in_mine_hbm, in_mine_ref),
            (out_got_hbm, out_got_ref),
            (in_got_hbm, in_got_ref),
        )
    ]
    for load in loads:
        load.start()
    units, wide = wo_ref.shape[1], wo_ref.shape[2]
    width, span = wi_ref.shape[1], wi_ref.shape[2]
    middle = units // 2
    stores = []
    for place, (out_part_ref, in_part_ref) in enumerate(parts):
        wo_first = bits_ref[0] if place == 0 else 1 - bits_ref[0]
        wi_first = bits_ref[1] if place == 0 else 1 - bits_ref[1]
        loads[2 * place].wait()
        wo_ref[place] = out_part_ref[...].astype(F32)
        column = pl.multiple_of(wo_first * wide, LANES)
        for rows in (slice(0, middle), slice(middle, units)):
            stores.append(copies.make(wo_ref.at[place, rows], wo_hbm.at[rows, pl.ds(column, wide)]))
            stores[-1].start()
        loads[2 * place + 1].wait()
        for side in range(span // LANES):
            lanes = slice(LANES * side, LANES * side + LANES)
            wi_ref[place, :, lanes] = in_part_ref[width * side : width * side + width].astype(F32)
            column = pl.multiple_of(wi_first * span + LANES * side, LANES)
            stores.append(copies.make(wi_ref.at[place, :, lanes], wi_hbm.at[:, pl.ds(column, LANES)]))
            stores[-1].start()
    for store in stores:
        store.wait()


def last_output_kernel(
    bits_ref,
    a_mine_hbm,
    b_mine_hbm,
    a_got_hbm,
    b_got_hbm,
    wq_ref,
    wa_ref,
    gain_one_ref,
    gain_two_ref,
    blend_ref,
    a_mine_ref,
    b_mine_ref,
    a_got_ref,
    b_got_ref,
    sems,
):
    copies = Copies(sems)
    loads = [
        copies.make(source, target)
        for source, target in (
            (a_mine_hbm, a_mine_ref),
            (b_mine_hbm, b_mine_ref),
            (a_got_hbm, a_got_ref),
            (b_got_hbm, b_got_ref),
        )
    ]
    for load in loads:
        load.start()
    for load in loads:
        load.wait()
    heads, width = wa_ref.shape
    parts = merged(bits_ref[0] == 0, a_mine_ref[...], a_got_ref[...])
    parts += merged(bits_ref[1] == 0, b_mine_ref[...], b_got_ref[...])
    rows = a_mine_ref.shape[0]
    put_rows(wq_ref, 0, 0, parts, 0, 3 * width)
    for side in range(width // LANES):
        put_rows(wa_ref, 0, LANES * side, parts, 3 * width + heads * side, heads)
    rest = parts[3][rows - EXTRA : rows - EXTRA + 16].astype(F32)
    gain_one_ref[...] = jnp.concatenate([rest[2:3], rest[3:4]], axis=1)
    gain_two_ref[...] = jnp.concatenate([rest[4:5], rest[5:6]], axis=1)
    sums = [jnp.sum(rest[:2, 64 * head : 64 * head + 64], axis=1, keepdims=True) for head in range(4)]
    blend_ref[...] = jnp.concatenate(sums, axis=1)


def steps_of(count, late_sizes):
    steps = []
    stride = 1
    while stride < count:
        left = count // stride
        size = next(size for size in ((2,) if len(steps) < 2 else late_sizes) if left % size == 0)
        steps.append((stride, size))
        stride *= size
    return steps


def flip(values, count, step):
    stride, _ = step
    pairs = [(src, src + stride * (1 - 2 * ((src // stride) % 2))) for src in range(count)]
    return lax.ppermute(values, "dp", pairs)


def trade(values, count, step):
    stride, size = step
    groups = [
        [first + stride * digit for digit in range(size)]
        for first in range(count)
        if (first // stride) % size == 0
    ]
    return lax.all_to_all(
        values, "dp", split_axis=0, concat_axis=0, axis_index_groups=groups, tiled=True
    )


class Reduction:
    def __init__(self, stacks, count, whole_late=False):
        self.stacks = [[(term, first) for term in terms] for terms, first, _ in stacks]
        self.rows = [rows for _, _, rows in stacks]
        self.count = count
        steps = steps_of(count, (2,) if whole_late else (4, 2))
        self.orders = [steps, steps[1::-1] + steps[2:]]
        self.whole_late = whole_late
        self.left = min(2, len(steps)) if whole_late else len(steps)
        self.taken = 0
        self.place = lax.axis_index("dp")
        self.held = None
        self.gots = []

    def digit(self, step):
        return (self.place // step[0]) % step[1]

    def cut(self, stack, first, rows):
        total = None
        for term, offset in self.stacks[stack]:
            part = lax.dynamic_slice_in_dim(term, offset + first, rows, 0).astype(F32)
            total = part if total is None else total + part
        return total.astype(BF)

    def after(self, *tokens):
        count = len(self.gots)
        tied = tie(*self.gots, *tokens)
        self.gots = list(tied[:count])
        return tied[count:]

    def gathering(self):
        return self.taken == len(self.orders[0])

    def level(self):
        return self.left - 1 if self.gathering() else self.taken

    def cuts(self):
        if self.gathering():
            if self.held is None:
                self.held = [self.cut(stack, 0, self.rows[stack]) for stack in range(2)]
            if self.level() < 2:
                return list(self.held)
            both = jnp.concatenate(self.held, axis=0)
            return [jnp.broadcast_to(both[None], (self.orders[0][self.level()][1],) + both.shape)]
        if self.level() < 2:
            cuts = []
            for stack in range(2):
                step = self.orders[stack][self.level()]
                rows = self.rows[stack] // 2
                cuts.append(self.cut(stack, (1 - self.digit(step)) * rows, rows))
            return cuts
        size = self.orders[0][self.level()][1]
        wholes = [self.cut(stack, 0, self.rows[stack]) for stack in range(2)]
        if self.whole_late:
            self.sent = jnp.concatenate(wholes, axis=0)
            return [self.sent]
        return [jnp.concatenate([part.reshape(size, -1, part.shape[1]) for part in wholes], axis=1)]

    def send(self, cuts):
        steps = [order[self.level()] for order in self.orders]
        if self.level() < 2:
            self.gots = [flip(cut, self.count, step) for cut, step in zip(cuts, steps)]
        elif self.whole_late:
            self.sent = cuts[0]
            self.gots = [flip(cuts[0], self.count, steps[0])]
        else:
            self.gots = [trade(cuts[0], self.count, steps[0])]

    def take(self):
        steps = [order[self.level()] for order in self.orders]
        size = steps[0][1]
        if self.gathering():
            if self.level() < 2:
                for stack in range(2):
                    low = self.digit(steps[stack]) == 0
                    mine, got = self.held[stack], self.gots[stack]
                    self.held[stack] = jnp.concatenate(
                        [jnp.where(low, mine, got), jnp.where(low, got, mine)], axis=0
                    )
            else:
                first = self.held[0].shape[0]
                (got,) = self.gots
                self.held = [part.reshape(-1, part.shape[2]) for part in (got[:, :first], got[:, first:])]
            self.left -= 1
            self.gots = []
            return
        if self.level() < 2:
            for stack in range(2):
                self.rows[stack] //= 2
                offset = self.digit(steps[stack]) * self.rows[stack]
                terms = [(term, first + offset) for term, first in self.stacks[stack]]
                self.stacks[stack] = terms + [(self.gots[stack], 0)]
        elif self.whole_late:
            (got,) = self.gots
            self.stacks = [[(self.sent, skip), (got, skip)] for skip in (0, self.rows[0])]
        else:
            (got,) = self.gots
            self.rows = [rows // size for rows in self.rows]
            flat = got.reshape(-1, got.shape[2])
            for stack in range(2):
                skip = self.rows[0] * stack
                self.stacks[stack] = [(flat, sum(self.rows) * piece + skip) for piece in range(size)]
        self.taken += 1
        self.gots = []

    def last(self):
        return self.gathering() and self.left <= 1

    def last_bits(self):
        return jnp.stack([self.digit(order[0]) if order else 0 * self.place for order in self.orders])

    def parts(self):
        if self.orders[0]:
            return [self.held[0], self.gots[0], self.held[1], self.gots[1]]
        halves = []
        for held in [self.cut(stack, 0, self.rows[stack]) for stack in range(2)]:
            middle = held.shape[0] // 2
            halves += [held[:middle], held[middle:]]
        return halves


def swap(values):
    return lax.ppermute(values, "tensor", [(0, 1), (1, 0)])


def body(count, tokens, lengths, w_qkv, w_attn, w_in, w_out, gain_attn, gain_mlp, blend, cotangent):
    rows, width = tokens.shape
    blocks = rows // BLOCK

    wq_own = w_qkv.transpose(1, 0, 2)
    wq_other = swap(wq_own)
    wa_other, wi_other, wo_other = swap(w_attn), swap(w_in), swap(w_out)
    blend_other = swap(blend)
    gain_one = gain_attn.reshape(1, width)
    gain_two = gain_mlp.reshape(1, width)
    smem = pl.BlockSpec(memory_space=pltpu.SMEM)

    def row_block(size, cols):
        return pl.BlockSpec((size, cols), lambda i: (i, 0))

    own_cols = 3 * wq_own.shape[2]
    normed, own = pl.pallas_call(
        norm_project_kernel,
        grid=(4,),
        in_specs=[row_block(rows // 4, width), whole((1, width)), whole(wq_own.shape)],
        out_specs=[row_block(rows // 4, width), row_block(rows // 4, own_cols)],
        out_shape=[jax.ShapeDtypeStruct((rows, width), BF), jax.ShapeDtypeStruct((rows, own_cols), BF)],
        compiler_params=params(60),
        cost_estimate=cost(5),
        name="norm_project",
    )(tokens, gain_one, wq_own)
    normed, wi_other, wo_other, wa_other = tie(normed, wi_other, wo_other, wa_other)
    other, packet = pl.pallas_call(
        project_state_kernel,
        in_specs=[smem] + [pl.BlockSpec(memory_space=pltpu.VMEM)] * 3,
        out_shape=[
            jax.ShapeDtypeStruct((rows, own_cols), BF),
            jax.ShapeDtypeStruct((PACKET, 128), BF),
        ],
        compiler_params=params(60),
        cost_estimate=cost(5),
        name="project_state",
    )(lengths, normed, wq_other, own)
    packet = swap(packet)

    units = w_out.shape[0]
    tall = rows // 4
    parts = units // (2 * LANES)
    vmem = pl.BlockSpec(memory_space=pltpu.VMEM)
    stack_rows = units * width // LANES
    attn_rows = w_attn.shape[0] * width // LANES
    anywhere = pl.BlockSpec(memory_space=pltpu.HBM)

    kept_shapes = [
        ((blocks, 4, 128, 128), BF),
        ((blocks, HALO, 1024), BF),
        ((blocks, 4, BLOCK + HALO, 256), BF),
        ((blocks, 4, BLOCK, 256), BF),
        ((rows, width), BF),
        ((rows, width), BF),
    ]
    stored_shapes = [((rows, width), BF)] + kept_shapes + [((rows, 2 * units), BF)]
    branch, gmix, ggain_mlp, *outs = pl.pallas_call(
        partial(layer_kernel, blocks, parts),
        in_specs=[smem] * 3 + [vmem] * 4 + [anywhere] * 8,
        out_specs=[vmem] * 5 + [anywhere] * 12,
        out_shape=[
            jax.ShapeDtypeStruct((rows, width), BF),
            jax.ShapeDtypeStruct((rows, width), BF),
            jax.ShapeDtypeStruct((8, width), F32),
            jax.ShapeDtypeStruct((attn_rows, LANES), BF),
            jax.ShapeDtypeStruct((attn_rows, LANES), BF),
        ]
        + [jax.ShapeDtypeStruct(shape, kind) for shape, kind in stored_shapes]
        + [jax.ShapeDtypeStruct((stack_rows, LANES), BF)] * 4,
        scratch_shapes=[
            pltpu.VMEM((rows, own_cols), BF),
            pltpu.VMEM((rows, own_cols), BF),
            pltpu.VMEM((rows, width), BF),
            pltpu.VMEM((rows, width), BF),
            pltpu.VMEM((2,) + w_in.shape, BF),
            pltpu.VMEM((2,) + w_out.shape, BF),
        ]
        + [pltpu.VMEM(shape, kind) for shape, kind in stored_shapes]
        + [
            pltpu.VMEM((2, 2, stack_rows, LANES), BF),
            pltpu.VMEM((4, 256, 128), F32),
            pltpu.VMEM((4, 8, 128), F32),
            pltpu.VMEM((HALO, 1024), BF),
            pltpu.VMEM((rows, width), F32),
            pltpu.VMEM((rows, 128), F32),
            pltpu.VMEM((rows, width), BF),
            pltpu.VMEM((width, rows), BF),
            pltpu.VMEM((width, rows), BF),
            pltpu.VMEM((rows, width), F32),
            pltpu.SemaphoreType.DMA((64,)),
        ],
        compiler_params=params(62),
        cost_estimate=cost(30),
        name="layer",
    )(
        lengths,
        blend,
        blend_other,
        packet,
        gain_two,
        w_attn,
        wa_other,
        own,
        other,
        tokens,
        cotangent,
        w_in,
        wi_other,
        w_out,
        wo_other,
    )
    attn_grads, outs = outs[:2], outs[2:]
    mixed, *kept = outs[:7]
    active, out_own, in_own, out_sent, in_sent = outs[7:]

    feed_sum = Reduction(
        [([out_own, swap(out_sent)], 0, stack_rows), ([in_own, swap(in_sent)], 0, stack_rows)], count
    )
    wanted = len(feed_sum.orders[0])
    if wanted > 0:
        gmix, *cuts = tie(gmix, *feed_sum.cuts())
        feed_sum.send(cuts)

    steps = blocks // STEP_BLOCKS

    def back_block(*shape):
        return pl.BlockSpec(
            (shape[0] * STEP_BLOCKS,) + shape[1:], lambda i: (steps - 1 - i,) + (0,) * (len(shape) - 1)
        )

    gq, gk, gv, packet_back, gblend = pl.pallas_call(
        mixer_backward_kernel,
        grid=(steps,),
        in_specs=[
            smem,
            smem,
            smem,
            back_block(BLOCK, own_cols),
            back_block(BLOCK, own_cols),
            back_block(1, 4, 128, 128),
            back_block(1, HALO, 1024),
            back_block(1, 4, BLOCK + HALO, 256),
            back_block(1, 4, BLOCK, 256),
            back_block(BLOCK, width),
            back_block(BLOCK, width),
            back_block(BLOCK, width),
        ],
        out_specs=[back_block(BLOCK, width)] * 3 + [whole((PACKET, 128)), whole((2, 4, 8, 128))],
        out_shape=[jax.ShapeDtypeStruct((rows, width), BF)] * 3
        + [jax.ShapeDtypeStruct((PACKET, 128), BF), jax.ShapeDtypeStruct((2, 4, 8, 128), F32)],
        scratch_shapes=[
            pltpu.VMEM((HALO, 1024), F32),
            pltpu.VMEM((4, 256, 128), F32),
            pltpu.VMEM((4, 8, 128), F32),
        ],
        compiler_params=params(60),
        cost_estimate=cost(20),
        name="mixer_backward",
    )(lengths, blend, blend_other, own, other, *kept, gmix)
    if wanted > 1:
        (packet_back,) = feed_sum.after(packet_back)
        feed_sum.take()
    packet_got = swap(packet_back)
    if wanted > 1:
        packet_got, *cuts = tie(packet_got, *feed_sum.cuts())
        feed_sum.send(cuts)

    wq_shape = (3 * width + attn_rows + EXTRA, own_cols // 3)
    kv_cols = 2 * own_cols // 3
    gproj, wq_mine, wq_sent = pl.pallas_call(
        finish_kernel,
        in_specs=[smem] + [vmem] * 3 + [anywhere] * 11,
        out_specs=[anywhere] * 3,
        out_shape=[
            jax.ShapeDtypeStruct((rows, 2 * kv_cols), BF),
            jax.ShapeDtypeStruct(wq_shape, BF),
            jax.ShapeDtypeStruct(wq_shape, BF),
        ],
        scratch_shapes=[
            pltpu.VMEM((PACKET, 128), BF),
            pltpu.VMEM((rows, kv_cols), BF),
            pltpu.VMEM((rows, kv_cols), BF),
        ]
        + [pltpu.VMEM((rows, width), BF)] * 4
        + [pltpu.VMEM(wq_own.shape, BF)] * 2
        + [
            pltpu.VMEM((rows, 2 * kv_cols), BF),
            pltpu.VMEM(wq_shape, BF),
            pltpu.VMEM(wq_shape, BF),
            pltpu.SemaphoreType.DMA((24,)),
        ],
        compiler_params=params(60),
        cost_estimate=cost(8),
        name="finish",
    )(
        lengths,
        gblend,
        ggain_mlp,
        gain_one,
        packet_got,
        own,
        other,
        gk,
        gv,
        gq,
        normed,
        wq_own,
        wq_other,
        *attn_grads,
    )

    def layer_output(active):
        return pl.pallas_call(
            output_kernel,
            grid=(4,),
            in_specs=[row_block(tall, width), row_block(tall, width), row_block(tall, 2 * units)]
            + [whole(w_attn.shape)] * 2
            + [whole(w_out.shape)] * 2,
            out_specs=row_block(tall, width),
            out_shape=jax.ShapeDtypeStruct((rows, width), BF),
            compiler_params=params(60),
            cost_estimate=cost(5),
            name="layer_output",
        )(tokens, mixed, active, w_attn, wa_other, w_out, wo_other)

    def input_gradient(gproj):
        return pl.pallas_call(
            input_grad_kernel,
            grid=(4,),
            in_specs=[
                row_block(tall, width),
                row_block(tall, 2 * kv_cols),
                row_block(tall, width),
                row_block(tall, width),
                whole((1, width)),
                whole(wq_own.shape),
                whole(wq_own.shape),
            ],
            out_specs=row_block(tall, width),
            out_shape=jax.ShapeDtypeStruct((rows, width), BF),
            compiler_params=params(60),
            cost_estimate=cost(7),
            name="input_grad",
        )(gq, gproj, tokens, branch, gain_one, wq_own, wq_other)

    if wanted > 1:
        (wq_sent,) = feed_sum.after(wq_sent)
        feed_sum.take()
    wq_got = swap(wq_sent)
    cut = wq_got.shape[0] // 2
    wq_sum = Reduction([([wq_mine, wq_got], 0, cut), ([wq_mine, wq_got], cut, cut)], count, True)
    if wanted == 3:
        feed_cuts = feed_sum.cuts()
        wq_cuts = wq_sum.cuts()
        gproj, *feed_cuts = tie(gproj, *feed_cuts)
        feed_sum.send(feed_cuts)
        gproj, *wq_cuts = tie(gproj, *wq_cuts)
        wq_sum.send(wq_cuts)
        grad_input = input_gradient(gproj)
        (grad_input,) = wq_sum.after(grad_input)
        (grad_input,) = feed_sum.after(grad_input)
        turns = ((wq_sum,), (feed_sum,), (wq_sum,), (feed_sum, wq_sum), (feed_sum,), (wq_sum,), (wq_sum,))
        for turn, reductions in enumerate(turns):
            if turn == len(turns) - 1:
                wq_sum.gots = list(feed_sum.after(*wq_sum.gots))
            some = []
            for reduction in reductions:
                reduction.take()
                some.append(reduction.cuts())
            active, *cuts = tie(active, *[cut for own_cuts in some for cut in own_cuts])
            for reduction, own_cuts in zip(reductions, some):
                reduction.send([cuts.pop(0) for _ in own_cuts])
            if turn == LATE_TURN:
                output = layer_output(active)
                (output,) = feed_sum.after(output)
                (output,) = wq_sum.after(output)
    else:
        grad_input, output = input_gradient(gproj), layer_output(active)
        for reduction in (feed_sum, wq_sum):
            while reduction.orders[0] and not (reduction.last() and reduction.gots and reduction.held is not None):
                if reduction.gots:
                    reduction.take()
                reduction.send(reduction.cuts())

    out_mine, out_got, in_mine, in_got = feed_sum.parts()
    bits = feed_sum.last_bits()
    feed_parts = [out_mine, in_mine, out_got, in_got]
    wo_grad, wi_grad = pl.pallas_call(
        feed_output_kernel,
        in_specs=[smem] + [anywhere] * 4,
        out_specs=[anywhere] * 2,
        out_shape=[jax.ShapeDtypeStruct(w_out.shape, F32), jax.ShapeDtypeStruct(w_in.shape, F32)],
        scratch_shapes=[pltpu.VMEM(part.shape, BF) for part in feed_parts]
        + [
            pltpu.VMEM((2, units, LANES), F32),
            pltpu.VMEM((2, width, units // 2), F32),
            pltpu.SemaphoreType.DMA((16,)),
        ],
        compiler_params=params(60),
        cost_estimate=cost(3),
        name="feed_output",
    )(bits, *feed_parts)
    if wanted > 1:
        (wi_grad,) = wq_sum.after(wi_grad)
    a_mine, a_got, b_mine, b_got = wq_sum.parts()
    wq_parts = [a_mine, b_mine, a_got, b_got]
    wq_grad, wa_grad, ggain_one, ggain_two, gblend_all = pl.pallas_call(
        last_output_kernel,
        in_specs=[smem] + [anywhere] * 4,
        out_specs=[vmem] * 5,
        out_shape=[
            jax.ShapeDtypeStruct((3 * width, own_cols // 3), F32),
            jax.ShapeDtypeStruct(w_attn.shape, F32),
            jax.ShapeDtypeStruct((1, width), F32),
            jax.ShapeDtypeStruct((1, width), F32),
            jax.ShapeDtypeStruct(blend.shape, F32),
        ],
        scratch_shapes=[pltpu.VMEM(part.shape, BF) for part in wq_parts] + [pltpu.SemaphoreType.DMA((4,))],
        compiler_params=params(60),
        cost_estimate=cost(3),
        name="last_output",
    )(bits, *wq_parts)

    return (
        output,
        grad_input,
        wq_grad.reshape(wq_own.shape).transpose(1, 0, 2),
        wa_grad,
        wi_grad,
        wo_grad,
        ggain_one.reshape(width),
        ggain_two.reshape(width),
        gblend_all,
    )


def solution(mesh):
    return jax.shard_map(
        partial(body, mesh.shape["dp"]),
        mesh=mesh,
        in_specs=(
            P(("dp", "tensor"), None),
            P("dp", None),
            P(None, None, "tensor"),
            P("tensor", None),
            P(None, "tensor"),
            P("tensor", None),
            P(),
            P(),
            P(None, "tensor"),
            P(("dp", "tensor"), None),
        ),
        out_specs=(
            P(("dp", "tensor"), None),
            P(("dp", "tensor"), None),
            P(None, None, "tensor"),
            P("tensor", None),
            P(None, "tensor"),
            P("tensor", None),
            P(),
            P(),
            P(None, "tensor"),
        ),
        check_vma=False,
    )
```

```python
from functools import partial

import jax
import jax.numpy as jnp
from jax import lax
from jax.experimental import pallas as pl
from jax.experimental.pallas import tpu as pltpu
from jax.sharding import PartitionSpec as P

BAND = 30
HALO = 32
EXTRA = 64
LATE_TURN = 2
BLOCK = 128
EPS = 1e-06
BF = jnp.bfloat16
F32 = jnp.float32
GELU_A = 0.7978845608028654
GELU_B = 0.044715


def nn(left, right):
    return lax.dot_general(left, right, (((1,), (0,)), ((), ())), preferred_element_type=F32)


def nt(left, right):
    return lax.dot_general(left, right, (((1,), (1,)), ((), ())), preferred_element_type=F32)


def tn(left, right):
    return lax.dot_general(left, right, (((0,), (0,)), ((), ())), preferred_element_type=F32)


def iota(shape, dim):
    return lax.broadcasted_iota(jnp.int32, shape, dim)


def whole(shape):
    return pl.BlockSpec(shape, lambda *_: (0,) * len(shape))


def params(mebibytes):
    return pltpu.CompilerParams(vmem_limit_bytes=mebibytes << 20)


def cost(micros):
    return pl.CostEstimate(flops=int(micros * 1e7), bytes_accessed=1 << 20, transcendentals=0)


def tie(*values):
    return lax.optimization_barrier(values)


class Copies:
    def __init__(self, sems):
        self.sems = sems
        self.used = 0

    def make(self, source, target):
        self.used += 1
        return pltpu.make_async_copy(source, target, self.sems.at[self.used - 1])


def document_ends(lengths_ref, rows):
    end = -lax.axis_index("tensor") * rows
    ends = [end]
    for doc in range(lengths_ref.shape[1]):
        end = end + lengths_ref[0, doc]
        ends.append(end)
    return ends[1:] + ends[:1]


def starts_of(ends, places):
    start = jnp.full(places.shape, ends[-1], jnp.int32)
    for end in ends[:-1]:
        start = jnp.where(places >= end, jnp.maximum(start, end), start)
    return start


def start_at(ends, place):
    start = ends[-1]
    for end in ends[:-1]:
        start = jnp.where(place >= end, jnp.maximum(start, end), start)
    return start


def norm_project_kernel(x_ref, gain_ref, w_ref, normed_ref, out_ref):
    x = x_ref[...].astype(F32)
    r = lax.rsqrt(jnp.mean(x * x, axis=1, keepdims=True) + EPS)
    normed = (x * r * gain_ref[...]).astype(BF)
    normed_ref[...] = normed
    project(normed, w_ref, out_ref)


def project(normed, w_ref, out_ref):
    cols = w_ref.shape[2]
    for kind in range(3):
        out_ref[:, cols * kind : cols * kind + cols] = nn(normed, w_ref[kind]).astype(BF)


PACKET = 4 * (128 + 16) + 8 * HALO


def packed_state(state):
    return jnp.concatenate([state[:64] + state[64:128], state[128:192] + state[192:]], axis=0).astype(BF)


def unpacked_state(packed, diag):
    one, two = packed[:64], packed[64:]
    state = jnp.concatenate([one, one, two, two], axis=0)
    return jnp.where(diag, state, jnp.zeros_like(state))


def pack(packet_ref, pair, state, total):
    base = 144 * pair
    packet_ref[base : base + 128] = packed_state(state)
    packet_ref[base + 128 : base + 144] = jnp.broadcast_to(total, (16, 128)).astype(BF)


def pack_halo(packet_ref, kind, pair, rows):
    base = 576 + HALO * (4 * kind + pair)
    packet_ref[base : base + HALO] = rows


def unpack(packet_ref, pair, diag):
    base = 144 * pair
    state = unpacked_state(packet_ref[base : base + 128].astype(F32), diag)
    return state, packet_ref[base + 128 : base + 144].astype(F32)[:8]


def unpack_halo(packet_ref, kind, pair):
    base = 576 + HALO * (4 * kind + pair)
    return packet_ref[base : base + HALO]


def first_feature(values):
    return jnp.where(values > 0, values + 1.0, jnp.exp(jnp.minimum(values, 0.0))).astype(BF)


def second_feature(values):
    return jnp.tanh(values).astype(BF)


def pair_diag(rows, cols):
    row = iota((rows, cols), 0)
    col = iota((rows, cols), 1)
    return ((row // 64) % 2) == ((col // 64) % 2)


def project_state_kernel(lengths_ref, normed_ref, w_ref, own_ref, out_ref, packet_ref):
    rows = normed_ref.shape[0]
    project(normed_ref[...], w_ref, out_ref)
    member_from = start_at(document_ends(lengths_ref, rows), rows - 1)
    member = iota((rows, 1), 0) >= member_from
    ks, vs = [heads_of(own_ref, out_ref, kind) for kind in (1, 2)]
    wide = [jnp.where(member, k.astype(F32), 0.0) for k in ks]
    ones = [jnp.where(member, first_feature(k).astype(F32), 0.0) for k in wide]
    features = each(lambda k, one: jnp.concatenate([one.astype(BF), second_feature(k)], axis=1), wide, ones)
    states = each(tn, features, vs)
    diag = pair_diag(256, 128)
    for pair in PAIRS:
        slot = (pair + 2) % 4
        pack(packet_ref, slot, jnp.where(diag, states[pair], 0.0), jnp.sum(ones[pair], axis=0, keepdims=True))
        pack_halo(packet_ref, 0, slot, ks[pair][rows - HALO :])
        pack_halo(packet_ref, 1, slot, vs[pair][rows - HALO :])


def block_masks(ends, first):
    row_places = first + iota((1, 256), 1) % BLOCK
    start_row = starts_of(ends, row_places)
    window_places = first - HALO + iota((BLOCK + HALO, 256), 0)
    banded = (window_places <= row_places) & (
        window_places >= jnp.maximum(start_row, row_places - (BAND - 1))
    )
    key_places = first + iota((BLOCK, 256), 0)
    causal = (key_places <= row_places) & (key_places >= start_row)
    col_places = first + iota((BLOCK, 1), 0)
    start_col = starts_of(ends, col_places)
    key_lane = first + iota((BLOCK, BLOCK), 1)
    causal_q = ((key_lane <= col_places) & (key_lane >= start_col)).astype(F32).astype(BF)
    count = (col_places - start_col + 1).astype(F32)
    carried = start_col < first
    member_from = start_at(ends, first + BLOCK - 1)
    member = col_places >= member_from
    keep = member_from < first
    return banded, causal, causal_q, count, carried, member, keep


def stack_heads(values):
    lane = iota(values.shape, 1) % 128
    zero = jnp.zeros_like(values)
    return jnp.concatenate(
        [jnp.where(lane < 64, values, zero), jnp.where(lane >= 64, values, zero)], axis=0
    )


def pick_heads(values):
    half = values.shape[0] // 2
    lane = iota((half, values.shape[1]), 1) % 128
    return jnp.where(lane < 64, values[:half], values[half:])


def ones_diagonal():
    return pair_diag(128, 128).astype(F32).astype(BF)


def only(mask, values):
    return jnp.where(mask, values, jnp.zeros_like(values))


def each(function, *lists):
    return [function(*values) for values in zip(*lists)]


class Front:
    def __init__(self, qs, ks, prev_ks, blends, carries, masks, ones_diag):
        banded, causal, causal_q, count, carried, member, keep = masks
        self.q_stack = each(lambda q: stack_heads(q * 0.125), qs)
        self.window = each(lambda prev, k: jnp.concatenate([prev, k], axis=0), prev_ks, ks)
        scores = each(nt, self.window, self.q_stack)
        self.k_one = each(lambda k: first_feature(k.astype(F32)), ks)
        products = each(lambda k_one: nn(causal_q, k_one), self.k_one)
        self.q_one = each(lambda q: first_feature(q.astype(F32)), qs)
        self.sums = each(lambda product, carry: product + jnp.where(carried, carry, 0.0), products, carries)
        self.total = each(
            lambda q_one, sums: nn((q_one.astype(F32) * sums).astype(BF), ones_diag), self.q_one, self.sums
        )
        self.q_two = each(lambda q: second_feature(q.astype(F32)), qs)
        self.k_both = each(
            lambda k_one, k: jnp.concatenate([k_one, second_feature(k.astype(F32))], axis=1), self.k_one, ks
        )
        scores = each(lambda score: jnp.where(banded, score, -1e30), scores)
        raised = each(lambda score: jnp.exp(score - jnp.max(score, axis=0, keepdims=True)), scores)
        self.near = each(lambda r: r * (1.0 / jnp.sum(r, axis=0, keepdims=True)), raised)
        inverse = 1.0 / count
        self.ratio_one = each(lambda blend, total: blend[0] / total, blends, self.total)
        self.ratio_two = each(lambda blend: blend[1] * inverse, blends)
        self.q_scaled = each(
            lambda q_one, q_two, one, two: jnp.concatenate(
                [(q_one.astype(F32) * one).astype(BF), (q_two.astype(F32) * two).astype(BF)], axis=1
            ),
            self.q_one,
            self.q_two,
            self.ratio_one,
            self.ratio_two,
        )
        self.s_stack = each(stack_heads, self.q_scaled)
        far = each(nt, self.k_both, self.s_stack)
        self.weights = each(
            lambda near, far: jnp.concatenate(
                [near[:HALO].astype(BF), (near[HALO:] + jnp.where(causal, far, 0.0)).astype(BF)], axis=0
            ),
            self.near,
            far,
        )


PAIRS = range(4)


def pair_lanes(pair):
    return slice(128 * pair, 128 * pair + 128)


def value_lanes(pair):
    return slice(512 + 128 * pair, 640 + 128 * pair)


def heads_of(own_ref, other_ref, kind):
    first = own_ref.shape[1] // 3 * kind
    return [
        (own_ref if pair < 2 else other_ref)[:, first + 128 * (pair % 2) : first + 128 * (pair % 2) + 128]
        for pair in PAIRS
    ]


def pair_blends(own_ref, other_ref):
    first_head = iota((1, 128), 1) < 64
    rows = []
    for pair in PAIRS:
        ref = own_ref if pair < 2 else other_ref
        head = 2 * (pair % 2)
        rows.append([jnp.where(first_head, ref[kind, head], ref[kind, head + 1]) for kind in range(2)])
    return rows


def mixer_forward_block(
    index,
    total_rows,
    lengths_ref,
    own_ref,
    other_ref,
    blend_own_ref,
    blend_other_ref,
    state_out_ref,
    prev_out_ref,
    near_ref,
    weights_ref,
    sums_ref,
    total_ref,
    state_ref,
    sum_ref,
    prev_ref,
):
    first = index * BLOCK

    masks = block_masks(document_ends(lengths_ref, total_rows), first)
    banded, causal, causal_q, count, carried, member, keep = masks
    diag = pair_diag(256, 128)
    qs, ks, vs = [heads_of(own_ref, other_ref, kind) for kind in range(3)]
    prev = prev_ref[...]
    states = [state_ref[pair] for pair in PAIRS]
    sums_in = [sum_ref[pair] for pair in PAIRS]
    blends = pair_blends(blend_own_ref, blend_other_ref)
    front = Front(
        qs,
        ks,
        [prev[:, pair_lanes(pair)] for pair in PAIRS],
        blends,
        [total[0:1] for total in sums_in],
        masks,
        ones_diagonal(),
    )
    state_low = each(lambda state: state.astype(BF), states)
    inter = each(lambda q, state: nn(only(carried, q), state), front.q_scaled, state_low)
    added = each(lambda k, v: tn(only(member, k), v), front.k_both, vs)
    outs = [
        tn(front.weights[pair], jnp.concatenate([prev[:, value_lanes(pair)], vs[pair]], axis=0))
        for pair in PAIRS
    ]
    outs = each(lambda out, term: pick_heads(out) + term, outs, inter)
    for pair in PAIRS:
        state_out_ref[0, pair] = packed_state(states[pair])
        near_ref[0, pair] = front.near[pair].astype(BF)
        weights_ref[0, pair] = front.weights[pair][HALO:]
        sums_ref[:, pair_lanes(pair)] = front.sums[pair].astype(BF)
        total_ref[:, pair_lanes(pair)] = (1.0 / front.total[pair]).astype(BF)
        state_ref[pair] = jnp.where(keep, states[pair], 0.0) + jnp.where(diag, added[pair], 0.0)
        sum_ref[pair] = jnp.broadcast_to(front.sums[pair][BLOCK - 1 : BLOCK], (8, 128))
        prev_ref[:, pair_lanes(pair)] = ks[pair][BLOCK - HALO :]
        prev_ref[:, value_lanes(pair)] = vs[pair][BLOCK - HALO :]
    prev_out_ref[0] = prev
    return jnp.concatenate(outs, axis=1).astype(BF)


def mixer_backward_block(
    index,
    total_rows,
    lengths_ref,
    blend_own_ref,
    blend_other_ref,
    own_ref,
    other_ref,
    state_ref,
    prev_ref,
    near_ref,
    weights_ref,
    sums_ref,
    total_ref,
    grad_ref,
    gq_ref,
    gk_ref,
    gv_ref,
    blend_out_ref,
    halo_ref,
    back_state_ref,
    back_sum_ref,
):
    first = index * BLOCK
    ends = document_ends(lengths_ref, total_rows)
    blends = pair_blends(blend_own_ref, blend_other_ref)
    row_places = first + iota((1, 256), 1) % BLOCK
    key_places = first + iota((BLOCK, 256), 0)
    causal = (key_places <= row_places) & (key_places >= starts_of(ends, row_places))
    causal_k = causal[:, :BLOCK].astype(F32).astype(BF)
    col_places = first + iota((BLOCK, 1), 0)
    start_col = starts_of(ends, col_places)
    inverse = 1.0 / (col_places - start_col + 1).astype(F32)
    carried = start_col < first
    member_from = start_at(ends, first + BLOCK - 1)
    member = col_places >= member_from
    keep = member_from < first
    diag = pair_diag(256, 128)
    ones_diag = ones_diagonal()
    qs, ks, vs = [heads_of(own_ref, other_ref, kind) for kind in range(3)]
    prev = prev_ref[0]
    grads = [grad_ref[:, pair_lanes(pair)] for pair in PAIRS]
    states = [unpacked_state(state_ref[0, pair], diag) for pair in PAIRS]
    backs = [back_state_ref[pair] for pair in PAIRS]
    back_sums = [back_sum_ref[pair][0:1] for pair in PAIRS]
    nears = [near_ref[0, pair] for pair in PAIRS]
    wide_ks = [k.astype(F32) for k in ks]
    wide_qs = [q.astype(F32) for q in qs]
    raised_k = [jnp.exp(jnp.minimum(k, 0.0)) for k in wide_ks]
    raised_q = [jnp.exp(jnp.minimum(q, 0.0)) for q in wide_qs]
    tanh_ks = [jnp.tanh(k) for k in wide_ks]
    tanh_qs = [jnp.tanh(q) for q in wide_qs]
    k_both = each(
        lambda k, raised, t: jnp.concatenate(
            [jnp.where(k > 0, k + 1.0, raised).astype(BF), t.astype(BF)], axis=1
        ),
        wide_ks,
        raised_k,
        tanh_ks,
    )
    q_one = each(lambda q, raised: jnp.where(q > 0, q + 1.0, raised).astype(BF).astype(F32), wide_qs, raised_q)
    inverse_total = [total_ref[:, pair_lanes(pair)].astype(F32) for pair in PAIRS]
    ratio_one = each(lambda blend, total: blend[0] * total, blends, inverse_total)
    ratio_two = [blend[1] * inverse for blend in blends]
    q_scaled = each(
        lambda one, ratio, t, other: jnp.concatenate(
            [(one * ratio).astype(BF), (t.astype(BF).astype(F32) * other).astype(BF)], axis=1
        ),
        q_one,
        ratio_one,
        tanh_qs,
        ratio_two,
    )
    g_stack = each(stack_heads, grads)
    v_window = [jnp.concatenate([prev[:, value_lanes(pair)], vs[pair]], axis=0) for pair in PAIRS]
    grad_weights = each(nt, v_window, g_stack)
    dv = [
        nn(jnp.concatenate([nears[pair][:HALO], weights_ref[0, pair]], axis=0), g_stack[pair]) for pair in PAIRS
    ]
    up_inter = each(lambda grad, state: nt(only(carried, grad), state), grads, states)
    far = each(lambda gw: jnp.where(causal, gw[HALO:], 0.0).astype(BF), grad_weights)
    up = each(tn, far, k_both)
    s_stack = each(stack_heads, q_scaled)
    dfeat = each(nn, far, s_stack)
    near_wide = each(lambda near: near.astype(F32), nears)
    inner = each(lambda near, gw: near * gw, near_wide, grad_weights)
    dscores = each(
        lambda near, inner: (inner - near * jnp.sum(inner, axis=0, keepdims=True)).astype(BF),
        near_wide,
        inner,
    )
    up = each(lambda up, inter: pick_heads(up) + inter, up, up_inter)
    mean_one = each(
        lambda q, up, total: nn((q * up[:, :128]).astype(BF), ones_diag) * total,
        q_one,
        up,
        inverse_total,
    )
    window = [jnp.concatenate([prev[:, pair_lanes(pair)], ks[pair]], axis=0) for pair in PAIRS]
    q_stack = each(lambda q: stack_heads(q * 0.125), qs)
    gq_near = each(tn, dscores, window)
    dk = each(nn, dscores, q_stack)
    back_low = each(lambda back: back.astype(BF), backs)
    dv_far = each(lambda k, back: nn(only(member, k), back), k_both, back_low)
    dfeat_far = each(lambda v, back: nt(only(member, v), back), vs, back_low)
    added = each(lambda q, grad: tn(only(carried, q), grad), q_scaled, grads)
    weighted = each(lambda mean, q: (mean * q[:, :128].astype(F32)).astype(BF), mean_one, q_scaled)
    mean_back = each(lambda weight: nn(causal_k, weight), weighted)
    for pair in PAIRS:
        lanes, values = pair_lanes(pair), value_lanes(pair)
        up_one, up_two = up[pair][:, :128], up[pair][:, 128:]
        tanh_q, slope_q = tanh_qs[pair], raised_q[pair]
        up_two = up_two * inverse
        grad_one = ratio_one[pair] * (up_one - mean_one[pair] * sums_ref[:, lanes].astype(F32))
        grad_two = blends[pair][1] * up_two
        gq = pick_heads(gq_near[pair]) * 0.125 + grad_one * slope_q + grad_two * (1.0 - tanh_q * tanh_q)
        gq_ref[:, lanes] = gq.astype(BF)
        blend_out_ref[0, pair] += jnp.broadcast_to(
            jnp.sum(mean_one[pair], axis=0, keepdims=True) / 64.0, (8, 128)
        )
        blend_out_ref[1, pair] += jnp.broadcast_to(jnp.sum(tanh_q * up_two, axis=0, keepdims=True), (8, 128))
        dv_own = dv[pair][HALO:] + dv_far[pair]
        dfeat_all = dfeat[pair] + dfeat_far[pair]
        d_one = dfeat_all[:, :128] - mean_back[pair] - jnp.where(member, back_sums[pair], 0.0)
        d_two = dfeat_all[:, 128:]
        tanh_k, slope_k = tanh_ks[pair], raised_k[pair]
        gk = dk[pair][HALO:] + d_one * slope_k + d_two * (1.0 - tanh_k * tanh_k)
        gk_ref[: BLOCK - HALO, lanes] = gk[: BLOCK - HALO].astype(BF)
        gk_ref[BLOCK - HALO :, lanes] = (gk[BLOCK - HALO :] + halo_ref[:, lanes]).astype(BF)
        gv_ref[: BLOCK - HALO, lanes] = dv_own[: BLOCK - HALO].astype(BF)
        gv_ref[BLOCK - HALO :, lanes] = (dv_own[BLOCK - HALO :] + halo_ref[:, values]).astype(BF)
        halo_ref[:, lanes] = dk[pair][:HALO]
        halo_ref[:, values] = dv[pair][:HALO]
        back_state_ref[pair] = jnp.where(keep, backs[pair], 0.0) + jnp.where(diag, added[pair], 0.0)
        added_sum = jnp.sum(only(carried, weighted[pair].astype(F32)), axis=0, keepdims=True)
        back_sum_ref[pair] = jnp.broadcast_to(
            jnp.where(keep, back_sums[pair], 0.0) + added_sum, (8, 128)
        )


STEP_BLOCKS = 2


def mixer_backward_kernel(lengths_ref, blend_own_ref, blend_other_ref, *refs):
    inputs, outputs = refs[:9], refs[9:12]
    packet_ref, blend_out_ref, halo_ref, back_state_ref, back_sum_ref = refs[12:]
    step = pl.program_id(0)
    steps = pl.num_programs(0)

    @pl.when(step == 0)
    def _():
        for ref in (halo_ref, back_state_ref, back_sum_ref, blend_out_ref):
            ref[...] = jnp.zeros_like(ref)

    for sub in reversed(range(STEP_BLOCKS)):
        views = []
        for ref in inputs + outputs:
            unit = ref.shape[0] // STEP_BLOCKS
            views.append(ref.at[sub * unit : sub * unit + unit])
        mixer_backward_block(
            (steps - 1 - step) * STEP_BLOCKS + sub,
            steps * STEP_BLOCKS * BLOCK,
            lengths_ref,
            blend_own_ref,
            blend_other_ref,
            *views,
            blend_out_ref,
            halo_ref,
            back_state_ref,
            back_sum_ref,
        )

    @pl.when(step == steps - 1)
    def _():
        for pair in PAIRS:
            slot = (pair + 2) % 4
            pack(packet_ref, slot, back_state_ref[pair], back_sum_ref[pair][0:1])
            pack_halo(packet_ref, 0, slot, halo_ref[:, pair_lanes(pair)].astype(BF))
            pack_halo(packet_ref, 1, slot, halo_ref[:, value_lanes(pair)].astype(BF))


LANES = 256


def layer_kernel(
    blocks,
    parts,
    lengths_ref,
    blend_own_ref,
    blend_other_ref,
    packet_ref,
    gain_ref,
    wa_own_ref,
    wa_other_ref,
    own_hbm,
    other_hbm,
    x_hbm,
    cot_hbm,
    wi_own_hbm,
    wi_other_hbm,
    wo_own_hbm,
    wo_other_hbm,
    branch_ref,
    gmix_ref,
    ggain_ref,
    attn_own_ref,
    attn_sent_ref,
    mixed_hbm,
    state_hbm,
    prev_hbm,
    near_hbm,
    weights_hbm,
    sums_hbm,
    total_hbm,
    active_hbm,
    out_own_hbm,
    in_own_hbm,
    out_sent_hbm,
    in_sent_hbm,
    own_ref,
    other_ref,
    x_ref,
    grad_ref,
    wi_ref,
    wo_ref,
    mixed_ref,
    state_out_ref,
    prev_out_ref,
    near_ref,
    weights_ref,
    sums_ref,
    total_ref,
    active_ref,
    stack_ref,
    state_ref,
    sum_ref,
    prev_ref,
    y_ref,
    r_ref,
    normed_ref,
    normed_turned_ref,
    grad_turned_ref,
    back_ref,
    sems,
):
    copies = Copies(sems)
    rows, width = x_ref.shape
    heads = wa_own_ref.shape[0]
    units = wo_ref.shape[1]
    chunk_units = units // parts
    tokens = ((own_hbm, own_ref), (other_hbm, other_ref), (x_hbm, x_ref), (cot_hbm, grad_ref))
    first_loads = [copies.make(source.at[:BLOCK], target.at[:BLOCK]) for source, target in tokens]
    later_loads = [copies.make(source.at[BLOCK:], target.at[BLOCK:]) for source, target in tokens]
    weight_loads = [
        copies.make(source, target)
        for source, target in (
            (wi_own_hbm, wi_ref.at[0]),
            (wo_own_hbm, wo_ref.at[0]),
            (wi_other_hbm, wi_ref.at[1]),
            (wo_other_hbm, wo_ref.at[1]),
        )
    ]
    for load in first_loads + later_loads + weight_loads:
        load.start()
    for pair in PAIRS:
        state_ref[pair], sum_ref[pair] = unpack(packet_ref, pair, pair_diag(256, 128))
        prev_ref[:, pair_lanes(pair)] = unpack_halo(packet_ref, 0, pair)
        prev_ref[:, value_lanes(pair)] = unpack_halo(packet_ref, 1, pair)
    back_ref[...] = jnp.zeros_like(back_ref)
    for load in first_loads:
        load.wait()

    def block(step, _):
        @pl.when(step == 1)
        def _():
            for load in later_loads:
                load.wait()

        here = pl.ds(pl.multiple_of(step * BLOCK, BLOCK), BLOCK)
        only_here = pl.ds(step, 1)
        mixed = mixer_forward_block(
            step,
            rows,
            lengths_ref,
            own_ref.at[here],
            other_ref.at[here],
            blend_own_ref,
            blend_other_ref,
            state_out_ref.at[only_here],
            prev_out_ref.at[only_here],
            near_ref.at[only_here],
            weights_ref.at[only_here],
            sums_ref.at[here],
            total_ref.at[here],
            state_ref,
            sum_ref,
            prev_ref,
        )
        mixed_ref[here, :] = mixed
        hidden = x_ref[here, :].astype(F32)
        hidden = hidden + nn(mixed[:, :heads], wa_own_ref[...]) + nn(mixed[:, heads:], wa_other_ref[...])
        r = lax.rsqrt(jnp.mean(hidden * hidden, axis=1, keepdims=True) + EPS)
        y = hidden * r
        y_ref[here, :] = y
        r_ref[here, :] = jnp.broadcast_to(r, (BLOCK, r_ref.shape[1]))
        normed = (y * gain_ref[...]).astype(BF)
        normed_ref[here, :] = normed
        normed_turned_ref[:, here] = normed.T
        grad_turned_ref[:, here] = grad_ref[here, :].T
        return 0

    def some_blocks(step, _):
        for sub in range(STEP_BLOCKS):
            block(step * STEP_BLOCKS + sub, 0)
        return 0

    lax.fori_loop(0, blocks // STEP_BLOCKS, some_blocks, 0)
    stores = [
        copies.make(source, target)
        for source, target in (
            (mixed_ref, mixed_hbm),
            (state_out_ref, state_hbm),
            (prev_out_ref, prev_hbm),
            (near_ref, near_hbm),
            (weights_ref, weights_hbm),
            (sums_ref, sums_hbm),
            (total_ref, total_hbm),
        )
    ]
    for store in stores:
        store.start()
    for load in weight_loads:
        load.wait()
    chunk_stores = []
    for late in range(2 * parts):
        half, place = late // parts, late % parts
        out_target, in_target = ((out_own_hbm, in_own_hbm), (out_sent_hbm, in_sent_hbm))[half]
        spots = [(0, out_target, units * side + chunk_units * place, chunk_units) for side in range(width // LANES)]
        count = width * chunk_units // LANES
        spots.append((1, in_target, count * place, count))
        columns = pl.ds(late * chunk_units, chunk_units)
        chunk_stores.append(
            [
                copies.make(stack_ref.at[half, kind, pl.ds(row, count), :], target.at[pl.ds(row, count), :])
                for kind, target, row, count in spots
            ]
            + [copies.make(active_ref.at[:, columns], active_hbm.at[:, columns])]
        )

    def chunk(late, _):
        half, place = late // parts, late % parts
        normed = normed_ref[...]
        grad = grad_ref[...]
        first = pl.multiple_of(place * chunk_units, chunk_units)
        wi = wi_ref[half, :, pl.ds(first, chunk_units)]
        wo = wo_ref[half, pl.ds(first, chunk_units), :]
        spans = [slice(LANES * piece, LANES * piece + LANES) for piece in range(chunk_units // LANES)]
        us = [nn(normed, wi[:, span]) for span in spans]
        gacts = [nt(grad, wo[span, :]) for span in spans]
        gpres = []
        for piece in range(len(spans)):
            u = us[piece]
            square = u * u
            t = jnp.tanh(u * (GELU_A + (GELU_A * GELU_B) * square))
            gate = 0.5 + 0.5 * t
            active = (u * gate).astype(BF)
            column = pl.multiple_of(late * chunk_units + LANES * piece, LANES)
            active_ref[:, pl.ds(column, LANES)] = active
            slope = gate + (u * (0.5 - 0.5 * t * t)) * (GELU_A + (3.0 * GELU_A * GELU_B) * square)
            gpre = (gacts[piece] * slope).astype(BF)
            gpres.append(gpre)
            gout = nn(grad_turned_ref[...], active).astype(BF).T
            spot = len(spans) * place + piece
            for side in range(width // LANES):
                row = pl.multiple_of(units * side + LANES * spot, LANES)
                stack_ref[half, 0, pl.ds(row, LANES), :] = gout[:, LANES * side : LANES * side + LANES]
            row = pl.multiple_of(width * spot, LANES)
            stack_ref[half, 1, pl.ds(row, width), :] = nn(normed_turned_ref[...], gpre).astype(BF)
        back_ref[...] += nt(jnp.concatenate(gpres, axis=1), wi)
        for number, some in enumerate(chunk_stores):

            @pl.when(late == number)
            def _(some=some):
                for store in some:
                    store.start()

        return 0

    lax.fori_loop(0, 2 * parts, chunk, 0)
    back, y = back_ref[...], y_ref[...]
    scaled = back * gain_ref[...]
    mean = jnp.mean(scaled * y, axis=1, keepdims=True)
    ghid = grad_ref[...].astype(F32) + r_ref[:, :1] * (scaled - y * mean)
    branch = ghid.astype(BF)
    branch_ref[...] = branch
    gmix_ref[:, :heads] = nt(branch, wa_own_ref[...]).astype(BF)
    gmix_ref[:, heads:] = nt(branch, wa_other_ref[...]).astype(BF)
    ggain_ref[...] = jnp.broadcast_to(jnp.sum(back * y, axis=0, keepdims=True), ggain_ref.shape)
    gattn = tn(mixed_ref[...], branch).astype(BF)
    for half, ref in enumerate((attn_own_ref, attn_sent_ref)):
        for side in range(width // LANES):
            lanes = slice(LANES * side, LANES * side + LANES)
            ref[heads * side : heads * side + heads] = gattn[heads * half : heads * half + heads, lanes]
    for store in stores + [store for some in chunk_stores for store in some]:
        store.wait()


def output_kernel(x_ref, mixed_ref, active_ref, wa_own_ref, wa_other_ref, wo_own_ref, wo_other_ref, out_ref):
    heads = wa_own_ref.shape[0]
    units = wo_own_ref.shape[0]
    total = x_ref[...].astype(F32)
    total = total + (nn(mixed_ref[:, :heads], wa_own_ref[...]) + nn(mixed_ref[:, heads:], wa_other_ref[...]))
    total = total + (nn(active_ref[:, :units], wo_own_ref[...]) + nn(active_ref[:, units:], wo_other_ref[...]))
    out_ref[...] = total.astype(BF)


def finish_kernel(
    lengths_ref,
    gblend_ref,
    ggain_ref,
    gain_ref,
    packet_hbm,
    own_hbm,
    other_hbm,
    gk_hbm,
    gv_hbm,
    gq_hbm,
    normed_hbm,
    w_own_hbm,
    w_other_hbm,
    attn_own_hbm,
    attn_sent_hbm,
    gkv_hbm,
    wgrad_own_hbm,
    wgrad_sent_hbm,
    packet_ref,
    own_ref,
    other_ref,
    gk_ref,
    gv_ref,
    gq_ref,
    normed_ref,
    w_own_ref,
    w_other_ref,
    gkv_ref,
    wgrad_own_ref,
    wgrad_sent_ref,
    sems,
):
    copies = Copies(sems)
    rows, width = normed_ref.shape
    cols = w_own_ref.shape[2]
    wgrads = (wgrad_own_ref, wgrad_sent_ref)
    attn_rows = attn_own_hbm.shape[0]
    keys_values = slice(cols, 3 * cols)
    loads = [
        copies.make(source, target)
        for source, target in (
            (packet_hbm, packet_ref),
            (own_hbm.at[:, keys_values], own_ref),
            (gk_hbm, gk_ref),
            (gv_hbm, gv_ref),
            (other_hbm.at[:, keys_values], other_ref),
            (normed_hbm, normed_ref),
            (gq_hbm, gq_ref),
            (w_own_hbm, w_own_ref),
            (w_other_hbm, w_other_ref),
            (attn_own_hbm, wgrad_own_ref.at[3 * width : 3 * width + attn_rows]),
            (attn_sent_hbm, wgrad_sent_ref.at[3 * width : 3 * width + attn_rows]),
        )
    ]
    gkv_stores, wgrad_stores = [], []
    for half, target in enumerate((wgrad_own_hbm, wgrad_sent_hbm)):
        lanes = slice(2 * cols * half, 2 * cols * half + 2 * cols)
        gkv_stores.append(copies.make(gkv_ref.at[:, lanes], gkv_hbm.at[:, lanes]))
        spans = [slice(width * kind, width * kind + width) for kind in range(3)]
        spans.append(slice(3 * width, wgrads[half].shape[0]))
        wgrad_stores.append([copies.make(wgrads[half].at[span], target.at[span]) for span in spans])
    for load in loads:
        load.start()
    live = lax.axis_index("tensor") == 0
    member_from = start_at(document_ends(lengths_ref, rows), rows - 1)
    member = (iota((rows, 1), 0) >= member_from) & live
    diag = pair_diag(256, 128)
    cut = rows - HALO
    for load in loads[:4]:
        load.wait()
    for pair in PAIRS:
        if pair == 2:
            loads[4].wait()
        src = own_ref if pair < 2 else other_ref
        col = 128 * (pair % 2)
        lanes = pair_lanes(pair)
        k = src[:, col : col + 128].astype(F32)
        v = src[:, cols + col : cols + col + 128]
        back, back_sum = unpack(packet_ref, pair, diag)
        back, back_sum = back.astype(BF), back_sum[0:1]
        t = jnp.tanh(k)
        raised = jnp.exp(jnp.minimum(k, 0.0))
        k_both = jnp.concatenate([jnp.where(k > 0, k + 1.0, raised).astype(BF), t.astype(BF)], axis=1)
        dfeat = nt(v, back)
        extra_k = (dfeat[:, :128] - back_sum) * raised + dfeat[:, 128:] * (1.0 - t * t)
        extra_v = nn(k_both, back)
        for kind, (grad_ref, extra) in enumerate(((gk_ref, extra_k), (gv_ref, extra_v))):
            grad = grad_ref[:, lanes].astype(F32) + jnp.where(member, extra, 0.0)
            halo = jnp.where(live, unpack_halo(packet_ref, kind, pair).astype(F32), 0.0)
            base = cols * (2 * (pair // 2) + kind) + col
            gkv_ref[:cut, base : base + 128] = grad[:cut].astype(BF)
            gkv_ref[cut:, base : base + 128] = (grad[cut:] + halo).astype(BF)
        if pair % 2 == 1:
            gkv_stores[pair // 2].start()
    for load in loads[5:]:
        load.wait()
    normed = normed_ref[...].T
    ones = jnp.ones((1, cols), BF)
    gain_grad = jnp.zeros((1, width), F32)
    for half, (wgrad_ref, w_ref) in enumerate(zip(wgrads, (w_own_ref, w_other_ref))):
        for kind in range(3):
            if kind == 0:
                grad = gq_ref[:, cols * half : cols * half + cols]
            else:
                first = cols * (2 * half + kind - 1)
                grad = gkv_ref[:, first : first + cols]
            wgrad = nn(normed, grad)
            wgrad_ref[width * kind : width * kind + width] = wgrad.astype(BF)
            wgrad_stores[half][kind].start()
            products = wgrad * w_ref[kind].astype(F32)
            high = products.astype(BF)
            low = (products - high.astype(F32)).astype(BF)
            gain_grad = gain_grad + nt(ones, high) + nt(ones, low)
    gain_grad = gain_grad / gain_ref[...]
    for half, wgrad_ref in enumerate(wgrads):
        blends = [
            jnp.concatenate([gblend_ref[kind, 2 * half + pair][0:1] for pair in range(2)], axis=1)
            for kind in range(2)
        ]
        gains = [gain_grad[:, :256], gain_grad[:, 256:], ggain_ref[0:1, :256], ggain_ref[0:1, 256:]]
        extra = jnp.concatenate(blends + gains + [jnp.zeros((10, 256), F32)], axis=0)
        base = 3 * width + attn_rows
        wgrad_ref[base : base + 16] = extra.astype(BF)
        wgrad_ref[base + 16 :] = jnp.zeros((EXTRA - 16, 256), BF)
        wgrad_stores[half][3].start()
    for store in gkv_stores + wgrad_stores[0] + wgrad_stores[1]:
        store.wait()


def input_grad_kernel(gq_ref, gkv_ref, x_ref, branch_ref, gain_ref, w_own_ref, w_other_ref, out_ref):
    cols = w_own_ref.shape[2]
    gnormed = None
    for half, w_ref in enumerate((w_own_ref, w_other_ref)):
        for kind in range(3):
            if kind == 0:
                grad = gq_ref[:, cols * half : cols * half + cols]
            else:
                first = cols * (2 * half + kind - 1)
                grad = gkv_ref[:, first : first + cols]
            term = nt(grad, w_ref[kind])
            gnormed = term if gnormed is None else gnormed + term
    x = x_ref[...].astype(F32)
    r = lax.rsqrt(jnp.mean(x * x, axis=1, keepdims=True) + EPS)
    y = x * r
    scaled = gnormed * gain_ref[...]
    grad = branch_ref[...].astype(F32) + r * (scaled - y * jnp.mean(scaled * y, axis=1, keepdims=True))
    out_ref[...] = grad.astype(BF)


def merged(low, mine, got):
    return jnp.where(low, mine, got), jnp.where(low, got, mine)


def put_rows(ref, first_row, lane, parts, first, count):
    rows = parts[0].shape[0]
    lanes = parts[0].shape[1]
    for place, part in enumerate(parts):
        low, high = max(first, rows * place), min(first + count, rows * place + rows)
        if low < high:
            values = part[low - rows * place : high - rows * place].astype(F32)
            ref[first_row + low - first : first_row + high - first, lane : lane + lanes] = values


def feed_output_kernel(
    bits_ref,
    out_mine_hbm,
    in_mine_hbm,
    out_got_hbm,
    in_got_hbm,
    wo_hbm,
    wi_hbm,
    out_mine_ref,
    in_mine_ref,
    out_got_ref,
    in_got_ref,
    wo_ref,
    wi_ref,
    sems,
):
    copies = Copies(sems)
    parts = ((out_mine_ref, in_mine_ref), (out_got_ref, in_got_ref))
    loads = [
        copies.make(source, target)
        for source, target in (
            (out_mine_hbm, out_mine_ref),
            (in_mine_hbm, in_mine_ref),
            (out_got_hbm, out_got_ref),
            (in_got_hbm, in_got_ref),
        )
    ]
    for load in loads:
        load.start()
    units, wide = wo_ref.shape[1], wo_ref.shape[2]
    width, span = wi_ref.shape[1], wi_ref.shape[2]
    middle = units // 2
    stores = []
    for place, (out_part_ref, in_part_ref) in enumerate(parts):
        wo_first = bits_ref[0] if place == 0 else 1 - bits_ref[0]
        wi_first = bits_ref[1] if place == 0 else 1 - bits_ref[1]
        loads[2 * place].wait()
        wo_ref[place] = out_part_ref[...].astype(F32)
        column = pl.multiple_of(wo_first * wide, LANES)
        for rows in (slice(0, middle), slice(middle, units)):
            stores.append(copies.make(wo_ref.at[place, rows], wo_hbm.at[rows, pl.ds(column, wide)]))
            stores[-1].start()
        loads[2 * place + 1].wait()
        for side in range(span // LANES):
            lanes = slice(LANES * side, LANES * side + LANES)
            wi_ref[place, :, lanes] = in_part_ref[width * side : width * side + width].astype(F32)
            column = pl.multiple_of(wi_first * span + LANES * side, LANES)
            stores.append(copies.make(wi_ref.at[place, :, lanes], wi_hbm.at[:, pl.ds(column, LANES)]))
            stores[-1].start()
    for store in stores:
        store.wait()


def last_output_kernel(
    bits_ref,
    a_mine_hbm,
    b_mine_hbm,
    a_got_hbm,
    b_got_hbm,
    wq_ref,
    wa_ref,
    gain_one_ref,
    gain_two_ref,
    blend_ref,
    a_mine_ref,
    b_mine_ref,
    a_got_ref,
    b_got_ref,
    sems,
):
    copies = Copies(sems)
    loads = [
        copies.make(source, target)
        for source, target in (
            (a_mine_hbm, a_mine_ref),
            (b_mine_hbm, b_mine_ref),
            (a_got_hbm, a_got_ref),
            (b_got_hbm, b_got_ref),
        )
    ]
    for load in loads:
        load.start()
    for load in loads:
        load.wait()
    heads, width = wa_ref.shape
    parts = merged(bits_ref[0] == 0, a_mine_ref[...], a_got_ref[...])
    parts += merged(bits_ref[1] == 0, b_mine_ref[...], b_got_ref[...])
    rows = a_mine_ref.shape[0]
    put_rows(wq_ref, 0, 0, parts, 0, 3 * width)
    for side in range(width // LANES):
        put_rows(wa_ref, 0, LANES * side, parts, 3 * width + heads * side, heads)
    rest = parts[3][rows - EXTRA : rows - EXTRA + 16].astype(F32)
    gain_one_ref[...] = jnp.concatenate([rest[2:3], rest[3:4]], axis=1)
    gain_two_ref[...] = jnp.concatenate([rest[4:5], rest[5:6]], axis=1)
    sums = [jnp.sum(rest[:2, 64 * head : 64 * head + 64], axis=1, keepdims=True) for head in range(4)]
    blend_ref[...] = jnp.concatenate(sums, axis=1)


def steps_of(count, late_sizes):
    steps = []
    stride = 1
    while stride < count:
        left = count // stride
        size = next(size for size in ((2,) if len(steps) < 2 else late_sizes) if left % size == 0)
        steps.append((stride, size))
        stride *= size
    return steps


def flip(values, count, step):
    stride, _ = step
    pairs = [(src, src + stride * (1 - 2 * ((src // stride) % 2))) for src in range(count)]
    return lax.ppermute(values, "dp", pairs)


def trade(values, count, step):
    stride, size = step
    groups = [
        [first + stride * digit for digit in range(size)]
        for first in range(count)
        if (first // stride) % size == 0
    ]
    return lax.all_to_all(
        values, "dp", split_axis=0, concat_axis=0, axis_index_groups=groups, tiled=True
    )


class Reduction:
    def __init__(self, stacks, count, whole_late=False):
        self.stacks = [[(term, first) for term in terms] for terms, first, _ in stacks]
        self.rows = [rows for _, _, rows in stacks]
        self.count = count
        steps = steps_of(count, (2,) if whole_late else (4, 2))
        self.orders = [steps, steps[1::-1] + steps[2:]]
        self.whole_late = whole_late
        self.left = min(2, len(steps)) if whole_late else len(steps)
        self.taken = 0
        self.place = lax.axis_index("dp")
        self.held = None
        self.gots = []

    def digit(self, step):
        return (self.place // step[0]) % step[1]

    def cut(self, stack, first, rows):
        total = None
        for term, offset in self.stacks[stack]:
            part = lax.dynamic_slice_in_dim(term, offset + first, rows, 0).astype(F32)
            total = part if total is None else total + part
        return total.astype(BF)

    def after(self, *tokens):
        count = len(self.gots)
        tied = tie(*self.gots, *tokens)
        self.gots = list(tied[:count])
        return tied[count:]

    def gathering(self):
        return self.taken == len(self.orders[0])

    def level(self):
        return self.left - 1 if self.gathering() else self.taken

    def cuts(self):
        if self.gathering():
            if self.held is None:
                self.held = [self.cut(stack, 0, self.rows[stack]) for stack in range(2)]
            if self.level() < 2:
                return list(self.held)
            both = jnp.concatenate(self.held, axis=0)
            return [jnp.broadcast_to(both[None], (self.orders[0][self.level()][1],) + both.shape)]
        if self.level() < 2:
            cuts = []
            for stack in range(2):
                step = self.orders[stack][self.level()]
                rows = self.rows[stack] // 2
                cuts.append(self.cut(stack, (1 - self.digit(step)) * rows, rows))
            return cuts
        size = self.orders[0][self.level()][1]
        wholes = [self.cut(stack, 0, self.rows[stack]) for stack in range(2)]
        if self.whole_late:
            self.sent = jnp.concatenate(wholes, axis=0)
            return [self.sent]
        return [jnp.concatenate([part.reshape(size, -1, part.shape[1]) for part in wholes], axis=1)]

    def send(self, cuts):
        steps = [order[self.level()] for order in self.orders]
        if self.level() < 2:
            self.gots = [flip(cut, self.count, step) for cut, step in zip(cuts, steps)]
        elif self.whole_late:
            self.sent = cuts[0]
            self.gots = [flip(cuts[0], self.count, steps[0])]
        else:
            self.gots = [trade(cuts[0], self.count, steps[0])]

    def take(self):
        steps = [order[self.level()] for order in self.orders]
        size = steps[0][1]
        if self.gathering():
            if self.level() < 2:
                for stack in range(2):
                    low = self.digit(steps[stack]) == 0
                    mine, got = self.held[stack], self.gots[stack]
                    self.held[stack] = jnp.concatenate(
                        [jnp.where(low, mine, got), jnp.where(low, got, mine)], axis=0
                    )
            else:
                first = self.held[0].shape[0]
                (got,) = self.gots
                self.held = [part.reshape(-1, part.shape[2]) for part in (got[:, :first], got[:, first:])]
            self.left -= 1
            self.gots = []
            return
        if self.level() < 2:
            for stack in range(2):
                self.rows[stack] //= 2
                offset = self.digit(steps[stack]) * self.rows[stack]
                terms = [(term, first + offset) for term, first in self.stacks[stack]]
                self.stacks[stack] = terms + [(self.gots[stack], 0)]
        elif self.whole_late:
            (got,) = self.gots
            self.stacks = [[(self.sent, skip), (got, skip)] for skip in (0, self.rows[0])]
        else:
            (got,) = self.gots
            self.rows = [rows // size for rows in self.rows]
            flat = got.reshape(-1, got.shape[2])
            for stack in range(2):
                skip = self.rows[0] * stack
                self.stacks[stack] = [(flat, sum(self.rows) * piece + skip) for piece in range(size)]
        self.taken += 1
        self.gots = []

    def last(self):
        return self.gathering() and self.left <= 1

    def last_bits(self):
        return jnp.stack([self.digit(order[0]) if order else 0 * self.place for order in self.orders])

    def parts(self):
        if self.orders[0]:
            return [self.held[0], self.gots[0], self.held[1], self.gots[1]]
        halves = []
        for held in [self.cut(stack, 0, self.rows[stack]) for stack in range(2)]:
            middle = held.shape[0] // 2
            halves += [held[:middle], held[middle:]]
        return halves


def swap(values):
    return lax.ppermute(values, "tensor", [(0, 1), (1, 0)])


def body(count, tokens, lengths, w_qkv, w_attn, w_in, w_out, gain_attn, gain_mlp, blend, cotangent):
    rows, width = tokens.shape
    blocks = rows // BLOCK

    wq_own = w_qkv.transpose(1, 0, 2)
    wq_other = swap(wq_own)
    wa_other, wi_other, wo_other = swap(w_attn), swap(w_in), swap(w_out)
    blend_other = swap(blend)
    gain_one = gain_attn.reshape(1, width)
    gain_two = gain_mlp.reshape(1, width)
    smem = pl.BlockSpec(memory_space=pltpu.SMEM)

    def row_block(size, cols):
        return pl.BlockSpec((size, cols), lambda i: (i, 0))

    own_cols = 3 * wq_own.shape[2]
    normed, own = pl.pallas_call(
        norm_project_kernel,
        grid=(4,),
        in_specs=[row_block(rows // 4, width), whole((1, width)), whole(wq_own.shape)],
        out_specs=[row_block(rows // 4, width), row_block(rows // 4, own_cols)],
        out_shape=[jax.ShapeDtypeStruct((rows, width), BF), jax.ShapeDtypeStruct((rows, own_cols), BF)],
        compiler_params=params(60),
        cost_estimate=cost(5),
        name="norm_project",
    )(tokens, gain_one, wq_own)
    normed, wi_other, wo_other, wa_other = tie(normed, wi_other, wo_other, wa_other)
    other, packet = pl.pallas_call(
        project_state_kernel,
        in_specs=[smem] + [pl.BlockSpec(memory_space=pltpu.VMEM)] * 3,
        out_shape=[
            jax.ShapeDtypeStruct((rows, own_cols), BF),
            jax.ShapeDtypeStruct((PACKET, 128), BF),
        ],
        compiler_params=params(60),
        cost_estimate=cost(5),
        name="project_state",
    )(lengths, normed, wq_other, own)
    packet = swap(packet)

    units = w_out.shape[0]
    tall = rows // 4
    parts = units // (2 * LANES)
    vmem = pl.BlockSpec(memory_space=pltpu.VMEM)
    stack_rows = units * width // LANES
    attn_rows = w_attn.shape[0] * width // LANES
    anywhere = pl.BlockSpec(memory_space=pltpu.HBM)

    kept_shapes = [
        ((blocks, 4, 128, 128), BF),
        ((blocks, HALO, 1024), BF),
        ((blocks, 4, BLOCK + HALO, 256), BF),
        ((blocks, 4, BLOCK, 256), BF),
        ((rows, width), BF),
        ((rows, width), BF),
    ]
    stored_shapes = [((rows, width), BF)] + kept_shapes + [((rows, 2 * units), BF)]
    branch, gmix, ggain_mlp, *outs = pl.pallas_call(
        partial(layer_kernel, blocks, parts),
        in_specs=[smem] * 3 + [vmem] * 4 + [anywhere] * 8,
        out_specs=[vmem] * 5 + [anywhere] * 12,
        out_shape=[
            jax.ShapeDtypeStruct((rows, width), BF),
            jax.ShapeDtypeStruct((rows, width), BF),
            jax.ShapeDtypeStruct((8, width), F32),
            jax.ShapeDtypeStruct((attn_rows, LANES), BF),
            jax.ShapeDtypeStruct((attn_rows, LANES), BF),
        ]
        + [jax.ShapeDtypeStruct(shape, kind) for shape, kind in stored_shapes]
        + [jax.ShapeDtypeStruct((stack_rows, LANES), BF)] * 4,
        scratch_shapes=[
            pltpu.VMEM((rows, own_cols), BF),
            pltpu.VMEM((rows, own_cols), BF),
            pltpu.VMEM((rows, width), BF),
            pltpu.VMEM((rows, width), BF),
            pltpu.VMEM((2,) + w_in.shape, BF),
            pltpu.VMEM((2,) + w_out.shape, BF),
        ]
        + [pltpu.VMEM(shape, kind) for shape, kind in stored_shapes]
        + [
            pltpu.VMEM((2, 2, stack_rows, LANES), BF),
            pltpu.VMEM((4, 256, 128), F32),
            pltpu.VMEM((4, 8, 128), F32),
            pltpu.VMEM((HALO, 1024), BF),
            pltpu.VMEM((rows, width), F32),
            pltpu.VMEM((rows, 128), F32),
            pltpu.VMEM((rows, width), BF),
            pltpu.VMEM((width, rows), BF),
            pltpu.VMEM((width, rows), BF),
            pltpu.VMEM((rows, width), F32),
            pltpu.SemaphoreType.DMA((64,)),
        ],
        compiler_params=params(62),
        cost_estimate=cost(30),
        name="layer",
    )(
        lengths,
        blend,
        blend_other,
        packet,
        gain_two,
        w_attn,
        wa_other,
        own,
        other,
        tokens,
        cotangent,
        w_in,
        wi_other,
        w_out,
        wo_other,
    )
    attn_grads, outs = outs[:2], outs[2:]
    mixed, *kept = outs[:7]
    active, out_own, in_own, out_sent, in_sent = outs[7:]

    feed_sum = Reduction(
        [([out_own, swap(out_sent)], 0, stack_rows), ([in_own, swap(in_sent)], 0, stack_rows)], count
    )
    wanted = len(feed_sum.orders[0])
    if wanted > 0:
        gmix, *cuts = tie(gmix, *feed_sum.cuts())
        feed_sum.send(cuts)

    steps = blocks // STEP_BLOCKS

    def back_block(*shape):
        return pl.BlockSpec(
            (shape[0] * STEP_BLOCKS,) + shape[1:], lambda i: (steps - 1 - i,) + (0,) * (len(shape) - 1)
        )

    gq, gk, gv, packet_back, gblend = pl.pallas_call(
        mixer_backward_kernel,
        grid=(steps,),
        in_specs=[
            smem,
            smem,
            smem,
            back_block(BLOCK, own_cols),
            back_block(BLOCK, own_cols),
            back_block(1, 4, 128, 128),
            back_block(1, HALO, 1024),
            back_block(1, 4, BLOCK + HALO, 256),
            back_block(1, 4, BLOCK, 256),
            back_block(BLOCK, width),
            back_block(BLOCK, width),
            back_block(BLOCK, width),
        ],
        out_specs=[back_block(BLOCK, width)] * 3 + [whole((PACKET, 128)), whole((2, 4, 8, 128))],
        out_shape=[jax.ShapeDtypeStruct((rows, width), BF)] * 3
        + [jax.ShapeDtypeStruct((PACKET, 128), BF), jax.ShapeDtypeStruct((2, 4, 8, 128), F32)],
        scratch_shapes=[
            pltpu.VMEM((HALO, 1024), F32),
            pltpu.VMEM((4, 256, 128), F32),
            pltpu.VMEM((4, 8, 128), F32),
        ],
        compiler_params=params(60),
        cost_estimate=cost(20),
        name="mixer_backward",
    )(lengths, blend, blend_other, own, other, *kept, gmix)
    if wanted > 1:
        (packet_back,) = feed_sum.after(packet_back)
        feed_sum.take()
    packet_got = swap(packet_back)
    if wanted > 1:
        packet_got, *cuts = tie(packet_got, *feed_sum.cuts())
        feed_sum.send(cuts)

    wq_shape = (3 * width + attn_rows + EXTRA, own_cols // 3)
    kv_cols = 2 * own_cols // 3
    gproj, wq_mine, wq_sent = pl.pallas_call(
        finish_kernel,
        in_specs=[smem] + [vmem] * 3 + [anywhere] * 11,
        out_specs=[anywhere] * 3,
        out_shape=[
            jax.ShapeDtypeStruct((rows, 2 * kv_cols), BF),
            jax.ShapeDtypeStruct(wq_shape, BF),
            jax.ShapeDtypeStruct(wq_shape, BF),
        ],
        scratch_shapes=[
            pltpu.VMEM((PACKET, 128), BF),
            pltpu.VMEM((rows, kv_cols), BF),
            pltpu.VMEM((rows, kv_cols), BF),
        ]
        + [pltpu.VMEM((rows, width), BF)] * 4
        + [pltpu.VMEM(wq_own.shape, BF)] * 2
        + [
            pltpu.VMEM((rows, 2 * kv_cols), BF),
            pltpu.VMEM(wq_shape, BF),
            pltpu.VMEM(wq_shape, BF),
            pltpu.SemaphoreType.DMA((24,)),
        ],
        compiler_params=params(60),
        cost_estimate=cost(8),
        name="finish",
    )(
        lengths,
        gblend,
        ggain_mlp,
        gain_one,
        packet_got,
        own,
        other,
        gk,
        gv,
        gq,
        normed,
        wq_own,
        wq_other,
        *attn_grads,
    )

    def layer_output(active):
        return pl.pallas_call(
            output_kernel,
            grid=(4,),
            in_specs=[row_block(tall, width), row_block(tall, width), row_block(tall, 2 * units)]
            + [whole(w_attn.shape)] * 2
            + [whole(w_out.shape)] * 2,
            out_specs=row_block(tall, width),
            out_shape=jax.ShapeDtypeStruct((rows, width), BF),
            compiler_params=params(60),
            cost_estimate=cost(5),
            name="layer_output",
        )(tokens, mixed, active, w_attn, wa_other, w_out, wo_other)

    def input_gradient(gproj):
        return pl.pallas_call(
            input_grad_kernel,
            grid=(4,),
            in_specs=[
                row_block(tall, width),
                row_block(tall, 2 * kv_cols),
                row_block(tall, width),
                row_block(tall, width),
                whole((1, width)),
                whole(wq_own.shape),
                whole(wq_own.shape),
            ],
            out_specs=row_block(tall, width),
            out_shape=jax.ShapeDtypeStruct((rows, width), BF),
            compiler_params=params(60),
            cost_estimate=cost(7),
            name="input_grad",
        )(gq, gproj, tokens, branch, gain_one, wq_own, wq_other)

    if wanted > 1:
        (wq_sent,) = feed_sum.after(wq_sent)
        feed_sum.take()
    wq_got = swap(wq_sent)
    cut = wq_got.shape[0] // 2
    wq_sum = Reduction([([wq_mine, wq_got], 0, cut), ([wq_mine, wq_got], cut, cut)], count, True)
    if wanted == 3:
        feed_cuts = feed_sum.cuts()
        wq_cuts = wq_sum.cuts()
        gproj, *feed_cuts = tie(gproj, *feed_cuts)
        feed_sum.send(feed_cuts)
        gproj, *wq_cuts = tie(gproj, *wq_cuts)
        wq_sum.send(wq_cuts)
        grad_input = input_gradient(gproj)
        (grad_input,) = wq_sum.after(grad_input)
        (grad_input,) = feed_sum.after(grad_input)
        turns = ((wq_sum,), (feed_sum,), (wq_sum,), (feed_sum, wq_sum), (feed_sum,), (wq_sum,), (wq_sum,))
        for turn, reductions in enumerate(turns):
            if turn == len(turns) - 1:
                wq_sum.gots = list(feed_sum.after(*wq_sum.gots))
            some = []
            for reduction in reductions:
                reduction.take()
                some.append(reduction.cuts())
            active, *cuts = tie(active, *[cut for own_cuts in some for cut in own_cuts])
            for reduction, own_cuts in zip(reductions, some):
                reduction.send([cuts.pop(0) for _ in own_cuts])
            if turn == LATE_TURN:
                output = layer_output(active)
                (output,) = feed_sum.after(output)
                (output,) = wq_sum.after(output)
    else:
        grad_input, output = input_gradient(gproj), layer_output(active)
        for reduction in (feed_sum, wq_sum):
            while reduction.orders[0] and not (reduction.last() and reduction.gots and reduction.held is not None):
                if reduction.gots:
                    reduction.take()
                reduction.send(reduction.cuts())

    out_mine, out_got, in_mine, in_got = feed_sum.parts()
    bits = feed_sum.last_bits()
    feed_parts = [out_mine, in_mine, out_got, in_got]
    wo_grad, wi_grad = pl.pallas_call(
        feed_output_kernel,
        in_specs=[smem] + [anywhere] * 4,
        out_specs=[anywhere] * 2,
        out_shape=[jax.ShapeDtypeStruct(w_out.shape, F32), jax.ShapeDtypeStruct(w_in.shape, F32)],
        scratch_shapes=[pltpu.VMEM(part.shape, BF) for part in feed_parts]
        + [
            pltpu.VMEM((2, units, LANES), F32),
            pltpu.VMEM((2, width, units // 2), F32),
            pltpu.SemaphoreType.DMA((16,)),
        ],
        compiler_params=params(60),
        cost_estimate=cost(3),
        name="feed_output",
    )(bits, *feed_parts)
    if wanted > 1:
        (wi_grad,) = wq_sum.after(wi_grad)
    a_mine, a_got, b_mine, b_got = wq_sum.parts()
    wq_parts = [a_mine, b_mine, a_got, b_got]
    wq_grad, wa_grad, ggain_one, ggain_two, gblend_all = pl.pallas_call(
        last_output_kernel,
        in_specs=[smem] + [anywhere] * 4,
        out_specs=[vmem] * 5,
        out_shape=[
            jax.ShapeDtypeStruct((3 * width, own_cols // 3), F32),
            jax.ShapeDtypeStruct(w_attn.shape, F32),
            jax.ShapeDtypeStruct((1, width), F32),
            jax.ShapeDtypeStruct((1, width), F32),
            jax.ShapeDtypeStruct(blend.shape, F32),
        ],
        scratch_shapes=[pltpu.VMEM(part.shape, BF) for part in wq_parts] + [pltpu.SemaphoreType.DMA((4,))],
        compiler_params=params(60),
        cost_estimate=cost(3),
        name="last_output",
    )(bits, *wq_parts)

    return (
        output,
        grad_input,
        wq_grad.reshape(wq_own.shape).transpose(1, 0, 2),
        wa_grad,
        wi_grad,
        wo_grad,
        ggain_one.reshape(width),
        ggain_two.reshape(width),
        gblend_all,
    )


def solution(mesh):
    return jax.shard_map(
        partial(body, mesh.shape["dp"]),
        mesh=mesh,
        in_specs=(
            P(("dp", "tensor"), None),
            P("dp", None),
            P(None, None, "tensor"),
            P("tensor", None),
            P(None, "tensor"),
            P("tensor", None),
            P(),
            P(),
            P(None, "tensor"),
            P(("dp", "tensor"), None),
        ),
        out_specs=(
            P(("dp", "tensor"), None),
            P(("dp", "tensor"), None),
            P(None, None, "tensor"),
            P("tensor", None),
            P(None, "tensor"),
            P("tensor", None),
            P(),
            P(),
            P(None, "tensor"),
        ),
        check_vma=False,
    )
```
